128 devices in a mesh: replica: 16 (over x_hi, y, core), fsdp: 8 (over x_lo, z).
Axes of the slice: x: 4 (x_hi: 2, x_lo: 2; x = x_hi * 2 + x_lo), y: 4, z: 4, core: 2. Of those that a mesh axis runs over, the one named last changes fastest.
Arguments:
- latents: bfloat16 [262144, 64], P(('replica', 'fsdp')), may hold values from -6 to 6
- target: bfloat16 [262144, 64], P(('replica', 'fsdp')), may hold values from -6 to 6
- timesteps: int32 [512], P(('replica', 'fsdp')), may hold values from 0 to 999
- patch_weight: float32 [16, 64, 5120], P('replica', None, 'fsdp'), may hold values from -0.75 to 0.75
- head_weight: float32 [16, 64, 5120], P('replica', None, 'fsdp'), may hold values from -0.078125 to 0.078125
- modulation: float32 [16, 2, 5120], P('replica', None, 'fsdp'), may hold values from -3 to 3
- time_weight: float32 [16, 256, 5120], P('replica', None, 'fsdp'), may hold values from -0.375 to 0.375
- anchor: float32 [5120, 5120], P('fsdp', 'replica'), may hold values from -6 to 6
- momentum: float32 [5120, 5120], P('fsdp', 'replica'), may hold values from -4 to 4
- frag_start: bfloat16 [5120, 5120], P('fsdp'), may hold values from -4.1 to 4.1, as said below
- frag_current: bfloat16 [16, 5120, 5120], P('replica', 'fsdp'), may hold values from -10.1 to 10.1, as said below
Outputs:
- patch_new: float32 [16, 64, 5120], P('replica', None, 'fsdp')
- head_new: float32 [16, 64, 5120], P('replica', None, 'fsdp')
- modulation_new: float32 [16, 2, 5120], P('replica', None, 'fsdp')
- time_new: float32 [16, 256, 5120], P('replica', None, 'fsdp')
- new_anchor: float32 [5120, 5120], P('fsdp', 'replica')
- new_momentum: float32 [5120, 5120], P('fsdp', 'replica')
- new_params: bfloat16 [5120, 5120], P('fsdp')
The draws below stay inside these ranges and needn't reach their ends.
Inputs may be any that keep to these rules, and one draw needn't show every extreme that they name: `frag_start`: every entry is at least 0.02 in magnitude. `frag_current`: every entry is at least 0.02 in magnitude.
All inputs are finite; a program needn't handle non-finite values.
Results may differ from the reference program's by a relative error of at most 0.028.
Values may be sent and summed in bfloat16 or wider, within the bound.
No kernel may reach another device: no remote copies, remote signals or barrier semaphores. Data moves between devices by JAX's collectives and lax.ppermute only.
A program may use at most 192 MiB of HBM per device.

```python
import math
import jax
import jax.numpy as jnp
from jax import lax

D = 5120
FREQ_DIM = 256
PATCH_DIM = 64
QBLOCK = 128
SAMPLE_TOKENS = 512
SAMPLES = 512
TOKENS = 262144
REPLICAS = 16
N_REPLICA = 16


def lift_magnitude(values):
    return jnp.where(values >= 0.0, values + 0.02, values - 0.02)


def rough_noise(key, shape):
    normal_part = jnp.clip(jax.random.normal(key, shape, jnp.float32), -4.0, 4.0)
    return normal_part


def fragment_base(key):
    return lift_magnitude(rough_noise(key, (D, D))).astype(jnp.bfloat16)


def draw_frag_start(key, part):
    return fragment_base(key)


def draw_frag_current(key, part):
    low_scale = 0.25
    start = fragment_base(key).astype(jnp.float32)
    key = jax.random.fold_in(key, 5)
    noise_key, column_key, row_key = jax.random.split(key, 3)
    drift_noise = rough_noise(noise_key, (REPLICAS, D, D))
    column_scale = jnp.exp(jax.random.uniform(column_key, (REPLICAS, 1, D), jnp.float32, math.log(low_scale), 0.0))
    row_scale = jnp.exp(jax.random.uniform(row_key, (1, D, 1), jnp.float32, math.log(0.5), math.log(1.5)))
    drift = drift_noise * column_scale * row_scale
    return lift_magnitude(start[None] - drift).astype(jnp.bfloat16)


def touch_ends(array, stream_key, low, high):
    longest = array.shape.index(max(array.shape))
    spots = []
    for shift in (0, 1):
        where = [jax.random.randint(jax.random.fold_in(stream_key, axis), (), 0, length) for axis, length in enumerate(array.shape)]
        where[longest] = (where[longest] + shift) % array.shape[longest]
        spots.append(tuple(where))
    return array.at[spots[0]].set(low).at[spots[1]].set(high)


def shard_levels(key, dims, pieces, smallest, largest):
    gain, own = 1.0, jax.random.fold_in(key, 6)
    for axis_at, blocks in pieces:
        heights = jnp.exp(jax.random.uniform(jax.random.fold_in(own, axis_at), (blocks,), jnp.float32, smallest / len(pieces), largest / len(pieces)))
        gain = gain * jnp.repeat(heights, dims[axis_at] // blocks).reshape([-1 if axis == axis_at else 1 for axis in range(len(dims))])
    return gain


def gaussian(stream_key, dims, scale, bound, cuts=(), kind=jnp.bfloat16):
    entries = jax.random.normal(stream_key, dims, jnp.float32) * scale
    if len(cuts) > 0:
        entries = shard_levels(stream_key, dims, cuts, -0.22, 0.18) * entries
    return jnp.clip(entries, min=-bound, max=bound).astype(kind)


def setup_inputs(seed: int = 0) -> dict:
    arg_keys = jax.random.split(jax.random.key(seed), 12)
    return {
        "latents": gaussian(arg_keys[0], (TOKENS, PATCH_DIM), 1.0, 6.0, ((0, 128),)),
        "target": gaussian(arg_keys[1], (TOKENS, PATCH_DIM), 1.0, 6.0, ((0, 128),)),
        "timesteps": touch_ends(jax.random.randint(arg_keys[2], (SAMPLES,), 0, 1000), jax.random.fold_in(arg_keys[2], 1), 0, 999).astype(jnp.int32),
        "patch_weight": gaussian(arg_keys[3], (REPLICAS, PATCH_DIM, D), PATCH_DIM ** -0.5, 0.75, ((0, 16), (2, 8)), jnp.float32),
        "head_weight": gaussian(arg_keys[4], (REPLICAS, PATCH_DIM, D), D ** -0.5, 0.078125, ((0, 16), (2, 8)), jnp.float32),
        "modulation": gaussian(arg_keys[5], (REPLICAS, 2, D), 0.3, 3.0, ((0, 16), (2, 8)), jnp.float32),
        "time_weight": gaussian(arg_keys[6], (REPLICAS, FREQ_DIM, D), FREQ_DIM ** -0.5, 0.375, ((0, 16), (2, 8)), jnp.float32),
        "anchor": gaussian(arg_keys[7], (D, D), 1.0, 6.0, ((0, 8), (1, 16)), jnp.float32),
        "momentum": gaussian(arg_keys[8], (D, D), 0.3, 4.0, ((0, 8), (1, 16)), jnp.float32),
        "frag_start": draw_frag_start(jax.random.fold_in(arg_keys[11], 71), 0),
        "frag_current": draw_frag_current(jax.random.fold_in(arg_keys[11], 71), 0),
    }


epsilon = 1e-06
inner_rate = 0.5
outer_rate = 0.7
momentum_decay = 0.9

def sinusoid(time_steps):
    index = jnp.arange(FREQ_DIM // 2, dtype=jnp.float32)
    frequency = jnp.exp(-math.log(10000.0) * index / (FREQ_DIM // 2))
    angles = time_steps.astype(jnp.float32)[:, None] * frequency[None, :]
    return jnp.concatenate([jnp.cos(angles), jnp.sin(angles)], axis=1)

def silu_slope(pre_act):
    sigmoid_val = jax.nn.sigmoid(pre_act)
    return sigmoid_val * (1.0 + pre_act * (1.0 - sigmoid_val))

def quantize(blocks, scale_bf):
    scale_f = scale_bf.astype(jnp.float32)[:, None, :]
    seven_abs = 7.0 * jnp.abs(blocks)
    levels = jnp.zeros_like(blocks)
    for rung_index in range(7):
        levels = levels + (seven_abs >= (rung_index + 0.5) * scale_f).astype(jnp.float32)
    return (jnp.sign(blocks) * levels).astype(jnp.bfloat16)

def make_visitor(patch_bf, head_bf, mod_bf, tok_count):

    def visit_block(totals, inputs):
        latent_blk, target_blk, embed_row = inputs
        hidden = jnp.dot(latent_blk, patch_bf, preferred_element_type=jnp.float32)
        center = hidden - lax.optimization_barrier(jnp.mean(hidden, axis=1, keepdims=True))
        inv_std = lax.rsqrt(lax.optimization_barrier(jnp.mean(center * center, axis=1, keepdims=True)) + epsilon)
        normed = center * inv_std
        gain_row = 1.0 + mod_bf[1].astype(jnp.float32) + embed_row
        modulated = (normed * gain_row + mod_bf[0].astype(jnp.float32) + embed_row).astype(jnp.bfloat16)
        output = lax.dot_general(modulated, head_bf, (((1,), (1,)), ((), ())), preferred_element_type=jnp.float32)
        grad_out = (2.0 * (output - target_blk.astype(jnp.float32)) / tok_count).astype(jnp.bfloat16)
        grad_head = lax.dot_general(grad_out, modulated, (((0,), (0,)), ((), ())), preferred_element_type=jnp.float32)
        grad_mixed = jnp.dot(grad_out, head_bf, preferred_element_type=jnp.float32)
        grad_shift = lax.optimization_barrier(jnp.sum(grad_mixed, axis=0))
        grad_scale = lax.optimization_barrier(jnp.sum(grad_mixed * normed, axis=0))
        grad_normed = grad_mixed * gain_row
        grad_hidden = ((grad_normed - lax.optimization_barrier(jnp.mean(grad_normed, axis=1, keepdims=True)) - normed * lax.optimization_barrier(jnp.mean(grad_normed * normed, axis=1, keepdims=True))) * inv_std).astype(jnp.bfloat16)
        grad_patch = lax.dot_general(latent_blk, grad_hidden, (((0,), (0,)), ((), ())), preferred_element_type=jnp.float32)
        new_totals = (totals[0] + grad_patch, totals[1] + grad_head, totals[2] + jnp.stack([grad_shift, grad_scale]))
        return (new_totals, grad_shift + grad_scale)
    return visit_block

def inner_replica(latent_r, target_r, steps_r, patch_r, head_r, mod_r, time_r):
    patch_bf = patch_r.astype(jnp.bfloat16)
    head_bf = head_r.astype(jnp.bfloat16)
    mod_bf = mod_r.astype(jnp.bfloat16)
    time_bf = time_r.astype(jnp.bfloat16)
    sines = sinusoid(steps_r).astype(jnp.bfloat16)
    pre_act = jnp.dot(sines, time_bf, preferred_element_type=jnp.float32)
    embed = jax.nn.silu(pre_act)
    sample_count = steps_r.shape[0]
    tok_count = latent_r.shape[0] * 1.0
    latent_blocks = latent_r.reshape(sample_count, SAMPLE_TOKENS, PATCH_DIM)
    target_blocks = target_r.reshape(sample_count, SAMPLE_TOKENS, PATCH_DIM)
    start_totals = (jnp.zeros((PATCH_DIM, D), jnp.float32), jnp.zeros((PATCH_DIM, D), jnp.float32), jnp.zeros((2, D), jnp.float32))
    totals, grad_embed = lax.scan(make_visitor(patch_bf, head_bf, mod_bf, tok_count), start_totals, (latent_blocks, target_blocks, embed))
    grad_pre = (grad_embed * silu_slope(pre_act)).astype(jnp.bfloat16)
    grad_time = lax.dot_general(sines, grad_pre, (((0,), (0,)), ((), ())), preferred_element_type=jnp.float32)
    return (patch_r - inner_rate * totals[0], head_r - inner_rate * totals[1], mod_r - inner_rate * totals[2], time_r - inner_rate * grad_time)

def per_replica(packed):
    return inner_replica(*packed)

def reference(latents, target, timesteps, patch_weight, head_weight, modulation, time_weight, anchor, momentum, frag_start, frag_current):
    packed = (latents.reshape(N_REPLICA, -1, PATCH_DIM), target.reshape(N_REPLICA, -1, PATCH_DIM), timesteps.reshape(N_REPLICA, -1), patch_weight, head_weight, modulation, time_weight)
    patch_new, head_new, modulation_new, time_new = lax.map(per_replica, packed)
    start_f = frag_start.astype(jnp.float32)

    def add_replica(total, current):
        delta = start_f - current.astype(jnp.float32)
        blocks = delta.reshape(D // QBLOCK, QBLOCK, D)
        scale = (lax.optimization_barrier(jnp.max(jnp.abs(blocks), axis=1)) + epsilon).astype(jnp.bfloat16)
        code = quantize(blocks, scale)
        term = (code.astype(jnp.float32) * scale.astype(jnp.float32)[:, None, :] / 7.0).reshape(D, D)
        return (total + term, None)
    total, unused = lax.scan(add_replica, jnp.zeros((D, D), jnp.float32), frag_current)
    average = total / N_REPLICA
    new_momentum = momentum_decay * momentum + average
    new_anchor = anchor - outer_rate * (average + momentum_decay * new_momentum)
    new_params = new_anchor.astype(jnp.bfloat16)
    return (patch_new, head_new, modulation_new, time_new, new_anchor, new_momentum, new_params)
```

```python
import functools
import math

import jax
import jax.numpy as jnp
from jax import lax
from jax.experimental import pallas as pl
from jax.experimental.pallas import tpu as pltpu
from jax.sharding import PartitionSpec as P

FREQ_DIM = 256
PATCH_DIM = 64
QBLOCK = 128
SAMPLE_TOKENS = 512

epsilon = 1e-06
inner_rate = 0.5
outer_rate = 0.7
momentum_decay = 0.9

f32 = jnp.float32
bf16 = jnp.bfloat16

N_Y, N_XH, N_CORE = 4, 2, 2
COL = 320
PAIR = 640
ROWS = 640
ROUND = 1.5 * 2.0**23
NUDGE = 1.0 + 2.0**-21

NT = (((1,), (1,)), ((), ()))
TN = (((0,), (0,)), ((), ()))
NN = (((1,), (0,)), ((), ()))


def dot(a, b, dims):
    return lax.dot_general(a, b, dims, preferred_element_type=f32)


def split2(x):
    hi = x.astype(bf16)
    return hi, (x - hi.astype(f32)).astype(bf16)


def quantized(delta):
    peak = jnp.max(jnp.abs(delta), axis=0, keepdims=True)
    scale = (peak + epsilon).astype(bf16).astype(f32)
    ratio = (7.0 / scale) * NUDGE
    shifted = delta * ratio + ROUND
    code = jnp.clip(shifted, ROUND - 7.0, ROUND + 7.0) - ROUND
    return code * (scale / 7.0)


def quant_kernel(keep, segments, pos_ref, *refs):
    start_main, start_rest, cur_main, cur_rest = refs[0:4]
    refs = refs[4:]
    if keep:
        other, refs = refs[0], refs[1:]
    outs = refs
    first_core = pos_ref[0] == 0
    low_side = first_core if keep else jnp.logical_not(first_core)
    low_lane = lax.broadcasted_iota(jnp.int32, (64, 128), 1) < 64
    straight = low_lane == low_side

    def put(row, lane, value):
        if keep:
            value = value + other[0, 0, row : row + 64, lane : lane + 128].astype(f32)
        value = value.astype(bf16)
        at = 0
        for out, size in zip(outs, segments):
            begin, end = max(row, at), min(row + 64, at + size)
            if begin < end:
                out[0, 0, begin - at : end - at, lane : lane + 128] = value[
                    begin - row : end - row
                ]
            at += size

    for block in range(ROWS // QBLOCK):
        rows = slice(block * QBLOCK, (block + 1) * QBLOCK)
        for tile in range(2):
            lanes = slice(tile * 128, (tile + 1) * 128)
            delta = start_main[rows, lanes].astype(f32) - cur_main[rows, lanes].astype(f32)
            term = quantized(delta)
            put(block * 64, tile * 128, term[:64])
            put(block * 64, 256 + tile * 128, term[64:])
        term = quantized(start_rest[rows].astype(f32) - cur_rest[rows].astype(f32))
        top, bottom = term[:64], term[64:]
        moved = pltpu.roll(jnp.where(low_side, bottom, top), 64, 1)
        still = jnp.where(low_side, top, bottom)
        put(block * 64, 512, jnp.where(straight, still, moved))


def quantize(pos, frag_start, frag_current, other, y_first, y_step, y_count, segments):
    keep = other is not None

    def chip(i, j, pos):
        return lax.rem(pos[2] + j, N_XH) * N_Y + lax.rem(pos[1] + y_first + i * y_step, N_Y)

    def high(pos):
        return pos[0] if keep else 1 - pos[0]

    main = pl.BlockSpec(
        (pl.Element(ROWS), pl.Element(256)),
        lambda i, j, pos: (0, (chip(i, j, pos) * 5 + 3 * high(pos)) * 128),
    )
    rest = pl.BlockSpec((ROWS, 128), lambda i, j, pos: (0, chip(i, j, pos) * 5 + 2))
    whole = pl.BlockSpec((1, 1, ROWS // 2, PAIR), lambda i, j, pos: (i, j, 0, 0))
    out_specs = [pl.BlockSpec((1, 1, n, PAIR), lambda i, j, pos: (i, j, 0, 0)) for n in segments]
    cells = y_count * N_XH * ROWS * COL
    return pl.pallas_call(
        functools.partial(quant_kernel, keep, segments),
        grid_spec=pltpu.PrefetchScalarGridSpec(
            num_scalar_prefetch=1,
            grid=(y_count, N_XH),
            in_specs=[main, rest, main, rest] + ([whole] if keep else []),
            out_specs=out_specs,
        ),
        out_shape=[jax.ShapeDtypeStruct((y_count, N_XH, n, PAIR), bf16) for n in segments],
        compiler_params=pltpu.CompilerParams(vmem_limit_bytes=24 * 2**20),
        cost_estimate=pl.CostEstimate(flops=16 * cells, bytes_accessed=6 * cells, transcendentals=0),
        name="keep_terms" if keep else "send_terms",
    )(pos, frag_start, frag_start, frag_current, frag_current, *([other] if keep else []))


def outer_kernel(pos_ref, own_ref, far_ref, anchor_ref, momentum_ref, new_anchor, new_momentum, params, native, fresh):
    low_lane = lax.broadcasted_iota(jnp.int32, (64, 128), 1) < 64
    first_core = pos_ref[0] == 0
    total = own_ref[...].astype(f32) + far_ref[...].astype(f32)
    rest = total[:, 512:640]
    swapped = pltpu.roll(rest, 64, 1)
    for half, tail in ((0, rest), (1, swapped)):
        rows = slice(half * 64, half * 64 + 64)
        main0 = total[:, half * 256 : half * 256 + 128]
        main1 = total[:, half * 256 + 128 : half * 256 + 256]

        @pl.when(first_core)
        def _():
            native[rows, 0:128] = main0
            native[rows, 128:256] = main1
            native[rows, 256:384] = tail

        @pl.when(jnp.logical_not(first_core))
        def _():
            turn0, turn1 = pltpu.roll(main0, 64, 1), pltpu.roll(main1, 64, 1)
            native[rows, 0:128] = jnp.where(low_lane, tail, turn0)
            native[rows, 128:256] = jnp.where(low_lane, turn0, turn1)
            native[rows, 256:384] = turn1

    average = native[:, 0:COL] / float(N_Y * N_XH * N_CORE)
    momentum = momentum_decay * momentum_ref[...] + average
    anchor = anchor_ref[...] - outer_rate * (average + momentum_decay * momentum)
    new_momentum[...] = momentum
    new_anchor[...] = anchor
    fresh[:, 0:COL] = anchor

    @pl.when(first_core)
    def _():
        for half in range(2):
            rows = slice(half * 64, half * 64 + 64)
            params[:, half * 256 : half * 256 + 256] = fresh[rows, 0:256].astype(bf16)
        top, bottom = fresh[0:64, 256:384], pltpu.roll(fresh[64:128, 256:384], 64, 1)
        params[:, 512:640] = jnp.where(low_lane, top, bottom).astype(bf16)

    @pl.when(jnp.logical_not(first_core))
    def _():
        for half in range(2):
            rows = slice(half * 64, half * 64 + 64)
            turn = [pltpu.roll(fresh[rows, t * 128 : t * 128 + 128], 64, 1) for t in range(3)]
            params[:, half * 256 : half * 256 + 128] = jnp.where(low_lane, turn[0], turn[1]).astype(bf16)
            params[:, half * 256 + 128 : half * 256 + 256] = jnp.where(low_lane, turn[1], turn[2]).astype(bf16)
        top, bottom = fresh[0:64, 0:128], pltpu.roll(fresh[64:128, 0:128], 64, 1)
        params[:, 512:640] = jnp.where(low_lane, top, bottom).astype(bf16)


def outer_update(pos, own, far, anchor, momentum):
    block = pl.BlockSpec((64, PAIR), lambda i, pos: (i, 0))
    plain = pl.BlockSpec((128, COL), lambda i, pos: (i, 0))
    cells = ROWS * COL
    return pl.pallas_call(
        outer_kernel,
        grid_spec=pltpu.PrefetchScalarGridSpec(
            num_scalar_prefetch=1,
            grid=(ROWS // 128,),
            in_specs=[block, block, plain, plain],
            out_specs=[plain, plain, block],
            scratch_shapes=[pltpu.VMEM((128, 384), f32), pltpu.VMEM((128, 384), f32)],
        ),
        out_shape=[
            jax.ShapeDtypeStruct((ROWS, COL), f32),
            jax.ShapeDtypeStruct((ROWS, COL), f32),
            jax.ShapeDtypeStruct((ROWS // 2, PAIR), bf16),
        ],
        cost_estimate=pl.CostEstimate(flops=10 * cells, bytes_accessed=22 * cells, transcendentals=0),
        name="outer_update",
    )(pos, own, far, anchor, momentum)


def place_kernel(row_count, pos_ref, mine, theirs, into, out):
    del into
    low_lane = lax.broadcasted_iota(jnp.int32, (64, 128), 1) < 64

    def write(low, high):
        for block in range(row_count // 64):
            rows = slice(block * 64, block * 64 + 64)
            base = block * 128
            for half in range(2):
                to = slice(base + half * 64, base + half * 64 + 64)
                out[to, 0:256] = low[rows, half * 256 : half * 256 + 256]
                out[to, 384:640] = high[rows, half * 256 : half * 256 + 256]
            low_rest, high_rest = low[rows, 512:640].astype(f32), high[rows, 512:640].astype(f32)
            top = jnp.where(low_lane, low_rest, pltpu.roll(high_rest, 64, 1))
            bottom = jnp.where(low_lane, pltpu.roll(low_rest, 64, 1), high_rest)
            out[base : base + 64, 256:384] = top.astype(bf16)
            out[base + 64 : base + 128, 256:384] = bottom.astype(bf16)

    @pl.when(pos_ref[0] == 0)
    def _():
        write(mine, theirs)

    @pl.when(pos_ref[0] != 0)
    def _():
        write(theirs, mine)


def place(pos, into, mine, theirs, dy, dx):
    rows = 64

    def spot(i, pos):
        return (i, lax.rem(pos[2] + dx, N_XH) * N_Y + lax.rem(pos[1] + dy, N_Y))

    block = pl.BlockSpec((rows, PAIR), lambda i, pos: (i, 0))
    out_shape = jax.ShapeDtypeStruct((ROWS, N_Y * N_XH * PAIR), bf16)
    first = into is None
    args = (pos, mine, theirs) + (() if first else (into,))
    kernel = functools.partial(place_kernel, rows)
    if first:
        body = lambda pos_ref, a, b, out: kernel(pos_ref, a, b, None, out)
    else:
        body = kernel
    return pl.pallas_call(
        body,
        grid_spec=pltpu.PrefetchScalarGridSpec(
            num_scalar_prefetch=1,
            grid=(ROWS // 128,),
            in_specs=[block, block] + ([] if first else [pl.BlockSpec(memory_space=pl.ANY)]),
            out_specs=pl.BlockSpec((rows * 2, PAIR), spot),
        ),
        out_shape=out_shape,
        input_output_aliases={} if first else {3: 0},
        cost_estimate=pl.CostEstimate(flops=0, bytes_accessed=4 * ROWS * PAIR, transcendentals=0),
        name="place",
    )(*args)


def fragment_sync(pos, anchor, momentum, frag_start, frag_current):
    to_core = [(r, r ^ 1) for r in range(16)]
    to_x = [(r, r ^ 8) for r in range(16)]

    def to_y(step):
        return [
            (xh * 8 + y * 2 + c, xh * 8 + ((y + step) % N_Y) * 2 + c)
            for xh in range(N_XH)
            for y in range(N_Y)
            for c in range(N_CORE)
        ]

    send = functools.partial(lax.ppermute, axis_name="replica")
    up, down = to_y(1), to_y(-1)
    half = ROWS // 4
    halves = (half, half)

    def sends(first, step, count):
        return quantize(pos, frag_start, frag_current, None, first, step, count, (2 * half,))[0]

    def keeps(dy, other):
        return quantize(pos, frag_start, frag_current, other, dy, 1, 1, halves)

    s2 = sends(2, 1, 1)
    r2 = send(s2, perm=to_core)
    s13 = sends(1, 2, 2)
    r13 = send(s13, perm=to_core)
    a2, b2 = keeps(2, r2)
    u1, d1 = send(a2, perm=up), send(b2, perm=down)
    s0 = sends(0, 1, 1)
    r0 = send(s0, perm=to_core)
    a1, b1 = keeps(1, r13[0:1])
    a3, b3 = keeps(3, r13[1:2])
    u2, d2 = send(b1, perm=up), send(a3, perm=down)
    a0, b0 = keeps(0, r0)

    def add(*parts):
        return sum(p.astype(f32) for p in parts)

    fa = [add(a1[0, x], u1[0, x]).astype(bf16) for x in range(2)]
    fb = [add(b3[0, x], d1[0, x]).astype(bf16) for x in range(2)]
    u3, d3 = [None, None], [None, None]
    for x in (1, 0):
        u3[x], d3[x] = send(fa[x], perm=up), send(fb[x], perm=down)

    def reduced(x):
        return jnp.concatenate([add(a0[0, x], d2[0, x], u3[x]), add(b0[0, x], u2[0, x], d3[x])], axis=0)

    far = send(reduced(1).astype(bf16), perm=to_x)
    new_anchor, new_momentum, n0 = outer_update(pos, reduced(0), far, anchor, momentum)

    n1 = send(n0, perm=to_x)
    up0, down0 = send(n0, perm=up), send(n0, perm=down)
    up1, down1 = send(n1, perm=up), send(n1, perm=down)
    ahead = {}
    ahead[0, 0], ahead[0, 1] = n0, n1
    ahead[3, 0], ahead[1, 0], ahead[3, 1], ahead[1, 1] = up0, down0, up1, down1
    rest = []
    for x, below, above in ((0, up0, down0), (1, up1, down1)):
        rest.append((x, send(below[0 : 2 * half // 2], perm=up), send(above[half:], perm=down)))
    for x, first, second in rest:
        ahead[2, x] = jnp.concatenate([first, second], axis=0)
    new_params = None
    for dy, dx in ((0, 0), (0, 1), (3, 0), (1, 0), (3, 1), (1, 1), (2, 0), (2, 1)):
        mine = ahead[dy, dx]
        new_params = place(pos, new_params, mine, send(mine, perm=to_core), dy, dx)
    return new_anchor, new_momentum, new_params


def column(row):
    eye = lax.broadcasted_iota(jnp.int32, (64, 128), 0) == lax.broadcasted_iota(jnp.int32, (64, 128), 1)
    return jnp.sum(jnp.where(eye, row, 0.0), axis=1, keepdims=True)


def gains(pre, mod_ref):
    embed = pre * jax.nn.sigmoid(pre)
    mod = mod_ref[...].astype(bf16).astype(f32)
    return 1.0 + mod[1:2] + embed, mod[0:1] + embed


def weights_kernel(width, *refs):
    count = 8
    heads = refs[:count]
    patch_ref, head_ref, mod_ref, time_ref = refs[count : count + 4]
    outs = refs[count + 4 : 2 * count + 4]
    pre_ref, center_ref, sines_ref, high, low = refs[2 * count + 4 :]
    total = heads[0][8:9, :]
    for k in range(1, count):
        total = total + heads[k][8:9, :]
    for k in range(count):
        sines_ref[4 * k : 4 * k + 4, 0:128] = heads[k][0:4, :]
        sines_ref[4 * k : 4 * k + 4, 128:256] = heads[k][4:8, :]
    pre = dot(sines_ref[...].astype(bf16), time_ref[...].astype(bf16), NN)
    pre_ref[...] = pre
    gain, shift = gains(pre, mod_ref)
    center = patch_ref[...].astype(bf16).astype(f32) - column(total / width)
    center_ref[...] = center
    samples = 4 * count
    for s in range(samples):
        k, i = s // 4, s % 4
        at = (i // 2) * (samples // 2 * 64) + (2 * k + i % 2) * 64
        hi, lo = split2(center * gain[s : s + 1])
        high[at : at + 64, :] = hi
        low[at : at + 64, :] = lo
    head = head_ref[...].astype(bf16)
    blank = jnp.zeros_like(head)
    left = jnp.concatenate([head, blank], axis=0)
    right = jnp.concatenate([blank, head], axis=0)
    part = samples // 2 * 64
    packed = dot(high[0:part], left, NT) + dot(low[0:part], left, NT)
    packed = packed + dot(high[part:], right, NT) + dot(low[part:], right, NT)
    chi, clo = split2(center)
    blank_left = jnp.zeros_like(chi)
    chi_left = jnp.concatenate([chi, blank_left], axis=0)
    clo_left = jnp.concatenate([clo, blank_left], axis=0)
    gram = dot(chi, chi_left, NT) + dot(clo, chi_left, NT) + dot(chi, clo_left, NT)
    for k in range(count):
        rows = jnp.concatenate([shift[4 * k : 4 * k + 4], gain[4 * k : 4 * k + 4]], axis=0)
        hi, lo = split2(rows)
        extra = dot(hi, right, NT) + dot(lo, right, NT)
        outs[k][0:128, :] = packed[128 * k : 128 * k + 128]
        outs[k][128:136, :] = gram[0:8] + extra
        outs[k][136:192, :] = gram[8:64]


def tokens_kernel(width, tokens, *refs):
    count = 8
    parts = refs[:count]
    latent_ref, target_ref, out, wide = refs[count:]
    total = parts[0][...]
    for k in range(1, count):
        total = total + parts[k][...]
    turned = pltpu.roll(total, 64, 1)
    gram = total[128:192, 0:64] / width
    g0 = gram.astype(bf16)
    g1, g2 = split2(gram - g0.astype(f32))
    shift_rows = turned[128:132, 0:64]
    gain_means = turned[132:136, :] / width
    wide[...] = jnp.zeros_like(wide)
    curve = jnp.zeros((64, 64), f32)
    sums = []
    for s in range(4):
        rows = slice(s * SAMPLE_TOKENS, (s + 1) * SAMPLE_TOKENS)
        latent = latent_ref[rows, :]
        latent_f = latent.astype(f32)
        mix = (total if s < 2 else turned)[(s % 2) * 64 : (s % 2) * 64 + 64, 0:64]
        mix_hi, mix_lo = split2(mix)
        spread = dot(latent, g0, NN) + dot(latent, g1, NN) + dot(latent, g2, NN)
        variance = jnp.sum(spread * latent_f, axis=1, keepdims=True)
        inv_std = lax.rsqrt(jnp.maximum(variance, 0.0) + epsilon)
        varied = inv_std * (dot(latent, mix_hi, NN) + dot(latent, mix_lo, NN))
        output = varied + shift_rows[s : s + 1]
        grad_out = (2.0 * (output - target_ref[rows, :].astype(f32)) / tokens).astype(bf16)
        grad_f = grad_out.astype(f32)
        along = jnp.sum(grad_f * varied, axis=1, keepdims=True) / width
        scaled = latent_f * inv_std
        scaled_b = scaled.astype(bf16)
        cross = dot(grad_out, scaled_b, TN)
        curve = curve + dot(scaled_b, (scaled * along).astype(bf16), TN)
        sums.append(jnp.sum(grad_f, axis=0, keepdims=True))
        if s < 2:
            out[s * 64 : s * 64 + 64, 0:64] = cross
        else:
            wide[(s - 2) * 64 : (s - 2) * 64 + 64, 0:64] = cross
    for s in range(4):
        wide[128 + s : 129 + s, 0:64] = sums[s]
    wide[132:136, 0:64] = gain_means[:, 0:64]
    packed = pltpu.roll(wide[...], 64, 1)
    low_lane = lax.broadcasted_iota(jnp.int32, (128, 128), 1) < 64
    out[0:128, :] = jnp.where(low_lane, out[0:128, :], packed[0:128])
    wide[128:192, 0:64] = curve
    out[128:192, :] = jnp.where(low_lane[0:64], wide[128:192, :], packed[128:192])


def finish_kernel(*refs):
    count = 8
    parts = refs[:count]
    pre_ref, center_ref, sines_ref, patch_ref, head_ref, mod_ref, time_ref = refs[count : count + 7]
    patch_new, head_new, mod_new, time_new, sums, slope_rows = refs[count + 7 :]
    pre = pre_ref[...]
    gain, shift = gains(pre, mod_ref)
    head = head_ref[...].astype(bf16)
    head_f = head.astype(f32)
    center = center_ref[...]
    chi, clo = split2(center)
    curve = parts[0][128:192, 0:64]
    for k in range(1, count):
        curve = curve + parts[k][128:192, 0:64]
    curve_hi, curve_lo = split2(curve)
    grad_patch = -(dot(curve_hi, chi, NN) + dot(curve_lo, chi, NN) + dot(curve_hi, clo, NN))
    grad_head = jnp.zeros_like(center)
    grad_scale = jnp.zeros_like(gain[0:1])
    for k in range(count):
        plain = parts[k][...]
        turned = pltpu.roll(plain, 64, 1)
        sums[4 * k : 4 * k + 4, :] = turned[128:132]
        crosses = jnp.concatenate(
            [plain[0:128, 0:64], turned[0:128, 0:64]], axis=0
        ).astype(bf16)
        mixed = dot(crosses, chi, NN)
        pulls = []
        for i in range(4):
            s = 4 * k + i
            one = mixed[i * 64 : i * 64 + 64]
            grad_head = grad_head + one * gain[s : s + 1]
            slope = jnp.sum(head_f * one, axis=0, keepdims=True)
            slope_rows[s : s + 1, :] = slope
            grad_scale = grad_scale + slope
            pulls.append((head_f * gain[s : s + 1] - column(turned[132 + i : 133 + i])).astype(bf16))
        grad_patch = grad_patch + dot(crosses, jnp.concatenate(pulls, axis=0), TN)
    sum_hi, sum_lo = split2(sums[:, 0:64])
    shift_hi, shift_lo = split2(shift)
    grad_head = grad_head + dot(sum_hi, shift_hi, TN) + dot(sum_lo, shift_hi, TN) + dot(sum_hi, shift_lo, TN)
    mixed_sums = dot(sum_hi, head, NN) + dot(sum_lo, head, NN)
    grad_shift = jnp.sum(mixed_sums, axis=0, keepdims=True)
    grad_embed = mixed_sums + slope_rows[...]
    sigmoid = jax.nn.sigmoid(pre)
    grad_pre = (grad_embed * (sigmoid * (1.0 + pre * (1.0 - sigmoid)))).astype(bf16)
    grad_time = dot(sines_ref[...].astype(bf16), grad_pre, TN)
    patch_new[...] = patch_ref[...] - inner_rate * grad_patch
    head_new[...] = head_ref[...] - inner_rate * grad_head
    mod_new[0:1, :] = mod_ref[0:1, :] - inner_rate * grad_shift
    mod_new[1:2, :] = mod_ref[1:2, :] - inner_rate * grad_scale
    time_new[...] = time_ref[...] - inner_rate * grad_time


def sinusoid(time_steps):
    index = jnp.arange(FREQ_DIM // 2, dtype=f32)
    frequency = jnp.exp(-math.log(10000.0) * index / (FREQ_DIM // 2))
    angles = time_steps.astype(f32)[:, None] * frequency[None, :]
    return jnp.cos(angles), jnp.sin(angles)


def inner_step(latents, target, timesteps, patch, head, mod, time):
    count = 8
    columns = patch.shape[1]
    width = float(columns * count)
    tokens = float(latents.shape[0] * count)
    limit = pltpu.CompilerParams(vmem_limit_bytes=32 * 2**20)

    def gather(value):
        found = [value]
        for k in range(1, count):
            found.append(lax.ppermute(value, "fsdp", [(i, (i - k) % count) for i in range(count)]))
        return found

    cos, sin = sinusoid(timesteps)
    row_sums = jnp.sum(patch.astype(bf16).astype(f32), axis=1)
    first = jnp.concatenate(
        [cos, sin, jnp.pad(row_sums, (0, 64))[None], jnp.zeros((7, 128), f32)], axis=0
    )
    heads = gather(first)
    pay = jax.ShapeDtypeStruct((192, 128), f32)
    weights = pl.pallas_call(
        functools.partial(weights_kernel, width),
        out_shape=[pay] * count
        + [
            jax.ShapeDtypeStruct((4 * count, columns), f32),
            jax.ShapeDtypeStruct((PATCH_DIM, columns), f32),
            jax.ShapeDtypeStruct((4 * count, FREQ_DIM), f32),
        ],
        scratch_shapes=[pltpu.VMEM((4 * count * 64, columns), bf16)] * 2,
        compiler_params=limit,
        cost_estimate=pl.CostEstimate(flops=10**9, bytes_accessed=10**7, transcendentals=0),
        name="weight_products",
    )(*heads, patch, head, mod, time)
    partials, (pre, center, sines) = weights[:count], weights[count:]
    received = [partials[0]]
    for k in range(1, count):
        received.append(lax.ppermute(partials[k], "fsdp", [(i, (i + k) % count) for i in range(count)]))
    matrices = pl.pallas_call(
        functools.partial(tokens_kernel, width, tokens),
        out_shape=pay,
        scratch_shapes=[pltpu.VMEM((192, 128), f32)],
        compiler_params=limit,
        cost_estimate=pl.CostEstimate(flops=10**9, bytes_accessed=10**7, transcendentals=0),
        name="token_sums",
    )(*received, latents, target)
    return pl.pallas_call(
        finish_kernel,
        out_shape=[jax.ShapeDtypeStruct(a.shape, f32) for a in (patch, head, mod, time)],
        scratch_shapes=[pltpu.VMEM((4 * count, 128), f32), pltpu.VMEM((4 * count, columns), f32)],
        compiler_params=limit,
        cost_estimate=pl.CostEstimate(flops=10**9, bytes_accessed=10**7, transcendentals=0),
        name="finish",
    )(*gather(matrices), pre, center, sines, patch, head, mod, time)


def per_device(
    latents,
    target,
    timesteps,
    patch_weight,
    head_weight,
    modulation,
    time_weight,
    anchor,
    momentum,
    frag_start,
    frag_current,
):
    replica = lax.axis_index("replica")
    pos = jnp.stack([replica % 2, (replica // 2) % 4, replica // 8]).astype(jnp.int32)
    new_anchor, new_momentum, new_params = fragment_sync(
        pos, anchor, momentum, frag_start, frag_current[0]
    )
    inner = inner_step(
        latents, target, timesteps, patch_weight[0], head_weight[0], modulation[0], time_weight[0]
    )
    return tuple(a[None] for a in inner) + (new_anchor, new_momentum, new_params)


def solution(mesh):
    in_specs = (
        P(("replica", "fsdp"), None),
        P(("replica", "fsdp"), None),
        P(("replica", "fsdp")),
        P("replica", None, "fsdp"),
        P("replica", None, "fsdp"),
        P("replica", None, "fsdp"),
        P("replica", None, "fsdp"),
        P("fsdp", "replica"),
        P("fsdp", "replica"),
        P("fsdp", None),
        P("replica", "fsdp", None),
    )
    out_specs = (
        P("replica", None, "fsdp"),
        P("replica", None, "fsdp"),
        P("replica", None, "fsdp"),
        P("replica", None, "fsdp"),
        P("fsdp", "replica"),
        P("fsdp", "replica"),
        P("fsdp", None),
    )
    return jax.shard_map(
        per_device, mesh=mesh, in_specs=in_specs, out_specs=out_specs, check_vma=False
    )
```

```python
import functools
import math

import jax
import jax.numpy as jnp
from jax import lax
from jax.experimental import pallas as pl
from jax.experimental.pallas import tpu as pltpu
from jax.sharding import PartitionSpec as P

FREQ_DIM = 256
PATCH_DIM = 64
QBLOCK = 128
SAMPLE_TOKENS = 512

epsilon = 1e-06
inner_rate = 0.5
outer_rate = 0.7
momentum_decay = 0.9

f32 = jnp.float32
bf16 = jnp.bfloat16

N_Y, N_XH, N_CORE, N_FSDP = 4, 2, 2, 8
COL = 320
PAIR = 640
ROWS = 640
ROUND = 1.5 * 2.0**23
NUDGE = 1.0 + 2.0**-21

limit = pltpu.CompilerParams(vmem_limit_bytes=56 * 2**20)
brief = pl.CostEstimate(flops=1, bytes_accessed=1, transcendentals=0)
unread = pl.BlockSpec(memory_space=pl.ANY)

NT = (((1,), (1,)), ((), ()))
TN = (((0,), (0,)), ((), ()))
NN = (((1,), (0,)), ((), ()))


def dot(a, b, dims):
    return lax.dot_general(a, b, dims, preferred_element_type=f32)


def split2(x):
    hi = x.astype(bf16)
    return hi, (x - hi.astype(f32)).astype(bf16)


def quantized(delta):
    peak = jnp.max(jnp.abs(delta), axis=0, keepdims=True)
    scale = (peak + epsilon).astype(bf16).astype(f32)
    ratio = (7.0 / scale) * NUDGE
    shifted = delta * ratio + ROUND
    code = jnp.clip(shifted, ROUND - 7.0, ROUND + 7.0) - ROUND
    return code * (scale / 7.0)


def quant_kernel(pos_ref, start_ref, current_ref, keep, send):
    first_core = pos_ref[0] == 0
    low_lane = lax.broadcasted_iota(jnp.int32, (64, 128), 1) < 64
    for chip in range(N_Y * N_XH):
        dy = lax.rem(chip % N_Y - pos_ref[1] + N_Y, N_Y)
        dx = lax.rem(chip // N_Y - pos_ref[2] + N_XH, N_XH)
        slot = dy * N_XH + dx

        def terms(tile):
            lanes = slice(chip * PAIR + tile * 128, chip * PAIR + (tile + 1) * 128)
            return quantized(start_ref[:, lanes].astype(f32) - current_ref[:, lanes].astype(f32))

        def put(lane, low, high):
            keep[slot, :, lane : lane + 128] = jnp.where(first_core, low, high).astype(bf16)
            send[slot, :, lane : lane + 128] = jnp.where(first_core, high, low).astype(bf16)

        for tile in range(2):
            low, high = terms(tile), terms(tile + 3)
            put(tile * 128, low[:64], high[:64])
            put(256 + tile * 128, low[64:], high[64:])
        both = terms(2)
        top, bottom = both[:64], both[64:]
        low = jnp.where(low_lane, top, pltpu.roll(bottom, 64, 1))
        high = jnp.where(low_lane, pltpu.roll(top, 64, 1), bottom)
        put(512, low, high)


def quantize(pos, frag_start, frag_current):
    chips = N_Y * N_XH
    whole = pl.BlockSpec((QBLOCK, frag_start.shape[1]), lambda i, pos: (i, 0))
    made = pl.BlockSpec((chips, QBLOCK // 2, PAIR), lambda i, pos: (0, i, 0))
    keep, sent = pl.pallas_call(
        quant_kernel,
        grid_spec=pltpu.PrefetchScalarGridSpec(
            num_scalar_prefetch=1,
            grid=(ROWS // QBLOCK,),
            in_specs=[whole, whole],
            out_specs=[made, made],
        ),
        out_shape=[jax.ShapeDtypeStruct((chips, ROWS // 2, PAIR), bf16)] * 2,
        compiler_params=limit,
        cost_estimate=brief,
        name="quantize",
    )(pos, frag_start, frag_current)
    return keep.reshape(N_Y, N_XH, ROWS // 2, PAIR), sent.reshape(N_Y, N_XH, ROWS // 2, PAIR)


def outer_kernel(pos_ref, own_ref, far_ref, anchor_ref, momentum_ref, unread_ref, new_anchor, new_momentum, params, native, fresh):
    low_lane = lax.broadcasted_iota(jnp.int32, (64, 128), 1) < 64
    first_core = pos_ref[0] == 0
    for block in range(ROWS // QBLOCK):
        message = slice(block * 64, block * 64 + 64)
        total = own_ref[message].astype(f32) + far_ref[message].astype(f32)
        rest = total[:, 512:640]
        for half, tail in ((0, rest), (1, pltpu.roll(rest, 64, 1))):
            rows = slice(block * 128 + half * 64, block * 128 + half * 64 + 64)
            main0 = total[:, half * 256 : half * 256 + 128]
            main1 = total[:, half * 256 + 128 : half * 256 + 256]
            turn0, turn1 = pltpu.roll(main0, 64, 1), pltpu.roll(main1, 64, 1)
            native[rows, 0:128] = jnp.where(first_core, main0, jnp.where(low_lane, tail, turn0))
            native[rows, 128:256] = jnp.where(first_core, main1, jnp.where(low_lane, turn0, turn1))
            native[rows, 256:384] = jnp.where(first_core, tail, turn1)
        rows = slice(block * 128, block * 128 + 128)
        average = native[rows, 0:COL] / float(N_Y * N_XH * N_CORE)
        momentum = momentum_decay * momentum_ref[rows] + average
        anchor = anchor_ref[rows] - outer_rate * (average + momentum_decay * momentum)
        new_momentum[rows] = momentum
        new_anchor[rows] = anchor
        fresh[rows, 0:COL] = anchor
        for half in range(2):
            rows = slice(block * 128 + half * 64, block * 128 + half * 64 + 64)
            tiles = [fresh[rows, t * 128 : t * 128 + 128] for t in range(3)]
            turn = [pltpu.roll(tile, 64, 1) for tile in tiles]
            for t in range(2):
                value = jnp.where(first_core, tiles[t], jnp.where(low_lane, turn[t], turn[t + 1]))
                at = half * 256 + t * 128
                params[message, at : at + 128] = value.astype(bf16)
            if half == 0:
                top = jnp.where(first_core, tiles[2], tiles[0])
            else:
                bottom = jnp.where(first_core, turn[2], turn[0])
        params[message, 512:640] = jnp.where(low_lane, top, bottom).astype(bf16)


def outer_update(pos, own, far, anchor, momentum, after):
    held = pl.BlockSpec(memory_space=pltpu.VMEM)
    return pl.pallas_call(
        outer_kernel,
        in_specs=[pl.BlockSpec(memory_space=pltpu.SMEM)] + [held] * 4 + [unread],
        out_specs=[held] * 3,
        scratch_shapes=[pltpu.VMEM((ROWS, 384), f32), pltpu.VMEM((ROWS, 384), f32)],
        out_shape=[
            jax.ShapeDtypeStruct((ROWS, COL), f32),
            jax.ShapeDtypeStruct((ROWS, COL), f32),
            jax.ShapeDtypeStruct((ROWS // 2, PAIR), bf16),
        ],
        compiler_params=limit,
        cost_estimate=brief,
        name="outer_update",
    )(pos, own, far, anchor, momentum, after)


def place_kernel(chips, after, pos_ref, *refs):
    out = refs[-1]
    count = sum(pieces for _, _, pieces in chips)
    mine, theirs = refs[:count], refs[count : 2 * count]
    first_core = pos_ref[0] == 0
    step = pl.program_id(0)
    early = step < pl.num_programs(0) // 2
    size = mine[0].shape[0]
    at = pl.multiple_of(lax.rem(step, 64 // size) * size, size)
    low_lane = lax.broadcasted_iota(jnp.int32, (size, 128), 1) < 64
    index = 0
    for dy, dx, pieces in chips:
        a, b = mine[index][...], theirs[index][...]
        if pieces == 2:
            a = jnp.where(early, a, mine[index + 1][...])
            b = jnp.where(early, b, theirs[index + 1][...])
        index += pieces
        low, high = jnp.where(first_core, a, b), jnp.where(first_core, b, a)
        chip = lax.rem(pos_ref[2] + dx, N_XH) * N_Y + lax.rem(pos_ref[1] + dy, N_Y)

        def put(half, lane, value):
            lanes = pl.ds(pl.multiple_of(chip * PAIR + lane, 128), value.shape[1])
            out[pl.ds(at + half * 64, size), lanes] = value

        for half in range(2):
            put(half, 0, low[:, half * 256 : half * 256 + 256])
            put(half, 384, high[:, half * 256 : half * 256 + 256])
        low_rest, high_rest = low[:, 512:640].astype(f32), high[:, 512:640].astype(f32)
        put(0, 256, jnp.where(low_lane, low_rest, pltpu.roll(high_rest, 64, 1)).astype(bf16))
        put(1, 256, jnp.where(low_lane, pltpu.roll(low_rest, 64, 1), high_rest).astype(bf16))


def place(pos, chips, mine, theirs, after):
    size = 32
    steps = ROWS // 2 // size

    def block(piece, pieces):
        if pieces == 1:
            return pl.BlockSpec((size, PAIR), lambda i, pos: (i, 0))
        if piece == 0:
            return pl.BlockSpec((size, PAIR), lambda i, pos: (jnp.minimum(i, steps // 2 - 1), 0))
        return pl.BlockSpec((size, PAIR), lambda i, pos: (jnp.maximum(i - steps // 2, 0), 0))

    blocks = [block(piece, pieces) for _, _, pieces in chips for piece in range(pieces)]
    return pl.pallas_call(
        functools.partial(place_kernel, chips, len(after)),
        grid_spec=pltpu.PrefetchScalarGridSpec(
            num_scalar_prefetch=1,
            grid=(steps,),
            in_specs=blocks * 2 + [unread] * len(after),
            out_specs=pl.BlockSpec((QBLOCK, N_Y * N_XH * PAIR), lambda i, pos: (i // (64 // size), 0)),
        ),
        out_shape=jax.ShapeDtypeStruct((ROWS, N_Y * N_XH * PAIR), bf16),
        compiler_params=limit,
        cost_estimate=brief,
        name="place",
    )(pos, *mine, *theirs, *after)


def halves_kernel(after, below, above, *refs):
    first, second = refs[after:]
    first[...] = below[...]
    second[...] = above[...]


def halves(below, above, after):
    rows, columns = below.shape
    shape = jax.ShapeDtypeStruct((rows // 2, columns), below.dtype)
    part = [pl.BlockSpec((rows // 2, columns), lambda i, j=j: (j, 0)) for j in range(2)]
    return pl.pallas_call(
        functools.partial(halves_kernel, len(after)),
        grid=(1,),
        in_specs=part + [unread] * len(after),
        out_specs=[part[0], part[0]],
        out_shape=[shape, shape],
        compiler_params=limit,
        cost_estimate=brief,
        name="halves",
    )(below, above, *after)


def join_kernel(after, *refs):
    parts, out = refs[: -1 - after], refs[-1]
    at = 0
    for part in parts:
        out[at : at + part.shape[0]] = part[...]
        at += part.shape[0]


def join(parts, after):
    count = sum(part.shape[0] for part in parts)
    return pl.pallas_call(
        functools.partial(join_kernel, len(after)),
        in_specs=[pl.BlockSpec(memory_space=pltpu.VMEM)] * len(parts) + [unread] * len(after),
        out_shape=jax.ShapeDtypeStruct((count,) + parts[0].shape[1:], f32),
        compiler_params=limit,
        cost_estimate=brief,
        name="join",
    )(*parts, *after)


def settle_kernel(a, b, a_out, b_out, token):
    del a, b, a_out, b_out
    token[...] = jnp.zeros_like(token)


def settle(a, b):
    return pl.pallas_call(
        settle_kernel,
        in_specs=[unread] * 2,
        out_specs=[unread] * 2 + [pl.BlockSpec(memory_space=pltpu.VMEM)],
        out_shape=[jax.ShapeDtypeStruct(x.shape, x.dtype) for x in (a, b)] + [jax.ShapeDtypeStruct((8, 128), f32)],
        input_output_aliases={0: 0, 1: 1},
        cost_estimate=brief,
        name="settle",
    )(a, b)


def gate_kernel(*refs):
    del refs


def gate(arrays, after):
    count = len(arrays)
    return pl.pallas_call(
        gate_kernel,
        in_specs=[unread] * (count + len(after)),
        out_specs=[unread] * count,
        out_shape=[jax.ShapeDtypeStruct(a.shape, a.dtype) for a in arrays],
        input_output_aliases={i: i for i in range(count)},
        cost_estimate=brief,
        name="gate",
    )(*arrays, *after)


def total(*refs):
    return sum(ref.astype(f32) for ref in refs)


def spot(dy, x, rows, columns, part=0):
    return pl.BlockSpec((1, 1, rows, columns), lambda i: (dy, x, part, 0))


def first_kernel(keep1, got1, keep2, got2, keep3, got3, up, down):
    half = up.shape[1]
    low, high = slice(0, half), slice(half, 2 * half)
    up[0] = total(keep2[0, 0, low], got2[0, 0, low]).astype(bf16)
    down[0] = total(keep2[0, 0, high], got2[0, 0, high]).astype(bf16)
    up[1] = total(keep1[0, 0], got1[0, 0]).astype(bf16)
    down[1] = total(keep3[0, 0], got3[0, 0]).astype(bf16)


def first_messages(keep, got, x, after):
    _, _, rows, columns = keep.shape
    half = rows // 2
    part = pl.BlockSpec((2, half, columns), lambda i: (0, 0, 0))
    shape = jax.ShapeDtypeStruct((2, half, columns), bf16)

    def kernel(*refs):
        first_kernel(*refs[:6], *refs[6 + len(after) :])

    return pl.pallas_call(
        kernel,
        grid=(1,),
        in_specs=[spot(1, x, half, columns, 1)] * 2
        + [spot(2, x, rows, columns)] * 2
        + [spot(3, x, half, columns, 0)] * 2
        + [unread] * len(after),
        out_specs=[part] * 2,
        out_shape=[shape] * 2,
        compiler_params=limit,
        cost_estimate=brief,
        name="first_messages",
    )(keep, got, keep, got, keep, got, *after)


def second_kernel(keep1, got1, keep3, got3, up, down, up_out, down_out):
    up_out[...] = total(keep1[0, 0], got1[0, 0], up[0]).astype(bf16)
    down_out[...] = total(keep3[0, 0], got3[0, 0], down[0]).astype(bf16)


def second_messages(keep, got, up, down, x):
    _, _, rows, columns = keep.shape
    half = rows // 2
    came = pl.BlockSpec((1, half, columns), lambda i: (0, 0, 0))
    part = pl.BlockSpec((half, columns), lambda i: (0, 0))
    shape = jax.ShapeDtypeStruct((half, columns), bf16)
    return pl.pallas_call(
        second_kernel,
        grid=(1,),
        in_specs=[spot(1, x, half, columns, 0)] * 2 + [spot(3, x, half, columns, 1)] * 2 + [came] * 2,
        out_specs=[part] * 2,
        out_shape=[shape] * 2,
        compiler_params=limit,
        cost_estimate=brief,
        name="second_messages",
    )(keep, got, keep, got, up, down)


def chip_kernel(keep, got, up, down, up2, down2, out):
    half = up.shape[1]
    low, high = slice(0, half), slice(half, 2 * half)
    out[low] = total(keep[0, 0, low], got[0, 0, low], down[0], up2[...]).astype(out.dtype)
    out[high] = total(keep[0, 0, high], got[0, 0, high], up[0], down2[...]).astype(out.dtype)


def chip_sum(keep, got, up, down, up2, down2, x, dtype):
    _, _, rows, columns = keep.shape
    came = pl.BlockSpec((1, rows // 2, columns), lambda i: (1, 0, 0))
    part = pl.BlockSpec((rows // 2, columns), lambda i: (0, 0))
    return pl.pallas_call(
        chip_kernel,
        grid=(1,),
        in_specs=[spot(0, x, rows, columns)] * 2 + [came] * 2 + [part] * 2,
        out_specs=pl.BlockSpec((rows, columns), lambda i: (0, 0)),
        out_shape=jax.ShapeDtypeStruct((rows, columns), dtype),
        compiler_params=limit,
        cost_estimate=brief,
        name="chip_sum",
    )(keep, got, up, down, up2, down2)


def per_device(
    latents,
    target,
    timesteps,
    patch_weight,
    head_weight,
    modulation,
    time_weight,
    anchor,
    momentum,
    frag_start,
    frag_current,
):
    frag_current = frag_current[0]
    params = (patch_weight[0], head_weight[0], modulation[0], time_weight[0])
    columns = params[0].shape[1]
    width = float(columns * N_FSDP)
    tokens = float(latents.shape[0] * N_FSDP)
    replica = lax.axis_index("replica")
    pos = jnp.stack([replica % 2, (replica // 2) % 4, replica // 8]).astype(jnp.int32)

    to_core = [(r, r ^ 1) for r in range(16)]
    to_x = [(r, r ^ 8) for r in range(16)]

    def to_y(step):
        return [
            (xh * 8 + y * 2 + c, xh * 8 + ((y + step) % N_Y) * 2 + c)
            for xh in range(N_XH)
            for y in range(N_Y)
            for c in range(N_CORE)
        ]

    send = functools.partial(lax.ppermute, axis_name="replica")
    to_sibling = functools.partial(send, perm=to_core)

    def across(value, bit):
        return lax.ppermute(value, "fsdp", [(i, i ^ bit) for i in range(N_FSDP)])

    h0 = step_head(timesteps, params[0])[None]
    h1 = across(h0, 1)
    keep, sent = quantize(pos, frag_start, frag_current)
    got = to_sibling(sent)
    h01 = join([h0, h1], [keep])
    h2 = across(h01, 2)
    up, down = [None, None], [None, None]

    def ring(x, messages):
        up[x], down[x] = send(messages[0], perm=to_y(1)), send(messages[1], perm=to_y(-1))

    message = first_messages(keep, got, 1, [])
    ring(1, message)
    h03 = join([h01, h2], [message[0]])
    h4 = across(h03, 4)
    near, away, pre, center, sines = weight_products(h03, h4, *params, [message[0]], width)
    away = across(away, 4)
    away2 = across(near[2:4] + away[2:4], 2)
    away1 = across(near[1:2] + away[1:2] + away2[1:2], 1)

    far = second_messages(keep, got, up[1], down[1], 1)
    far_up, far_down = send(far[0], perm=to_y(1)), send(far[1], perm=to_y(-1))
    ring(0, first_messages(keep, got, 0, [far[0]]))
    far = send(chip_sum(keep, got, up[1], down[1], far_up, far_down, 1, bf16), perm=to_x)
    own = second_messages(keep, got, up[0], down[0], 0)
    own_up, own_down = send(own[0], perm=to_y(1)), send(own[1], perm=to_y(-1))
    q0 = token_sums(near[0:1] + away[0:1] + away2[0:1], away1, latents.T, target.T, [anchor, momentum], width, tokens)
    q1 = across(q0, 1)
    own = chip_sum(keep, got, up[0], down[0], own_up, own_down, 0, f32)
    new_anchor, new_momentum, n0 = outer_update(pos, own, far, anchor, momentum, q0)

    n1 = send(n0, perm=to_x)
    up0, down0 = send(n0, perm=to_y(1)), send(n0, perm=to_y(-1))
    q01 = join([q0, q1], [])
    q2 = across(q01, 2)
    anchor_t, momentum_t, settled = settle(new_anchor.T, new_momentum.T)
    q4 = across(join([q01, q2], []), 4)
    first0 = halves(up0, down0, [])
    on0 = send(first0[0], perm=to_y(1)), send(first0[1], perm=to_y(-1))
    up1, down1 = send(n1, perm=to_y(1)), send(n1, perm=to_y(-1))
    inner = finish(q0, q1, q2, q4, pre, center, sines, params, [])
    first1 = halves(up1, down1, [])
    on1 = send(first1[0], perm=to_y(1)), send(first1[1], perm=to_y(-1))
    mine = [n0, up0, down0, n1, up1, down1, *on0]
    mine = gate(mine, [first1[0], inner[2], settled])
    mine = [*mine, *on1]
    theirs = [to_sibling(part) for part in mine]
    chips = ((0, 0, 1), (3, 0, 1), (1, 0, 1), (0, 1, 1), (3, 1, 1), (1, 1, 1), (2, 0, 2), (2, 1, 2))
    new_params = place(pos, chips, mine, theirs, [inner[2], settled])
    return tuple(a[None] for a in inner) + (anchor_t.T, momentum_t.T, new_params)


def column(row):
    eye = lax.broadcasted_iota(jnp.int32, (64, 128), 0) == lax.broadcasted_iota(jnp.int32, (64, 128), 1)
    return jnp.sum(jnp.where(eye, row, 0.0), axis=1, keepdims=True)


def gains(pre, mod_ref):
    embed = pre * jax.nn.sigmoid(pre)
    mod = mod_ref[...].astype(bf16).astype(f32)
    return 1.0 + mod[1:2] + embed, mod[0:1] + embed


def weights_kernel(width, after, near_heads, away_heads, patch_ref, head_ref, mod_ref, time_ref, *refs):
    near, away, pre_ref, center_ref, sines_ref, high, low = refs[after:]
    count = N_FSDP
    total = jnp.zeros((1, 128), f32)
    for k in range(count):
        head = (near_heads if k < count // 2 else away_heads)[k % (count // 2)]
        total = total + head[8:9]
        sines_ref[4 * k : 4 * k + 4, 0:128] = head[0:4]
        sines_ref[4 * k : 4 * k + 4, 128:256] = head[4:8]
    pre = dot(sines_ref[...].astype(bf16), time_ref[...].astype(bf16), NN)
    pre_ref[...] = pre
    gain, shift = gains(pre, mod_ref)
    center = patch_ref[...].astype(bf16).astype(f32) - column(total / width)
    center_ref[...] = center
    samples = 4 * count
    for s in range(samples):
        k, i = s // 4, s % 4
        at = (i // 2) * (samples // 2 * 64) + (2 * k + i % 2) * 64
        hi, lo = split2(center * gain[s : s + 1])
        high[at : at + 64, :] = hi
        low[at : at + 64, :] = lo
    head = head_ref[...].astype(bf16)
    blank = jnp.zeros_like(head)
    left = jnp.concatenate([head, blank], axis=0)
    right = jnp.concatenate([blank, head], axis=0)
    part = samples // 2 * 64
    packed = dot(high[0:part], left, NT) + dot(low[0:part], left, NT)
    packed = packed + dot(high[part:], right, NT) + dot(low[part:], right, NT)
    chi, clo = split2(center)
    chi_left = jnp.concatenate([chi, blank], axis=0)
    clo_left = jnp.concatenate([clo, blank], axis=0)
    gram = dot(chi, chi_left, NT) + dot(clo, chi_left, NT) + dot(chi, clo_left, NT)
    for k in range(count):
        out = near if k < count // 2 else away
        slot = k % (count // 2)
        rows = jnp.concatenate([shift[4 * k : 4 * k + 4], gain[4 * k : 4 * k + 4]], axis=0)
        hi, lo = split2(rows)
        extra = dot(hi, right, NT) + dot(lo, right, NT)
        out[slot, 0:128, :] = packed[128 * k : 128 * k + 128]
        out[slot, 128:136, :] = gram[0:8] + extra
        out[slot, 136:192, :] = gram[8:64]


def row(column):
    eye = lax.broadcasted_iota(jnp.int32, (64, 128), 0) == lax.broadcasted_iota(jnp.int32, (64, 128), 1)
    return jnp.sum(jnp.where(eye, column, 0.0), axis=0, keepdims=True)


def tokens_kernel(width, tokens, after, own_ref, away_ref, latent_ref, target_ref, *refs):
    out, wide = refs[after:]
    total = own_ref[0] + away_ref[0]
    turned = pltpu.roll(total, 64, 1)
    gram = total[128:192, 0:64] / width
    g0 = gram.astype(bf16)
    g1, g2 = split2(gram - g0.astype(f32))
    gain_means = turned[132:136, :] / width
    wide[...] = jnp.zeros_like(wide)
    curve = jnp.zeros((64, 64), f32)
    sums = []
    for s in range(4):
        at = slice(s * SAMPLE_TOKENS, (s + 1) * SAMPLE_TOKENS)
        latent = latent_ref[:, at]
        latent_f = latent.astype(f32)
        mix = (total if s < 2 else turned)[(s % 2) * 64 : (s % 2) * 64 + 64, 0:64]
        mix_hi, mix_lo = split2(mix)
        spread = dot(g0, latent, NN) + dot(g1, latent, NN) + dot(g2, latent, NN)
        variance = jnp.sum(spread * latent_f, axis=0, keepdims=True)
        inv_std = lax.rsqrt(jnp.maximum(variance, 0.0) + epsilon)
        varied = inv_std * (dot(mix_hi, latent, TN) + dot(mix_lo, latent, TN))
        output = varied + column(turned[128 + s : 129 + s, :])
        grad_out = (2.0 * (output - target_ref[:, at].astype(f32)) / tokens).astype(bf16)
        grad_f = grad_out.astype(f32)
        along = jnp.sum(grad_f * varied, axis=0, keepdims=True) / width
        cross = dot((grad_f * inv_std).astype(bf16), latent, NT)
        curve = curve + dot((latent_f * (along * inv_std * inv_std)).astype(bf16), latent, NT)
        sums.append(row(jnp.sum(grad_f, axis=1, keepdims=True)))
        if s < 2:
            out[0, s * 64 : s * 64 + 64, 0:64] = cross
        else:
            wide[(s - 2) * 64 : (s - 2) * 64 + 64, 0:64] = cross
    for s in range(4):
        wide[128 + s : 129 + s, :] = sums[s]
    wide[132:136, 0:64] = gain_means[:, 0:64]
    packed = pltpu.roll(wide[...], 64, 1)
    low_lane = lax.broadcasted_iota(jnp.int32, (128, 128), 1) < 64
    out[0, 0:128, :] = jnp.where(low_lane, out[0, 0:128, :], packed[0:128])
    wide[128:192, 0:64] = curve
    out[0, 128:192, :] = jnp.where(low_lane[0:64], wide[128:192, :], packed[128:192])


def finish_kernel(
    after,
    parts0,
    parts1,
    parts2,
    parts4,
    pre_ref,
    center_ref,
    sines_ref,
    patch_ref,
    head_ref,
    mod_ref,
    time_ref,
    *refs,
):
    patch_new, head_new, mod_new, time_new, sums, slope_rows = refs[after:]
    count = N_FSDP
    parts = [ref[i] for ref in (parts0, parts1, parts2, parts4) for i in range(ref.shape[0])]
    pre = pre_ref[...]
    gain, shift = gains(pre, mod_ref)
    head = head_ref[...].astype(bf16)
    head_f = head.astype(f32)
    center = center_ref[...]
    chi, clo = split2(center)
    curve = parts[0][128:192, 0:64]
    for k in range(1, count):
        curve = curve + parts[k][128:192, 0:64]
    curve_hi, curve_lo = split2(curve)
    grad_patch = -(dot(curve_hi, chi, NN) + dot(curve_lo, chi, NN) + dot(curve_hi, clo, NN))
    grad_head = jnp.zeros_like(center)
    grad_scale = jnp.zeros_like(gain[0:1])
    for k in range(count):
        plain = parts[k]
        turned = pltpu.roll(plain, 64, 1)
        sums[4 * k : 4 * k + 4, :] = turned[128:132]
        crosses, fine = split2(jnp.concatenate([plain[0:128, 0:64], turned[0:128, 0:64]], axis=0))
        mixed = dot(crosses, chi, NN) + dot(fine, chi, NN) + dot(crosses, clo, NN)
        pulls = []
        for i in range(4):
            s = 4 * k + i
            one = mixed[i * 64 : i * 64 + 64]
            grad_head = grad_head + one * gain[s : s + 1]
            slope = jnp.sum(head_f * one, axis=0, keepdims=True)
            slope_rows[s : s + 1, :] = slope
            grad_scale = grad_scale + slope
            pulls.append((head_f * gain[s : s + 1] - column(turned[132 + i : 133 + i])).astype(bf16))
        grad_patch = grad_patch + dot(crosses, jnp.concatenate(pulls, axis=0), TN)
    sum_hi, sum_lo = split2(sums[:, 0:64])
    shift_hi, shift_lo = split2(shift)
    grad_head = grad_head + dot(sum_hi, shift_hi, TN) + dot(sum_lo, shift_hi, TN) + dot(sum_hi, shift_lo, TN)
    mixed_sums = dot(sum_hi, head, NN) + dot(sum_lo, head, NN)
    grad_shift = jnp.sum(mixed_sums, axis=0, keepdims=True)
    grad_embed = mixed_sums + slope_rows[...]
    sigmoid = jax.nn.sigmoid(pre)
    grad_pre = (grad_embed * (sigmoid * (1.0 + pre * (1.0 - sigmoid)))).astype(bf16)
    grad_time = dot(sines_ref[...].astype(bf16), grad_pre, TN)
    patch_new[...] = patch_ref[...] - inner_rate * grad_patch
    head_new[...] = head_ref[...] - inner_rate * grad_head
    mod_new[0:1, :] = mod_ref[0:1, :] - inner_rate * grad_shift
    mod_new[1:2, :] = mod_ref[1:2, :] - inner_rate * grad_scale
    time_new[...] = time_ref[...] - inner_rate * grad_time


def sinusoid(time_steps):
    index = jnp.arange(FREQ_DIM // 2, dtype=f32)
    frequency = jnp.exp(-math.log(10000.0) * index / (FREQ_DIM // 2))
    angles = time_steps.astype(f32)[:, None] * frequency[None, :]
    return jnp.cos(angles), jnp.sin(angles)


def step_head(timesteps, patch):
    cos, sin = sinusoid(timesteps)
    row_sums = jnp.sum(patch.astype(bf16).astype(f32), axis=1)
    return jnp.concatenate(
        [cos, sin, jnp.pad(row_sums, (0, 128 - PATCH_DIM))[None], jnp.zeros((7, 128), f32)], axis=0
    )


def weight_products(near, away, patch, head, mod, time, after, width):
    columns = patch.shape[1]
    samples = 4 * N_FSDP
    share = jax.ShapeDtypeStruct((N_FSDP // 2, 192, 128), f32)
    return pl.pallas_call(
        functools.partial(weights_kernel, width, len(after)),
        in_specs=[pl.BlockSpec(memory_space=pltpu.VMEM)] * 6 + [unread] * len(after),
        out_shape=[
            share,
            share,
            jax.ShapeDtypeStruct((samples, columns), f32),
            jax.ShapeDtypeStruct((PATCH_DIM, columns), f32),
            jax.ShapeDtypeStruct((samples, FREQ_DIM), f32),
        ],
        scratch_shapes=[pltpu.VMEM((samples * PATCH_DIM, columns), bf16)] * 2,
        compiler_params=limit,
        cost_estimate=brief,
        name="weight_products",
    )(near, away, patch, head, mod, time, *after)


def token_sums(own, away, latents, target, after, width, tokens):
    return pl.pallas_call(
        functools.partial(tokens_kernel, width, tokens, len(after)),
        in_specs=[pl.BlockSpec(memory_space=pltpu.VMEM)] * 4 + [unread] * len(after),
        out_shape=jax.ShapeDtypeStruct((1, 192, 128), f32),
        scratch_shapes=[pltpu.VMEM((192, 128), f32)],
        compiler_params=limit,
        cost_estimate=brief,
        name="token_sums",
    )(own, away, latents, target, *after)


def finish(q0, q1, q2, q4, pre, center, sines, params, after):
    samples, columns = pre.shape
    return pl.pallas_call(
        functools.partial(finish_kernel, len(after)),
        in_specs=[pl.BlockSpec(memory_space=pltpu.VMEM)] * 11 + [unread] * len(after),
        out_shape=[jax.ShapeDtypeStruct(a.shape, f32) for a in params],
        scratch_shapes=[pltpu.VMEM((samples, 128), f32), pltpu.VMEM((samples, columns), f32)],
        compiler_params=limit,
        cost_estimate=brief,
        name="finish",
    )(q0, q1, q2, q4, pre, center, sines, *params, *after)


def solution(mesh):
    in_specs = (
        P(("replica", "fsdp"), None),
        P(("replica", "fsdp"), None),
        P(("replica", "fsdp")),
        P("replica", None, "fsdp"),
        P("replica", None, "fsdp"),
        P("replica", None, "fsdp"),
        P("replica", None, "fsdp"),
        P("fsdp", "replica"),
        P("fsdp", "replica"),
        P("fsdp", None),
        P("replica", "fsdp", None),
    )
    out_specs = (
        P("replica", None, "fsdp"),
        P("replica", None, "fsdp"),
        P("replica", None, "fsdp"),
        P("replica", None, "fsdp"),
        P("fsdp", "replica"),
        P("fsdp", "replica"),
        P("fsdp", None),
    )
    return jax.shard_map(
        per_device, mesh=mesh, in_specs=in_specs, out_specs=out_specs, check_vma=False
    )
```

```python
import functools
import math

import jax
import jax.numpy as jnp
from jax import lax
from jax.experimental import pallas as pl
from jax.experimental.pallas import tpu as pltpu
from jax.sharding import PartitionSpec as P

FREQ_DIM = 256
PATCH_DIM = 64
QBLOCK = 128
SAMPLE_TOKENS = 512

epsilon = 1e-06
inner_rate = 0.5
outer_rate = 0.7
momentum_decay = 0.9

f32 = jnp.float32
bf16 = jnp.bfloat16

N_Y, N_XH, N_CORE, N_FSDP = 4, 2, 2, 8
COL = 320
PAIR = 640
ROWS = 640
ROUND = 1.5 * 2.0**23
NUDGE = 1.0 + 2.0**-21

limit = pltpu.CompilerParams(vmem_limit_bytes=56 * 2**20)
brief = pl.CostEstimate(flops=1, bytes_accessed=1, transcendentals=0)
unread = pl.BlockSpec(memory_space=pl.ANY)

NT = (((1,), (1,)), ((), ()))
TN = (((0,), (0,)), ((), ()))
NN = (((1,), (0,)), ((), ()))


def dot(a, b, dims):
    return lax.dot_general(a, b, dims, preferred_element_type=f32)


def split2(x):
    hi = x.astype(bf16)
    return hi, (x - hi.astype(f32)).astype(bf16)


def quantized(delta):
    peak = jnp.max(jnp.abs(delta), axis=0, keepdims=True)
    scale = (peak + epsilon).astype(bf16).astype(f32)
    ratio = (7.0 / scale) * NUDGE
    shifted = delta * ratio + ROUND
    code = jnp.clip(shifted, ROUND - 7.0, ROUND + 7.0) - ROUND
    return code * (scale / 7.0)


def quant_kernel(pos_ref, start_ref, current_ref, keep, send):
    first_core = pos_ref[0] == 0
    low_lane = lax.broadcasted_iota(jnp.int32, (64, 128), 1) < 64
    for chip in range(N_Y * N_XH):
        dy = lax.rem(chip % N_Y - pos_ref[1] + N_Y, N_Y)
        dx = lax.rem(chip // N_Y - pos_ref[2] + N_XH, N_XH)
        slot = dy * N_XH + dx

        def terms(tile):
            lanes = slice(chip * PAIR + tile * 128, chip * PAIR + (tile + 1) * 128)
            return quantized(start_ref[:, lanes].astype(f32) - current_ref[:, lanes].astype(f32))

        def put(lane, low, high):
            keep[slot, :, lane : lane + 128] = jnp.where(first_core, low, high).astype(bf16)
            send[slot, :, lane : lane + 128] = jnp.where(first_core, high, low).astype(bf16)

        for tile in range(2):
            low, high = terms(tile), terms(tile + 3)
            put(tile * 128, low[:64], high[:64])
            put(256 + tile * 128, low[64:], high[64:])
        both = terms(2)
        top, bottom = both[:64], both[64:]
        low = jnp.where(low_lane, top, pltpu.roll(bottom, 64, 1))
        high = jnp.where(low_lane, pltpu.roll(top, 64, 1), bottom)
        put(512, low, high)


def quantize(pos, frag_start, frag_current):
    chips = N_Y * N_XH
    whole = pl.BlockSpec((QBLOCK, frag_start.shape[1]), lambda i, pos: (i, 0))
    made = pl.BlockSpec((chips, QBLOCK // 2, PAIR), lambda i, pos: (0, i, 0))
    keep, sent = pl.pallas_call(
        quant_kernel,
        grid_spec=pltpu.PrefetchScalarGridSpec(
            num_scalar_prefetch=1,
            grid=(ROWS // QBLOCK,),
            in_specs=[whole, whole],
            out_specs=[made, made],
        ),
        out_shape=[jax.ShapeDtypeStruct((chips, ROWS // 2, PAIR), bf16)] * 2,
        compiler_params=limit,
        cost_estimate=brief,
        name="quantize",
    )(pos, frag_start, frag_current)
    return keep.reshape(N_Y, N_XH, ROWS // 2, PAIR), sent.reshape(N_Y, N_XH, ROWS // 2, PAIR)


def outer_kernel(pos_ref, own_ref, far_ref, anchor_ref, momentum_ref, unread_ref, new_anchor, new_momentum, params, native, fresh):
    low_lane = lax.broadcasted_iota(jnp.int32, (64, 128), 1) < 64
    first_core = pos_ref[0] == 0
    for block in range(ROWS // QBLOCK):
        message = slice(block * 64, block * 64 + 64)
        total = own_ref[message].astype(f32) + far_ref[message].astype(f32)
        rest = total[:, 512:640]
        for half, tail in ((0, rest), (1, pltpu.roll(rest, 64, 1))):
            rows = slice(block * 128 + half * 64, block * 128 + half * 64 + 64)
            main0 = total[:, half * 256 : half * 256 + 128]
            main1 = total[:, half * 256 + 128 : half * 256 + 256]
            turn0, turn1 = pltpu.roll(main0, 64, 1), pltpu.roll(main1, 64, 1)
            native[rows, 0:128] = jnp.where(first_core, main0, jnp.where(low_lane, tail, turn0))
            native[rows, 128:256] = jnp.where(first_core, main1, jnp.where(low_lane, turn0, turn1))
            native[rows, 256:384] = jnp.where(first_core, tail, turn1)
        rows = slice(block * 128, block * 128 + 128)
        average = native[rows, 0:COL] / float(N_Y * N_XH * N_CORE)
        momentum = momentum_decay * momentum_ref[rows] + average
        anchor = anchor_ref[rows] - outer_rate * (average + momentum_decay * momentum)
        new_momentum[rows] = momentum
        new_anchor[rows] = anchor
        fresh[rows, 0:COL] = anchor
        for half in range(2):
            rows = slice(block * 128 + half * 64, block * 128 + half * 64 + 64)
            tiles = [fresh[rows, t * 128 : t * 128 + 128] for t in range(3)]
            turn = [pltpu.roll(tile, 64, 1) for tile in tiles]
            for t in range(2):
                value = jnp.where(first_core, tiles[t], jnp.where(low_lane, turn[t], turn[t + 1]))
                at = half * 256 + t * 128
                params[message, at : at + 128] = value.astype(bf16)
            if half == 0:
                top = jnp.where(first_core, tiles[2], tiles[0])
            else:
                bottom = jnp.where(first_core, turn[2], turn[0])
        params[message, 512:640] = jnp.where(low_lane, top, bottom).astype(bf16)


def outer_update(pos, own, far, anchor, momentum, after):
    held = pl.BlockSpec(memory_space=pltpu.VMEM)
    return pl.pallas_call(
        outer_kernel,
        in_specs=[pl.BlockSpec(memory_space=pltpu.SMEM)] + [held] * 4 + [unread],
        out_specs=[held] * 3,
        scratch_shapes=[pltpu.VMEM((ROWS, 384), f32), pltpu.VMEM((ROWS, 384), f32)],
        out_shape=[
            jax.ShapeDtypeStruct((ROWS, COL), f32),
            jax.ShapeDtypeStruct((ROWS, COL), f32),
            jax.ShapeDtypeStruct((ROWS // 2, PAIR), bf16),
        ],
        compiler_params=limit,
        cost_estimate=brief,
        name="outer_update",
    )(pos, own, far, anchor, momentum, after)


def place_kernel(chips, pos_ref, *refs):
    out = refs[-1]
    count = sum(2 if cut else 1 for _, _, cut in chips)
    mine, theirs = refs[:count], refs[count : 2 * count]
    first_core = pos_ref[0] == 0
    low_lane = lax.broadcasted_iota(jnp.int32, (64, 128), 1) < 64
    index = 0
    for dy, dx, cut in chips:
        a, b = mine[index][...], theirs[index][...]
        index += 1
        if cut:
            early = pl.program_id(0) < cut
            a = jnp.where(early, a, mine[index][...])
            b = jnp.where(early, b, theirs[index][...])
            index += 1
        low, high = jnp.where(first_core, a, b), jnp.where(first_core, b, a)
        chip = lax.rem(pos_ref[2] + dx, N_XH) * N_Y + lax.rem(pos_ref[1] + dy, N_Y)

        def put(half, lane, value):
            lanes = pl.ds(pl.multiple_of(chip * PAIR + lane, 128), value.shape[1])
            out[half * 64 : half * 64 + 64, lanes] = value

        for half in range(2):
            put(half, 0, low[:, half * 256 : half * 256 + 256])
            put(half, 384, high[:, half * 256 : half * 256 + 256])
        low_rest, high_rest = low[:, 512:640].astype(f32), high[:, 512:640].astype(f32)
        put(0, 256, jnp.where(low_lane, low_rest, pltpu.roll(high_rest, 64, 1)).astype(bf16))
        put(1, 256, jnp.where(low_lane, pltpu.roll(low_rest, 64, 1), high_rest).astype(bf16))


def place(pos, chips, mine, theirs, after):
    def blocks(cut):
        if not cut:
            return [pl.BlockSpec((64, PAIR), lambda i, pos: (i, 0))]
        return [
            pl.BlockSpec((64, PAIR), lambda i, pos: (jnp.minimum(i, cut - 1), 0)),
            pl.BlockSpec((64, PAIR), lambda i, pos: (jnp.maximum(i - cut, 0), 0)),
        ]

    specs = [spec for _, _, cut in chips for spec in blocks(cut)]
    return pl.pallas_call(
        functools.partial(place_kernel, chips),
        grid_spec=pltpu.PrefetchScalarGridSpec(
            num_scalar_prefetch=1,
            grid=(ROWS // QBLOCK,),
            in_specs=specs * 2 + [unread] * len(after),
            out_specs=pl.BlockSpec((QBLOCK, N_Y * N_XH * PAIR), lambda i, pos: (i, 0)),
        ),
        out_shape=jax.ShapeDtypeStruct((ROWS, N_Y * N_XH * PAIR), bf16),
        compiler_params=limit,
        cost_estimate=brief,
        name="place",
    )(pos, *mine, *theirs, *after)


def parts_kernel(below, above, first, second):
    cut = first.shape[0]
    first[...] = below[0:cut]
    second[...] = above[cut:]


def parts(below, above, cut):
    rows, columns = below.shape
    return pl.pallas_call(
        parts_kernel,
        out_shape=[jax.ShapeDtypeStruct((n, columns), below.dtype) for n in (cut * 64, rows - cut * 64)],
        compiler_params=limit,
        cost_estimate=brief,
        name="parts",
    )(below, above)


def join_kernel(after, *refs):
    parts, out = refs[: -1 - after], refs[-1]
    at = 0
    for part in parts:
        out[at : at + part.shape[0]] = part[...]
        at += part.shape[0]


def join(parts, after):
    count = sum(part.shape[0] for part in parts)
    return pl.pallas_call(
        functools.partial(join_kernel, len(after)),
        in_specs=[pl.BlockSpec(memory_space=pltpu.VMEM)] * len(parts) + [unread] * len(after),
        out_shape=jax.ShapeDtypeStruct((count,) + parts[0].shape[1:], f32),
        compiler_params=limit,
        cost_estimate=brief,
        name="join",
    )(*parts, *after)


def settle_kernel(a, b, unread_ref, a_out, b_out, token):
    del a, b, unread_ref, a_out, b_out
    token[...] = jnp.zeros_like(token)


def settle(a, b, after):
    return pl.pallas_call(
        settle_kernel,
        in_specs=[unread] * 3,
        out_specs=[unread] * 2 + [pl.BlockSpec(memory_space=pltpu.VMEM)],
        out_shape=[jax.ShapeDtypeStruct(x.shape, x.dtype) for x in (a, b)] + [jax.ShapeDtypeStruct((8, 128), f32)],
        input_output_aliases={0: 0, 1: 1},
        cost_estimate=brief,
        name="settle",
    )(a, b, after)


def gate_kernel(*refs):
    del refs


def gate(arrays, after):
    count = len(arrays)
    return pl.pallas_call(
        gate_kernel,
        in_specs=[unread] * (count + len(after)),
        out_specs=[unread] * count,
        out_shape=[jax.ShapeDtypeStruct(a.shape, a.dtype) for a in arrays],
        input_output_aliases={i: i for i in range(count)},
        cost_estimate=brief,
        name="gate",
    )(*arrays, *after)


def total(*refs):
    return sum(ref.astype(f32) for ref in refs)


def spot(dy, x, rows, columns, part=0):
    return pl.BlockSpec((1, 1, rows, columns), lambda i: (dy, x, part, 0))


def first_kernel(keep1, got1, keep2, got2, keep3, got3, up, down):
    half = up.shape[1]
    low, high = slice(0, half), slice(half, 2 * half)
    up[0] = total(keep2[0, 0, low], got2[0, 0, low]).astype(bf16)
    down[0] = total(keep2[0, 0, high], got2[0, 0, high]).astype(bf16)
    up[1] = total(keep1[0, 0], got1[0, 0]).astype(bf16)
    down[1] = total(keep3[0, 0], got3[0, 0]).astype(bf16)


def first_messages(keep, got, x, after):
    _, _, rows, columns = keep.shape
    half = rows // 2
    part = pl.BlockSpec((2, half, columns), lambda i: (0, 0, 0))
    shape = jax.ShapeDtypeStruct((2, half, columns), bf16)

    def kernel(*refs):
        first_kernel(*refs[:6], *refs[6 + len(after) :])

    return pl.pallas_call(
        kernel,
        grid=(1,),
        in_specs=[spot(1, x, half, columns, 1)] * 2
        + [spot(2, x, rows, columns)] * 2
        + [spot(3, x, half, columns, 0)] * 2
        + [unread] * len(after),
        out_specs=[part] * 2,
        out_shape=[shape] * 2,
        compiler_params=limit,
        cost_estimate=brief,
        name="first_messages",
    )(keep, got, keep, got, keep, got, *after)


def second_kernel(keep1, got1, keep3, got3, up, down, up_out, down_out):
    up_out[...] = total(keep1[0, 0], got1[0, 0], up[0]).astype(bf16)
    down_out[...] = total(keep3[0, 0], got3[0, 0], down[0]).astype(bf16)


def second_messages(keep, got, up, down, x):
    _, _, rows, columns = keep.shape
    half = rows // 2
    came = pl.BlockSpec((1, half, columns), lambda i: (0, 0, 0))
    part = pl.BlockSpec((half, columns), lambda i: (0, 0))
    shape = jax.ShapeDtypeStruct((half, columns), bf16)
    return pl.pallas_call(
        second_kernel,
        grid=(1,),
        in_specs=[spot(1, x, half, columns, 0)] * 2 + [spot(3, x, half, columns, 1)] * 2 + [came] * 2,
        out_specs=[part] * 2,
        out_shape=[shape] * 2,
        compiler_params=limit,
        cost_estimate=brief,
        name="second_messages",
    )(keep, got, keep, got, up, down)


def chip_kernel(keep, got, up, down, up2, down2, out):
    half = up.shape[1]
    low, high = slice(0, half), slice(half, 2 * half)
    out[low] = total(keep[0, 0, low], got[0, 0, low], down[0], up2[...]).astype(out.dtype)
    out[high] = total(keep[0, 0, high], got[0, 0, high], up[0], down2[...]).astype(out.dtype)


def chip_sum(keep, got, up, down, up2, down2, x, dtype):
    _, _, rows, columns = keep.shape
    came = pl.BlockSpec((1, rows // 2, columns), lambda i: (1, 0, 0))
    part = pl.BlockSpec((rows // 2, columns), lambda i: (0, 0))
    return pl.pallas_call(
        chip_kernel,
        grid=(1,),
        in_specs=[spot(0, x, rows, columns)] * 2 + [came] * 2 + [part] * 2,
        out_specs=pl.BlockSpec((rows, columns), lambda i: (0, 0)),
        out_shape=jax.ShapeDtypeStruct((rows, columns), dtype),
        compiler_params=limit,
        cost_estimate=brief,
        name="chip_sum",
    )(keep, got, up, down, up2, down2)


def per_device(
    latents,
    target,
    timesteps,
    patch_weight,
    head_weight,
    modulation,
    time_weight,
    anchor,
    momentum,
    frag_start,
    frag_current,
):
    frag_current = frag_current[0]
    params = (patch_weight[0], head_weight[0], modulation[0], time_weight[0])
    columns = params[0].shape[1]
    width = float(columns * N_FSDP)
    tokens = float(latents.shape[0] * N_FSDP)
    replica = lax.axis_index("replica")
    pos = jnp.stack([replica % 2, (replica // 2) % 4, replica // 8]).astype(jnp.int32)

    to_core = [(r, r ^ 1) for r in range(16)]
    to_x = [(r, r ^ 8) for r in range(16)]

    def to_y(step):
        return [
            (xh * 8 + y * 2 + c, xh * 8 + ((y + step) % N_Y) * 2 + c)
            for xh in range(N_XH)
            for y in range(N_Y)
            for c in range(N_CORE)
        ]

    send = functools.partial(lax.ppermute, axis_name="replica")
    to_sibling = functools.partial(send, perm=to_core)

    def across(value, bit):
        return lax.ppermute(value, "fsdp", [(i, i ^ bit) for i in range(N_FSDP)])

    h0 = step_head(timesteps, params[0])[None]
    h1 = across(h0, 1)
    keep, sent = quantize(pos, frag_start, frag_current)
    got = to_sibling(sent)
    h01 = join([h0, h1], [keep])
    h2 = across(h01, 2)
    up, down = [None, None], [None, None]

    def ring(x, messages):
        up[x], down[x] = send(messages[0], perm=to_y(1)), send(messages[1], perm=to_y(-1))

    message = first_messages(keep, got, 1, [])
    ring(1, message)
    h03 = join([h01, h2], [message[0]])
    h4 = across(h03, 4)
    near, away, pre, center, sines = weight_products(h03, h4, *params, [message[0]], width)
    away = across(away, 4)
    away2 = across(near[2:4] + away[2:4], 2)
    away1 = across(near[1:2] + away[1:2] + away2[1:2], 1)

    far = second_messages(keep, got, up[1], down[1], 1)
    far_up, far_down = send(far[0], perm=to_y(1)), send(far[1], perm=to_y(-1))
    ring(0, first_messages(keep, got, 0, [far[0]]))
    far = send(chip_sum(keep, got, up[1], down[1], far_up, far_down, 1, bf16), perm=to_x)
    own = second_messages(keep, got, up[0], down[0], 0)
    own_up, own_down = send(own[0], perm=to_y(1)), send(own[1], perm=to_y(-1))
    q0 = token_sums(near[0:1] + away[0:1] + away2[0:1], away1, latents.T, target.T, [anchor, momentum], width, tokens)
    q1 = across(q0, 1)
    own = chip_sum(keep, got, up[0], down[0], own_up, own_down, 0, f32)
    new_anchor, new_momentum, n0 = outer_update(pos, own, far, anchor, momentum, q0)

    n1 = send(n0, perm=to_x)
    up0, down0 = send(n0, perm=to_y(1)), send(n0, perm=to_y(-1))
    q01 = join([q0, q1], [])
    q2 = across(q01, 2)
    q4 = across(join([q01, q2], []), 4)
    first0 = parts(up0, down0, 2)
    on0 = send(first0[0], perm=to_y(1)), send(first0[1], perm=to_y(-1))
    (n1,) = gate([n1], [q01])
    up1, down1 = send(n1, perm=to_y(1)), send(n1, perm=to_y(-1))
    first1 = parts(up1, down1, 3)
    on1 = send(first1[0], perm=to_y(1)), send(first1[1], perm=to_y(-1))
    inner = finish(q0, q1, q2, q4, pre, center, sines, params, [first1[0]])
    anchor_t, momentum_t, settled = settle(new_anchor.T, new_momentum.T, first1[0])
    mine = [n0, up0, down0, n1, up1, down1, *on0]
    mine = gate(mine, [*on1, inner[2], settled])
    mine = [*mine, *on1]
    theirs = [to_sibling(part) for part in mine]
    chips = ((0, 0, 0), (3, 0, 0), (1, 0, 0), (0, 1, 0), (3, 1, 0), (1, 1, 0), (2, 0, 2), (2, 1, 3))
    new_params = place(pos, chips, mine, theirs, [inner[2], settled])
    return tuple(a[None] for a in inner) + (anchor_t.T, momentum_t.T, new_params)


def column(row):
    eye = lax.broadcasted_iota(jnp.int32, (64, 128), 0) == lax.broadcasted_iota(jnp.int32, (64, 128), 1)
    return jnp.sum(jnp.where(eye, row, 0.0), axis=1, keepdims=True)


def gains(pre, mod_ref):
    embed = pre * jax.nn.sigmoid(pre)
    mod = mod_ref[...].astype(bf16).astype(f32)
    return 1.0 + mod[1:2] + embed, mod[0:1] + embed


def weights_kernel(width, after, near_heads, away_heads, patch_ref, head_ref, mod_ref, time_ref, *refs):
    near, away, pre_ref, center_ref, sines_ref, high, low = refs[after:]
    count = N_FSDP
    total = jnp.zeros((1, 128), f32)
    for k in range(count):
        head = (near_heads if k < count // 2 else away_heads)[k % (count // 2)]
        total = total + head[8:9]
        sines_ref[4 * k : 4 * k + 4, 0:128] = head[0:4]
        sines_ref[4 * k : 4 * k + 4, 128:256] = head[4:8]
    pre = dot(sines_ref[...].astype(bf16), time_ref[...].astype(bf16), NN)
    pre_ref[...] = pre
    gain, shift = gains(pre, mod_ref)
    center = patch_ref[...].astype(bf16).astype(f32) - column(total / width)
    center_ref[...] = center
    samples = 4 * count
    for s in range(samples):
        k, i = s // 4, s % 4
        at = (i // 2) * (samples // 2 * 64) + (2 * k + i % 2) * 64
        hi, lo = split2(center * gain[s : s + 1])
        high[at : at + 64, :] = hi
        low[at : at + 64, :] = lo
    head = head_ref[...].astype(bf16)
    blank = jnp.zeros_like(head)
    left = jnp.concatenate([head, blank], axis=0)
    right = jnp.concatenate([blank, head], axis=0)
    part = samples // 2 * 64
    packed = dot(high[0:part], left, NT) + dot(low[0:part], left, NT)
    packed = packed + dot(high[part:], right, NT) + dot(low[part:], right, NT)
    chi, clo = split2(center)
    chi_left = jnp.concatenate([chi, blank], axis=0)
    clo_left = jnp.concatenate([clo, blank], axis=0)
    gram = dot(chi, chi_left, NT) + dot(clo, chi_left, NT) + dot(chi, clo_left, NT)
    for k in range(count):
        out = near if k < count // 2 else away
        slot = k % (count // 2)
        rows = jnp.concatenate([shift[4 * k : 4 * k + 4], gain[4 * k : 4 * k + 4]], axis=0)
        hi, lo = split2(rows)
        extra = dot(hi, right, NT) + dot(lo, right, NT)
        out[slot, 0:128, :] = packed[128 * k : 128 * k + 128]
        out[slot, 128:136, :] = gram[0:8] + extra
        out[slot, 136:192, :] = gram[8:64]


def row(column):
    eye = lax.broadcasted_iota(jnp.int32, (64, 128), 0) == lax.broadcasted_iota(jnp.int32, (64, 128), 1)
    return jnp.sum(jnp.where(eye, column, 0.0), axis=0, keepdims=True)


def tokens_kernel(width, tokens, after, own_ref, away_ref, latent_ref, target_ref, *refs):
    out, wide = refs[after:]
    total = own_ref[0] + away_ref[0]
    turned = pltpu.roll(total, 64, 1)
    gram = total[128:192, 0:64] / width
    g0 = gram.astype(bf16)
    g1, g2 = split2(gram - g0.astype(f32))
    gain_means = turned[132:136, :] / width
    wide[...] = jnp.zeros_like(wide)
    curve = jnp.zeros((64, 64), f32)
    sums = []
    for s in range(4):
        at = slice(s * SAMPLE_TOKENS, (s + 1) * SAMPLE_TOKENS)
        latent = latent_ref[:, at]
        latent_f = latent.astype(f32)
        mix = (total if s < 2 else turned)[(s % 2) * 64 : (s % 2) * 64 + 64, 0:64]
        mix_hi, mix_lo = split2(mix)
        spread = dot(g0, latent, NN) + dot(g1, latent, NN) + dot(g2, latent, NN)
        variance = jnp.sum(spread * latent_f, axis=0, keepdims=True)
        inv_std = lax.rsqrt(jnp.maximum(variance, 0.0) + epsilon)
        varied = inv_std * (dot(mix_hi, latent, TN) + dot(mix_lo, latent, TN))
        output = varied + column(turned[128 + s : 129 + s, :])
        grad_out = (2.0 * (output - target_ref[:, at].astype(f32)) / tokens).astype(bf16)
        grad_f = grad_out.astype(f32)
        along = jnp.sum(grad_f * varied, axis=0, keepdims=True) / width
        cross = dot((grad_f * inv_std).astype(bf16), latent, NT)
        curve = curve + dot((latent_f * (along * inv_std * inv_std)).astype(bf16), latent, NT)
        sums.append(row(jnp.sum(grad_f, axis=1, keepdims=True)))
        if s < 2:
            out[0, s * 64 : s * 64 + 64, 0:64] = cross
        else:
            wide[(s - 2) * 64 : (s - 2) * 64 + 64, 0:64] = cross
    for s in range(4):
        wide[128 + s : 129 + s, :] = sums[s]
    wide[132:136, 0:64] = gain_means[:, 0:64]
    packed = pltpu.roll(wide[...], 64, 1)
    low_lane = lax.broadcasted_iota(jnp.int32, (128, 128), 1) < 64
    out[0, 0:128, :] = jnp.where(low_lane, out[0, 0:128, :], packed[0:128])
    wide[128:192, 0:64] = curve
    out[0, 128:192, :] = jnp.where(low_lane[0:64], wide[128:192, :], packed[128:192])


def finish_kernel(
    after,
    parts0,
    parts1,
    parts2,
    parts4,
    pre_ref,
    center_ref,
    sines_ref,
    patch_ref,
    head_ref,
    mod_ref,
    time_ref,
    *refs,
):
    patch_new, head_new, mod_new, time_new, sums, slope_rows = refs[after:]
    count = N_FSDP
    parts = [ref[i] for ref in (parts0, parts1, parts2, parts4) for i in range(ref.shape[0])]
    pre = pre_ref[...]
    gain, shift = gains(pre, mod_ref)
    head = head_ref[...].astype(bf16)
    head_f = head.astype(f32)
    center = center_ref[...]
    chi, clo = split2(center)
    curve = parts[0][128:192, 0:64]
    for k in range(1, count):
        curve = curve + parts[k][128:192, 0:64]
    curve_hi, curve_lo = split2(curve)
    grad_patch = -(dot(curve_hi, chi, NN) + dot(curve_lo, chi, NN) + dot(curve_hi, clo, NN))
    grad_head = jnp.zeros_like(center)
    grad_scale = jnp.zeros_like(gain[0:1])
    for k in range(count):
        plain = parts[k]
        turned = pltpu.roll(plain, 64, 1)
        sums[4 * k : 4 * k + 4, :] = turned[128:132]
        crosses, fine = split2(jnp.concatenate([plain[0:128, 0:64], turned[0:128, 0:64]], axis=0))
        mixed = dot(crosses, chi, NN) + dot(fine, chi, NN) + dot(crosses, clo, NN)
        pulls = []
        for i in range(4):
            s = 4 * k + i
            one = mixed[i * 64 : i * 64 + 64]
            grad_head = grad_head + one * gain[s : s + 1]
            slope = jnp.sum(head_f * one, axis=0, keepdims=True)
            slope_rows[s : s + 1, :] = slope
            grad_scale = grad_scale + slope
            pulls.append((head_f * gain[s : s + 1] - column(turned[132 + i : 133 + i])).astype(bf16))
        grad_patch = grad_patch + dot(crosses, jnp.concatenate(pulls, axis=0), TN)
    sum_hi, sum_lo = split2(sums[:, 0:64])
    shift_hi, shift_lo = split2(shift)
    grad_head = grad_head + dot(sum_hi, shift_hi, TN) + dot(sum_lo, shift_hi, TN) + dot(sum_hi, shift_lo, TN)
    mixed_sums = dot(sum_hi, head, NN) + dot(sum_lo, head, NN)
    grad_shift = jnp.sum(mixed_sums, axis=0, keepdims=True)
    grad_embed = mixed_sums + slope_rows[...]
    sigmoid = jax.nn.sigmoid(pre)
    grad_pre = (grad_embed * (sigmoid * (1.0 + pre * (1.0 - sigmoid)))).astype(bf16)
    grad_time = dot(sines_ref[...].astype(bf16), grad_pre, TN)
    patch_new[...] = patch_ref[...] - inner_rate * grad_patch
    head_new[...] = head_ref[...] - inner_rate * grad_head
    mod_new[0:1, :] = mod_ref[0:1, :] - inner_rate * grad_shift
    mod_new[1:2, :] = mod_ref[1:2, :] - inner_rate * grad_scale
    time_new[...] = time_ref[...] - inner_rate * grad_time


def sinusoid(time_steps):
    index = jnp.arange(FREQ_DIM // 2, dtype=f32)
    frequency = jnp.exp(-math.log(10000.0) * index / (FREQ_DIM // 2))
    angles = time_steps.astype(f32)[:, None] * frequency[None, :]
    return jnp.cos(angles), jnp.sin(angles)


def step_head(timesteps, patch):
    cos, sin = sinusoid(timesteps)
    row_sums = jnp.sum(patch.astype(bf16).astype(f32), axis=1)
    return jnp.concatenate(
        [cos, sin, jnp.pad(row_sums, (0, 128 - PATCH_DIM))[None], jnp.zeros((7, 128), f32)], axis=0
    )


def weight_products(near, away, patch, head, mod, time, after, width):
    columns = patch.shape[1]
    samples = 4 * N_FSDP
    share = jax.ShapeDtypeStruct((N_FSDP // 2, 192, 128), f32)
    return pl.pallas_call(
        functools.partial(weights_kernel, width, len(after)),
        in_specs=[pl.BlockSpec(memory_space=pltpu.VMEM)] * 6 + [unread] * len(after),
        out_shape=[
            share,
            share,
            jax.ShapeDtypeStruct((samples, columns), f32),
            jax.ShapeDtypeStruct((PATCH_DIM, columns), f32),
            jax.ShapeDtypeStruct((samples, FREQ_DIM), f32),
        ],
        scratch_shapes=[pltpu.VMEM((samples * PATCH_DIM, columns), bf16)] * 2,
        compiler_params=limit,
        cost_estimate=brief,
        name="weight_products",
    )(near, away, patch, head, mod, time, *after)


def token_sums(own, away, latents, target, after, width, tokens):
    return pl.pallas_call(
        functools.partial(tokens_kernel, width, tokens, len(after)),
        in_specs=[pl.BlockSpec(memory_space=pltpu.VMEM)] * 4 + [unread] * len(after),
        out_shape=jax.ShapeDtypeStruct((1, 192, 128), f32),
        scratch_shapes=[pltpu.VMEM((192, 128), f32)],
        compiler_params=limit,
        cost_estimate=brief,
        name="token_sums",
    )(own, away, latents, target, *after)


def finish(q0, q1, q2, q4, pre, center, sines, params, after):
    samples, columns = pre.shape
    return pl.pallas_call(
        functools.partial(finish_kernel, len(after)),
        in_specs=[pl.BlockSpec(memory_space=pltpu.VMEM)] * 11 + [unread] * len(after),
        out_shape=[jax.ShapeDtypeStruct(a.shape, f32) for a in params],
        scratch_shapes=[pltpu.VMEM((samples, 128), f32), pltpu.VMEM((samples, columns), f32)],
        compiler_params=limit,
        cost_estimate=brief,
        name="finish",
    )(q0, q1, q2, q4, pre, center, sines, *params, *after)


def solution(mesh):
    in_specs = (
        P(("replica", "fsdp"), None),
        P(("replica", "fsdp"), None),
        P(("replica", "fsdp")),
        P("replica", None, "fsdp"),
        P("replica", None, "fsdp"),
        P("replica", None, "fsdp"),
        P("replica", None, "fsdp"),
        P("fsdp", "replica"),
        P("fsdp", "replica"),
        P("fsdp", None),
        P("replica", "fsdp", None),
    )
    out_specs = (
        P("replica", None, "fsdp"),
        P("replica", None, "fsdp"),
        P("replica", None, "fsdp"),
        P("replica", None, "fsdp"),
        P("fsdp", "replica"),
        P("fsdp", "replica"),
        P("fsdp", None),
    )
    return jax.shard_map(
        per_device, mesh=mesh, in_specs=in_specs, out_specs=out_specs, check_vma=False
    )
```

```python
import functools
import math

import jax
import jax.numpy as jnp
from jax import lax
from jax.experimental import pallas as pl
from jax.experimental.pallas import tpu as pltpu
from jax.sharding import PartitionSpec as P

FREQ_DIM = 256
PATCH_DIM = 64
QBLOCK = 128
SAMPLE_TOKENS = 512

epsilon = 1e-06
inner_rate = 0.5
outer_rate = 0.7
momentum_decay = 0.9

f32 = jnp.float32
bf16 = jnp.bfloat16

N_Y, N_XH, N_CORE, N_FSDP = 4, 2, 2, 8
COL = 320
PAIR = 640
ROWS = 640
ROUND = 1.5 * 2.0**23
NUDGE = 1.0 + 2.0**-21

limit = pltpu.CompilerParams(vmem_limit_bytes=56 * 2**20)
brief = pl.CostEstimate(flops=1, bytes_accessed=1, transcendentals=0)
unread = pl.BlockSpec(memory_space=pl.ANY)

NT = (((1,), (1,)), ((), ()))
TN = (((0,), (0,)), ((), ()))
NN = (((1,), (0,)), ((), ()))


def dot(a, b, dims):
    return lax.dot_general(a, b, dims, preferred_element_type=f32)


def split2(x):
    hi = x.astype(bf16)
    return hi, (x - hi.astype(f32)).astype(bf16)


def quantized(delta):
    peak = jnp.max(jnp.abs(delta), axis=0, keepdims=True)
    scale = (peak + epsilon).astype(bf16).astype(f32)
    ratio = (7.0 / scale) * NUDGE
    shifted = delta * ratio + ROUND
    code = jnp.clip(shifted, ROUND - 7.0, ROUND + 7.0) - ROUND
    return code * (scale / 7.0)


def quant_kernel(pos_ref, start_ref, current_ref, keep, send):
    first_core = pos_ref[0] == 0
    low_lane = lax.broadcasted_iota(jnp.int32, (64, 128), 1) < 64
    for chip in range(N_Y * N_XH):
        dy = lax.rem(chip % N_Y - pos_ref[1] + N_Y, N_Y)
        dx = lax.rem(chip // N_Y - pos_ref[2] + N_XH, N_XH)
        slot = dy * N_XH + dx

        def terms(tile):
            lanes = slice(chip * PAIR + tile * 128, chip * PAIR + (tile + 1) * 128)
            return quantized(start_ref[:, lanes].astype(f32) - current_ref[:, lanes].astype(f32))

        def put(lane, low, high):
            keep[slot, :, lane : lane + 128] = jnp.where(first_core, low, high).astype(bf16)
            send[slot, :, lane : lane + 128] = jnp.where(first_core, high, low).astype(bf16)

        for tile in range(2):
            low, high = terms(tile), terms(tile + 3)
            put(tile * 128, low[:64], high[:64])
            put(256 + tile * 128, low[64:], high[64:])
        both = terms(2)
        top, bottom = both[:64], both[64:]
        low = jnp.where(low_lane, top, pltpu.roll(bottom, 64, 1))
        high = jnp.where(low_lane, pltpu.roll(top, 64, 1), bottom)
        put(512, low, high)


def quantize(pos, frag_start, frag_current):
    chips = N_Y * N_XH
    whole = pl.BlockSpec((QBLOCK, frag_start.shape[1]), lambda i, pos: (i, 0))
    made = pl.BlockSpec((chips, QBLOCK // 2, PAIR), lambda i, pos: (0, i, 0))
    keep, sent = pl.pallas_call(
        quant_kernel,
        grid_spec=pltpu.PrefetchScalarGridSpec(
            num_scalar_prefetch=1,
            grid=(ROWS // QBLOCK,),
            in_specs=[whole, whole],
            out_specs=[made, made],
        ),
        out_shape=[jax.ShapeDtypeStruct((chips, ROWS // 2, PAIR), bf16)] * 2,
        compiler_params=limit,
        cost_estimate=brief,
        name="quantize",
    )(pos, frag_start, frag_current)
    return keep.reshape(N_Y, N_XH, ROWS // 2, PAIR), sent.reshape(N_Y, N_XH, ROWS // 2, PAIR)


def outer_kernel(pos_ref, own_ref, far_ref, anchor_ref, momentum_ref, unread_ref, new_anchor, new_momentum, params, native, fresh):
    low_lane = lax.broadcasted_iota(jnp.int32, (64, 128), 1) < 64
    first_core = pos_ref[0] == 0
    for block in range(ROWS // QBLOCK):
        message = slice(block * 64, block * 64 + 64)
        total = own_ref[message].astype(f32) + far_ref[message].astype(f32)
        rest = total[:, 512:640]
        for half, tail in ((0, rest), (1, pltpu.roll(rest, 64, 1))):
            rows = slice(block * 128 + half * 64, block * 128 + half * 64 + 64)
            main0 = total[:, half * 256 : half * 256 + 128]
            main1 = total[:, half * 256 + 128 : half * 256 + 256]
            turn0, turn1 = pltpu.roll(main0, 64, 1), pltpu.roll(main1, 64, 1)
            native[rows, 0:128] = jnp.where(first_core, main0, jnp.where(low_lane, tail, turn0))
            native[rows, 128:256] = jnp.where(first_core, main1, jnp.where(low_lane, turn0, turn1))
            native[rows, 256:384] = jnp.where(first_core, tail, turn1)
        rows = slice(block * 128, block * 128 + 128)
        average = native[rows, 0:COL] / float(N_Y * N_XH * N_CORE)
        momentum = momentum_decay * momentum_ref[rows] + average
        anchor = anchor_ref[rows] - outer_rate * (average + momentum_decay * momentum)
        new_momentum[rows] = momentum
        new_anchor[rows] = anchor
        fresh[rows, 0:COL] = anchor
        for half in range(2):
            rows = slice(block * 128 + half * 64, block * 128 + half * 64 + 64)
            tiles = [fresh[rows, t * 128 : t * 128 + 128] for t in range(3)]
            turn = [pltpu.roll(tile, 64, 1) for tile in tiles]
            for t in range(2):
                value = jnp.where(first_core, tiles[t], jnp.where(low_lane, turn[t], turn[t + 1]))
                at = half * 256 + t * 128
                params[message, at : at + 128] = value.astype(bf16)
            if half == 0:
                top = jnp.where(first_core, tiles[2], tiles[0])
            else:
                bottom = jnp.where(first_core, turn[2], turn[0])
        params[message, 512:640] = jnp.where(low_lane, top, bottom).astype(bf16)


def outer_update(pos, own, far, anchor, momentum, after):
    held = pl.BlockSpec(memory_space=pltpu.VMEM)
    return pl.pallas_call(
        outer_kernel,
        in_specs=[pl.BlockSpec(memory_space=pltpu.SMEM)] + [held] * 4 + [unread],
        out_specs=[held] * 3,
        scratch_shapes=[pltpu.VMEM((ROWS, 384), f32), pltpu.VMEM((ROWS, 384), f32)],
        out_shape=[
            jax.ShapeDtypeStruct((ROWS, COL), f32),
            jax.ShapeDtypeStruct((ROWS, COL), f32),
            jax.ShapeDtypeStruct((ROWS // 2, PAIR), bf16),
        ],
        compiler_params=limit,
        cost_estimate=brief,
        name="outer_update",
    )(pos, own, far, anchor, momentum, after)


def place_kernel(chips, pos_ref, *refs):
    out = refs[-1]
    count = sum(2 if cut else 1 for _, _, cut in chips)
    mine, theirs = refs[:count], refs[count : 2 * count]
    first_core = pos_ref[0] == 0
    low_lane = lax.broadcasted_iota(jnp.int32, (64, 128), 1) < 64
    index = 0
    for dy, dx, cut in chips:
        a, b = mine[index][...], theirs[index][...]
        index += 1
        if cut:
            early = pl.program_id(0) < cut
            a = jnp.where(early, a, mine[index][...])
            b = jnp.where(early, b, theirs[index][...])
            index += 1
        low, high = jnp.where(first_core, a, b), jnp.where(first_core, b, a)
        chip = lax.rem(pos_ref[2] + dx, N_XH) * N_Y + lax.rem(pos_ref[1] + dy, N_Y)

        def put(half, lane, value):
            lanes = pl.ds(pl.multiple_of(chip * PAIR + lane, 128), value.shape[1])
            out[half * 64 : half * 64 + 64, lanes] = value

        for half in range(2):
            put(half, 0, low[:, half * 256 : half * 256 + 256])
            put(half, 384, high[:, half * 256 : half * 256 + 256])
        low_rest, high_rest = low[:, 512:640].astype(f32), high[:, 512:640].astype(f32)
        put(0, 256, jnp.where(low_lane, low_rest, pltpu.roll(high_rest, 64, 1)).astype(bf16))
        put(1, 256, jnp.where(low_lane, pltpu.roll(low_rest, 64, 1), high_rest).astype(bf16))


def place(pos, chips, mine, theirs, after):
    def blocks(cut):
        if not cut:
            return [pl.BlockSpec((64, PAIR), lambda i, pos: (i, 0))]
        return [
            pl.BlockSpec((64, PAIR), lambda i, pos: (jnp.minimum(i, cut - 1), 0)),
            pl.BlockSpec((64, PAIR), lambda i, pos: (jnp.maximum(i - cut, 0), 0)),
        ]

    specs = [spec for _, _, cut in chips for spec in blocks(cut)]
    return pl.pallas_call(
        functools.partial(place_kernel, chips),
        grid_spec=pltpu.PrefetchScalarGridSpec(
            num_scalar_prefetch=1,
            grid=(ROWS // QBLOCK,),
            in_specs=specs * 2 + [unread] * len(after),
            out_specs=pl.BlockSpec((QBLOCK, N_Y * N_XH * PAIR), lambda i, pos: (i, 0)),
        ),
        out_shape=jax.ShapeDtypeStruct((ROWS, N_Y * N_XH * PAIR), bf16),
        compiler_params=limit,
        cost_estimate=brief,
        name="place",
    )(pos, *mine, *theirs, *after)


def parts_kernel(below, above, first, second):
    cut = first.shape[0]
    first[...] = below[0:cut]
    second[...] = above[cut:]


def parts(below, above, cut):
    rows, columns = below.shape
    return pl.pallas_call(
        parts_kernel,
        out_shape=[jax.ShapeDtypeStruct((n, columns), below.dtype) for n in (cut * 64, rows - cut * 64)],
        compiler_params=limit,
        cost_estimate=brief,
        name="parts",
    )(below, above)


def join_kernel(after, *refs):
    parts, out = refs[: -1 - after], refs[-1]
    at = 0
    for part in parts:
        out[at : at + part.shape[0]] = part[...]
        at += part.shape[0]


def join(parts, after):
    count = sum(part.shape[0] for part in parts)
    return pl.pallas_call(
        functools.partial(join_kernel, len(after)),
        in_specs=[pl.BlockSpec(memory_space=pltpu.VMEM)] * len(parts) + [unread] * len(after),
        out_shape=jax.ShapeDtypeStruct((count,) + parts[0].shape[1:], f32),
        compiler_params=limit,
        cost_estimate=brief,
        name="join",
    )(*parts, *after)


def settle_kernel(a, b, unread_ref, a_out, b_out, token):
    del a, b, unread_ref, a_out, b_out
    token[...] = jnp.zeros_like(token)


def settle(a, b, after):
    return pl.pallas_call(
        settle_kernel,
        in_specs=[unread] * 3,
        out_specs=[unread] * 2 + [pl.BlockSpec(memory_space=pltpu.VMEM)],
        out_shape=[jax.ShapeDtypeStruct(x.shape, x.dtype) for x in (a, b)] + [jax.ShapeDtypeStruct((8, 128), f32)],
        input_output_aliases={0: 0, 1: 1},
        cost_estimate=brief,
        name="settle",
    )(a, b, after)


def gate_kernel(*refs):
    del refs


def gate(arrays, after):
    count = len(arrays)
    return pl.pallas_call(
        gate_kernel,
        in_specs=[unread] * (count + len(after)),
        out_specs=[unread] * count,
        out_shape=[jax.ShapeDtypeStruct(a.shape, a.dtype) for a in arrays],
        input_output_aliases={i: i for i in range(count)},
        cost_estimate=brief,
        name="gate",
    )(*arrays, *after)


def total(*refs):
    return sum(ref.astype(f32) for ref in refs)


def spot(dy, x, rows, columns, part=0):
    return pl.BlockSpec((1, 1, rows, columns), lambda i: (dy, x, part, 0))


def first_kernel(keep1, got1, keep2, got2, keep3, got3, up, down):
    half = up.shape[1]
    low, high = slice(0, half), slice(half, 2 * half)
    up[0] = total(keep2[0, 0, low], got2[0, 0, low]).astype(bf16)
    down[0] = total(keep2[0, 0, high], got2[0, 0, high]).astype(bf16)
    up[1] = total(keep1[0, 0], got1[0, 0]).astype(bf16)
    down[1] = total(keep3[0, 0], got3[0, 0]).astype(bf16)


def first_messages(keep, got, x, after):
    _, _, rows, columns = keep.shape
    half = rows // 2
    part = pl.BlockSpec((2, half, columns), lambda i: (0, 0, 0))
    shape = jax.ShapeDtypeStruct((2, half, columns), bf16)

    def kernel(*refs):
        first_kernel(*refs[:6], *refs[6 + len(after) :])

    return pl.pallas_call(
        kernel,
        grid=(1,),
        in_specs=[spot(1, x, half, columns, 1)] * 2
        + [spot(2, x, rows, columns)] * 2
        + [spot(3, x, half, columns, 0)] * 2
        + [unread] * len(after),
        out_specs=[part] * 2,
        out_shape=[shape] * 2,
        compiler_params=limit,
        cost_estimate=brief,
        name="first_messages",
    )(keep, got, keep, got, keep, got, *after)


def second_kernel(keep1, got1, keep3, got3, up, down, *refs):
    up_out, down_out = refs[-2:]
    up_out[...] = total(keep1[0, 0], got1[0, 0], up[0]).astype(bf16)
    down_out[...] = total(keep3[0, 0], got3[0, 0], down[0]).astype(bf16)


def second_messages(keep, got, up, down, x, after):
    _, _, rows, columns = keep.shape
    half = rows // 2
    came = pl.BlockSpec((1, half, columns), lambda i: (0, 0, 0))
    part = pl.BlockSpec((half, columns), lambda i: (0, 0))
    shape = jax.ShapeDtypeStruct((half, columns), bf16)
    return pl.pallas_call(
        second_kernel,
        grid=(1,),
        in_specs=[spot(1, x, half, columns, 0)] * 2 + [spot(3, x, half, columns, 1)] * 2 + [came] * 2 + [unread] * len(after),
        out_specs=[part] * 2,
        out_shape=[shape] * 2,
        compiler_params=limit,
        cost_estimate=brief,
        name="second_messages",
    )(keep, got, keep, got, up, down, *after)


def chip_kernel(keep, got, up, down, up2, down2, out):
    half = up.shape[1]
    low, high = slice(0, half), slice(half, 2 * half)
    out[low] = total(keep[0, 0, low], got[0, 0, low], down[0], up2[...]).astype(out.dtype)
    out[high] = total(keep[0, 0, high], got[0, 0, high], up[0], down2[...]).astype(out.dtype)


def chip_sum(keep, got, up, down, up2, down2, x, dtype):
    _, _, rows, columns = keep.shape
    came = pl.BlockSpec((1, rows // 2, columns), lambda i: (1, 0, 0))
    part = pl.BlockSpec((rows // 2, columns), lambda i: (0, 0))
    return pl.pallas_call(
        chip_kernel,
        grid=(1,),
        in_specs=[spot(0, x, rows, columns)] * 2 + [came] * 2 + [part] * 2,
        out_specs=pl.BlockSpec((rows, columns), lambda i: (0, 0)),
        out_shape=jax.ShapeDtypeStruct((rows, columns), dtype),
        compiler_params=limit,
        cost_estimate=brief,
        name="chip_sum",
    )(keep, got, up, down, up2, down2)


def per_device(
    latents,
    target,
    timesteps,
    patch_weight,
    head_weight,
    modulation,
    time_weight,
    anchor,
    momentum,
    frag_start,
    frag_current,
):
    frag_current = frag_current[0]
    params = (patch_weight[0], head_weight[0], modulation[0], time_weight[0])
    columns = params[0].shape[1]
    width = float(columns * N_FSDP)
    tokens = float(latents.shape[0] * N_FSDP)
    replica = lax.axis_index("replica")
    pos = jnp.stack([replica % 2, (replica // 2) % 4, replica // 8]).astype(jnp.int32)

    to_core = [(r, r ^ 1) for r in range(16)]
    to_x = [(r, r ^ 8) for r in range(16)]

    def to_y(step):
        return [
            (xh * 8 + y * 2 + c, xh * 8 + ((y + step) % N_Y) * 2 + c)
            for xh in range(N_XH)
            for y in range(N_Y)
            for c in range(N_CORE)
        ]

    send = functools.partial(lax.ppermute, axis_name="replica")
    to_sibling = functools.partial(send, perm=to_core)

    def across(value, bit):
        return lax.ppermute(value, "fsdp", [(i, i ^ bit) for i in range(N_FSDP)])

    h0 = step_head(timesteps, params[0])[None]
    h1 = across(h0, 1)
    keep, sent = quantize(pos, frag_start, frag_current)
    got = to_sibling(sent)
    h01 = join([h0, h1], [keep])
    h2 = across(h01, 2)
    up, down = [None, None], [None, None]

    def ring(x, messages):
        up[x], down[x] = send(messages[0], perm=to_y(1)), send(messages[1], perm=to_y(-1))

    message = first_messages(keep, got, 1, [])
    ring(1, message)
    h03 = join([h01, h2], [message[0]])
    h4 = across(h03, 4)
    near, away, pre, center, sines = weight_products(h03, h4, *params, [message[0]], width)
    away = across(away, 4)
    away2 = across(near[2:4] + away[2:4], 2)
    away1 = across(near[1:2] + away[1:2] + away2[1:2], 1)

    far = second_messages(keep, got, up[1], down[1], 1, [])
    far_up, far_down = send(far[0], perm=to_y(1)), send(far[1], perm=to_y(-1))
    ring(0, first_messages(keep, got, 0, [far[0]]))
    far = send(chip_sum(keep, got, up[1], down[1], far_up, far_down, 1, bf16), perm=to_x)
    own = second_messages(keep, got, up[0], down[0], 0, [anchor, momentum])
    own_up, own_down = send(own[0], perm=to_y(1)), send(own[1], perm=to_y(-1))
    q0 = token_sums(near[0:1] + away[0:1] + away2[0:1], away1, latents.T, target.T, [], width, tokens)
    q1 = across(q0, 1)
    own = chip_sum(keep, got, up[0], down[0], own_up, own_down, 0, f32)
    new_anchor, new_momentum, n0 = outer_update(pos, own, far, anchor, momentum, q0)

    n1 = send(n0, perm=to_x)
    up0, down0 = send(n0, perm=to_y(1)), send(n0, perm=to_y(-1))
    q01 = join([q0, q1], [])
    q2 = across(q01, 2)
    anchor_t, momentum_t, settled = settle(new_anchor.T, new_momentum.T, q01)
    q4 = across(join([q01, q2], [settled]), 4)
    first0 = parts(up0, down0, 2)
    on0 = send(first0[0], perm=to_y(1)), send(first0[1], perm=to_y(-1))
    (n1,) = gate([n1], [q01])
    up1, down1 = send(n1, perm=to_y(1)), send(n1, perm=to_y(-1))
    first1 = parts(up1, down1, 3)
    on1 = send(first1[0], perm=to_y(1)), send(first1[1], perm=to_y(-1))
    inner = finish(q0, q1, q2, q4, pre, center, sines, params, [first1[0]])
    mine = [n0, up0, down0, n1, up1, down1, *on0]
    mine = gate(mine, [*on1, inner[2], settled])
    mine = [*mine, *on1]
    theirs = [to_sibling(part) for part in mine]
    chips = ((0, 0, 0), (3, 0, 0), (1, 0, 0), (0, 1, 0), (3, 1, 0), (1, 1, 0), (2, 0, 2), (2, 1, 3))
    new_params = place(pos, chips, mine, theirs, [inner[2], settled])
    return tuple(a[None] for a in inner) + (anchor_t.T, momentum_t.T, new_params)


def column(row):
    eye = lax.broadcasted_iota(jnp.int32, (64, 128), 0) == lax.broadcasted_iota(jnp.int32, (64, 128), 1)
    return jnp.sum(jnp.where(eye, row, 0.0), axis=1, keepdims=True)


def gains(pre, mod_ref):
    embed = pre * jax.nn.sigmoid(pre)
    mod = mod_ref[...].astype(bf16).astype(f32)
    return 1.0 + mod[1:2] + embed, mod[0:1] + embed


def weights_kernel(width, after, near_heads, away_heads, patch_ref, head_ref, mod_ref, time_ref, *refs):
    near, away, pre_ref, center_ref, sines_ref, high, low = refs[after:]
    count = N_FSDP
    total = jnp.zeros((1, 128), f32)
    for k in range(count):
        head = (near_heads if k < count // 2 else away_heads)[k % (count // 2)]
        total = total + head[8:9]
        sines_ref[4 * k : 4 * k + 4, 0:128] = head[0:4]
        sines_ref[4 * k : 4 * k + 4, 128:256] = head[4:8]
    pre = dot(sines_ref[...].astype(bf16), time_ref[...].astype(bf16), NN)
    pre_ref[...] = pre
    gain, shift = gains(pre, mod_ref)
    center = patch_ref[...].astype(bf16).astype(f32) - column(total / width)
    center_ref[...] = center
    samples = 4 * count
    for s in range(samples):
        k, i = s // 4, s % 4
        at = (i // 2) * (samples // 2 * 64) + (2 * k + i % 2) * 64
        hi, lo = split2(center * gain[s : s + 1])
        high[at : at + 64, :] = hi
        low[at : at + 64, :] = lo
    head = head_ref[...].astype(bf16)
    blank = jnp.zeros_like(head)
    left = jnp.concatenate([head, blank], axis=0)
    right = jnp.concatenate([blank, head], axis=0)
    part = samples // 2 * 64
    packed = dot(high[0:part], left, NT) + dot(low[0:part], left, NT)
    packed = packed + dot(high[part:], right, NT) + dot(low[part:], right, NT)
    chi, clo = split2(center)
    chi_left = jnp.concatenate([chi, blank], axis=0)
    clo_left = jnp.concatenate([clo, blank], axis=0)
    gram = dot(chi, chi_left, NT) + dot(clo, chi_left, NT) + dot(chi, clo_left, NT)
    for k in range(count):
        out = near if k < count // 2 else away
        slot = k % (count // 2)
        rows = jnp.concatenate([shift[4 * k : 4 * k + 4], gain[4 * k : 4 * k + 4]], axis=0)
        hi, lo = split2(rows)
        extra = dot(hi, right, NT) + dot(lo, right, NT)
        out[slot, 0:128, :] = packed[128 * k : 128 * k + 128]
        out[slot, 128:136, :] = gram[0:8] + extra
        out[slot, 136:192, :] = gram[8:64]


def row(column):
    eye = lax.broadcasted_iota(jnp.int32, (64, 128), 0) == lax.broadcasted_iota(jnp.int32, (64, 128), 1)
    return jnp.sum(jnp.where(eye, column, 0.0), axis=0, keepdims=True)


def tokens_kernel(width, tokens, after, own_ref, away_ref, latent_ref, target_ref, *refs):
    out, wide = refs[after:]
    total = own_ref[0] + away_ref[0]
    turned = pltpu.roll(total, 64, 1)
    gram = total[128:192, 0:64] / width
    g0 = gram.astype(bf16)
    g1, g2 = split2(gram - g0.astype(f32))
    gain_means = turned[132:136, :] / width
    wide[...] = jnp.zeros_like(wide)
    curve = jnp.zeros((64, 64), f32)
    sums = []
    for s in range(4):
        at = slice(s * SAMPLE_TOKENS, (s + 1) * SAMPLE_TOKENS)
        latent = latent_ref[:, at]
        latent_f = latent.astype(f32)
        mix = (total if s < 2 else turned)[(s % 2) * 64 : (s % 2) * 64 + 64, 0:64]
        mix_hi, mix_lo = split2(mix)
        spread = dot(g0, latent, NN) + dot(g1, latent, NN) + dot(g2, latent, NN)
        variance = jnp.sum(spread * latent_f, axis=0, keepdims=True)
        inv_std = lax.rsqrt(jnp.maximum(variance, 0.0) + epsilon)
        varied = inv_std * (dot(mix_hi, latent, TN) + dot(mix_lo, latent, TN))
        output = varied + column(turned[128 + s : 129 + s, :])
        grad_out = (2.0 * (output - target_ref[:, at].astype(f32)) / tokens).astype(bf16)
        grad_f = grad_out.astype(f32)
        along = jnp.sum(grad_f * varied, axis=0, keepdims=True) / width
        cross = dot((grad_f * inv_std).astype(bf16), latent, NT)
        curve = curve + dot((latent_f * (along * inv_std * inv_std)).astype(bf16), latent, NT)
        sums.append(row(jnp.sum(grad_f, axis=1, keepdims=True)))
        if s < 2:
            out[0, s * 64 : s * 64 + 64, 0:64] = cross
        else:
            wide[(s - 2) * 64 : (s - 2) * 64 + 64, 0:64] = cross
    for s in range(4):
        wide[128 + s : 129 + s, :] = sums[s]
    wide[132:136, 0:64] = gain_means[:, 0:64]
    packed = pltpu.roll(wide[...], 64, 1)
    low_lane = lax.broadcasted_iota(jnp.int32, (128, 128), 1) < 64
    out[0, 0:128, :] = jnp.where(low_lane, out[0, 0:128, :], packed[0:128])
    wide[128:192, 0:64] = curve
    out[0, 128:192, :] = jnp.where(low_lane[0:64], wide[128:192, :], packed[128:192])


def finish_kernel(
    after,
    parts0,
    parts1,
    parts2,
    parts4,
    pre_ref,
    center_ref,
    sines_ref,
    patch_ref,
    head_ref,
    mod_ref,
    time_ref,
    *refs,
):
    patch_new, head_new, mod_new, time_new, sums, slope_rows = refs[after:]
    count = N_FSDP
    parts = [ref[i] for ref in (parts0, parts1, parts2, parts4) for i in range(ref.shape[0])]
    pre = pre_ref[...]
    gain, shift = gains(pre, mod_ref)
    head = head_ref[...].astype(bf16)
    head_f = head.astype(f32)
    center = center_ref[...]
    chi, clo = split2(center)
    curve = parts[0][128:192, 0:64]
    for k in range(1, count):
        curve = curve + parts[k][128:192, 0:64]
    curve_hi, curve_lo = split2(curve)
    grad_patch = -(dot(curve_hi, chi, NN) + dot(curve_lo, chi, NN) + dot(curve_hi, clo, NN))
    grad_head = jnp.zeros_like(center)
    grad_scale = jnp.zeros_like(gain[0:1])
    for k in range(count):
        plain = parts[k]
        turned = pltpu.roll(plain, 64, 1)
        sums[4 * k : 4 * k + 4, :] = turned[128:132]
        crosses, fine = split2(jnp.concatenate([plain[0:128, 0:64], turned[0:128, 0:64]], axis=0))
        mixed = dot(crosses, chi, NN) + dot(fine, chi, NN) + dot(crosses, clo, NN)
        pulls = []
        for i in range(4):
            s = 4 * k + i
            one = mixed[i * 64 : i * 64 + 64]
            grad_head = grad_head + one * gain[s : s + 1]
            slope = jnp.sum(head_f * one, axis=0, keepdims=True)
            slope_rows[s : s + 1, :] = slope
            grad_scale = grad_scale + slope
            pulls.append((head_f * gain[s : s + 1] - column(turned[132 + i : 133 + i])).astype(bf16))
        grad_patch = grad_patch + dot(crosses, jnp.concatenate(pulls, axis=0), TN)
    sum_hi, sum_lo = split2(sums[:, 0:64])
    shift_hi, shift_lo = split2(shift)
    grad_head = grad_head + dot(sum_hi, shift_hi, TN) + dot(sum_lo, shift_hi, TN) + dot(sum_hi, shift_lo, TN)
    mixed_sums = dot(sum_hi, head, NN) + dot(sum_lo, head, NN)
    grad_shift = jnp.sum(mixed_sums, axis=0, keepdims=True)
    grad_embed = mixed_sums + slope_rows[...]
    sigmoid = jax.nn.sigmoid(pre)
    grad_pre = (grad_embed * (sigmoid * (1.0 + pre * (1.0 - sigmoid)))).astype(bf16)
    grad_time = dot(sines_ref[...].astype(bf16), grad_pre, TN)
    patch_new[...] = patch_ref[...] - inner_rate * grad_patch
    head_new[...] = head_ref[...] - inner_rate * grad_head
    mod_new[0:1, :] = mod_ref[0:1, :] - inner_rate * grad_shift
    mod_new[1:2, :] = mod_ref[1:2, :] - inner_rate * grad_scale
    time_new[...] = time_ref[...] - inner_rate * grad_time


def sinusoid(time_steps):
    index = jnp.arange(FREQ_DIM // 2, dtype=f32)
    frequency = jnp.exp(-math.log(10000.0) * index / (FREQ_DIM // 2))
    angles = time_steps.astype(f32)[:, None] * frequency[None, :]
    return jnp.cos(angles), jnp.sin(angles)


def step_head(timesteps, patch):
    cos, sin = sinusoid(timesteps)
    row_sums = jnp.sum(patch.astype(bf16).astype(f32), axis=1)
    return jnp.concatenate(
        [cos, sin, jnp.pad(row_sums, (0, 128 - PATCH_DIM))[None], jnp.zeros((7, 128), f32)], axis=0
    )


def weight_products(near, away, patch, head, mod, time, after, width):
    columns = patch.shape[1]
    samples = 4 * N_FSDP
    share = jax.ShapeDtypeStruct((N_FSDP // 2, 192, 128), f32)
    return pl.pallas_call(
        functools.partial(weights_kernel, width, len(after)),
        in_specs=[pl.BlockSpec(memory_space=pltpu.VMEM)] * 6 + [unread] * len(after),
        out_shape=[
            share,
            share,
            jax.ShapeDtypeStruct((samples, columns), f32),
            jax.ShapeDtypeStruct((PATCH_DIM, columns), f32),
            jax.ShapeDtypeStruct((samples, FREQ_DIM), f32),
        ],
        scratch_shapes=[pltpu.VMEM((samples * PATCH_DIM, columns), bf16)] * 2,
        compiler_params=limit,
        cost_estimate=brief,
        name="weight_products",
    )(near, away, patch, head, mod, time, *after)


def token_sums(own, away, latents, target, after, width, tokens):
    return pl.pallas_call(
        functools.partial(tokens_kernel, width, tokens, len(after)),
        in_specs=[pl.BlockSpec(memory_space=pltpu.VMEM)] * 4 + [unread] * len(after),
        out_shape=jax.ShapeDtypeStruct((1, 192, 128), f32),
        scratch_shapes=[pltpu.VMEM((192, 128), f32)],
        compiler_params=limit,
        cost_estimate=brief,
        name="token_sums",
    )(own, away, latents, target, *after)


def finish(q0, q1, q2, q4, pre, center, sines, params, after):
    samples, columns = pre.shape
    return pl.pallas_call(
        functools.partial(finish_kernel, len(after)),
        in_specs=[pl.BlockSpec(memory_space=pltpu.VMEM)] * 11 + [unread] * len(after),
        out_shape=[jax.ShapeDtypeStruct(a.shape, f32) for a in params],
        scratch_shapes=[pltpu.VMEM((samples, 128), f32), pltpu.VMEM((samples, columns), f32)],
        compiler_params=limit,
        cost_estimate=brief,
        name="finish",
    )(q0, q1, q2, q4, pre, center, sines, *params, *after)


def solution(mesh):
    in_specs = (
        P(("replica", "fsdp"), None),
        P(("replica", "fsdp"), None),
        P(("replica", "fsdp")),
        P("replica", None, "fsdp"),
        P("replica", None, "fsdp"),
        P("replica", None, "fsdp"),
        P("replica", None, "fsdp"),
        P("fsdp", "replica"),
        P("fsdp", "replica"),
        P("fsdp", None),
        P("replica", "fsdp", None),
    )
    out_specs = (
        P("replica", None, "fsdp"),
        P("replica", None, "fsdp"),
        P("replica", None, "fsdp"),
        P("replica", None, "fsdp"),
        P("fsdp", "replica"),
        P("fsdp", "replica"),
        P("fsdp", None),
    )
    return jax.shard_map(
        per_device, mesh=mesh, in_specs=in_specs, out_specs=out_specs, check_vma=False
    )
```

```python
import functools
import math

import jax
import jax.numpy as jnp
from jax import lax
from jax.experimental import pallas as pl
from jax.experimental.pallas import tpu as pltpu
from jax.sharding import PartitionSpec as P

FREQ_DIM = 256
PATCH_DIM = 64
QBLOCK = 128
SAMPLE_TOKENS = 512

epsilon = 1e-06
inner_rate = 0.5
outer_rate = 0.7
momentum_decay = 0.9

f32 = jnp.float32
bf16 = jnp.bfloat16

N_Y, N_XH, N_CORE, N_FSDP = 4, 2, 2, 8
COL = 320
PAIR = 640
ROWS = 640
ROUND = 1.5 * 2.0**23
NUDGE = 1.0 + 2.0**-21

limit = pltpu.CompilerParams(vmem_limit_bytes=56 * 2**20)
brief = pl.CostEstimate(flops=1, bytes_accessed=1, transcendentals=0)
unread = pl.BlockSpec(memory_space=pl.ANY)

NT = (((1,), (1,)), ((), ()))
TN = (((0,), (0,)), ((), ()))
NN = (((1,), (0,)), ((), ()))


def dot(a, b, dims):
    return lax.dot_general(a, b, dims, preferred_element_type=f32)


def split2(x):
    hi = x.astype(bf16)
    return hi, (x - hi.astype(f32)).astype(bf16)


def quantized(delta):
    peak = jnp.max(jnp.abs(delta), axis=0, keepdims=True)
    scale = (peak + epsilon).astype(bf16).astype(f32)
    ratio = (7.0 / scale) * NUDGE
    shifted = delta * ratio + ROUND
    code = jnp.clip(shifted, ROUND - 7.0, ROUND + 7.0) - ROUND
    return code * (scale / 7.0)


def quant_kernel(pos_ref, start_ref, current_ref, keep, send):
    first_core = pos_ref[0] == 0
    low_lane = lax.broadcasted_iota(jnp.int32, (64, 128), 1) < 64
    for chip in range(N_Y * N_XH):
        dy = lax.rem(chip % N_Y - pos_ref[1] + N_Y, N_Y)
        dx = lax.rem(chip // N_Y - pos_ref[2] + N_XH, N_XH)
        slot = dy * N_XH + dx

        def terms(tile):
            lanes = slice(chip * PAIR + tile * 128, chip * PAIR + (tile + 1) * 128)
            return quantized(start_ref[:, lanes].astype(f32) - current_ref[:, lanes].astype(f32))

        def put(lane, low, high):
            keep[slot, :, lane : lane + 128] = jnp.where(first_core, low, high).astype(bf16)
            send[slot, :, lane : lane + 128] = jnp.where(first_core, high, low).astype(bf16)

        for tile in range(2):
            low, high = terms(tile), terms(tile + 3)
            put(tile * 128, low[:64], high[:64])
            put(256 + tile * 128, low[64:], high[64:])
        both = terms(2)
        top, bottom = both[:64], both[64:]
        low = jnp.where(low_lane, top, pltpu.roll(bottom, 64, 1))
        high = jnp.where(low_lane, pltpu.roll(top, 64, 1), bottom)
        put(512, low, high)


def quantize(pos, frag_start, frag_current):
    chips = N_Y * N_XH
    whole = pl.BlockSpec((QBLOCK, frag_start.shape[1]), lambda i, pos: (i, 0))
    made = pl.BlockSpec((chips, QBLOCK // 2, PAIR), lambda i, pos: (0, i, 0))
    keep, sent = pl.pallas_call(
        quant_kernel,
        grid_spec=pltpu.PrefetchScalarGridSpec(
            num_scalar_prefetch=1,
            grid=(ROWS // QBLOCK,),
            in_specs=[whole, whole],
            out_specs=[made, made],
        ),
        out_shape=[jax.ShapeDtypeStruct((chips, ROWS // 2, PAIR), bf16)] * 2,
        compiler_params=limit,
        cost_estimate=brief,
        name="quantize",
    )(pos, frag_start, frag_current)
    return keep.reshape(N_Y, N_XH, ROWS // 2, PAIR), sent.reshape(N_Y, N_XH, ROWS // 2, PAIR)


def outer_kernel(pos_ref, keep, got, up, down, up2, down2, far_ref, anchor_ref, momentum_ref, unread_ref, *refs):
    del unread_ref
    new_anchor, new_momentum, params, native, fresh, own_ref = refs
    chip_kernel(keep, got, up, down, up2, down2, own_ref)
    low_lane = lax.broadcasted_iota(jnp.int32, (64, 128), 1) < 64
    first_core = pos_ref[0] == 0
    for block in range(ROWS // QBLOCK):
        message = slice(block * 64, block * 64 + 64)
        both = own_ref[message] + far_ref[message].astype(f32)
        rest = both[:, 512:640]
        for half, tail in ((0, rest), (1, pltpu.roll(rest, 64, 1))):
            rows = slice(block * 128 + half * 64, block * 128 + half * 64 + 64)
            main0 = both[:, half * 256 : half * 256 + 128]
            main1 = both[:, half * 256 + 128 : half * 256 + 256]
            turn0, turn1 = pltpu.roll(main0, 64, 1), pltpu.roll(main1, 64, 1)
            native[rows, 0:128] = jnp.where(first_core, main0, jnp.where(low_lane, tail, turn0))
            native[rows, 128:256] = jnp.where(first_core, main1, jnp.where(low_lane, turn0, turn1))
            native[rows, 256:384] = jnp.where(first_core, tail, turn1)
        rows = slice(block * 128, block * 128 + 128)
        average = native[rows, 0:COL] / float(N_Y * N_XH * N_CORE)
        momentum = momentum_decay * momentum_ref[rows] + average
        anchor = anchor_ref[rows] - outer_rate * (average + momentum_decay * momentum)
        new_momentum[rows] = momentum
        new_anchor[rows] = anchor
        fresh[rows, 0:COL] = anchor
        for half in range(2):
            rows = slice(block * 128 + half * 64, block * 128 + half * 64 + 64)
            tiles = [fresh[rows, t * 128 : t * 128 + 128] for t in range(3)]
            turn = [pltpu.roll(tile, 64, 1) for tile in tiles]
            for t in range(2):
                value = jnp.where(first_core, tiles[t], jnp.where(low_lane, turn[t], turn[t + 1]))
                at = half * 256 + t * 128
                params[message, at : at + 128] = value.astype(bf16)
            if half == 0:
                top = jnp.where(first_core, tiles[2], tiles[0])
            else:
                bottom = jnp.where(first_core, turn[2], turn[0])
        params[message, 512:640] = jnp.where(low_lane, top, bottom).astype(bf16)


def outer_update(pos, keep, got, up, down, up2, down2, far, anchor, momentum, after):
    _, _, rows, columns = keep.shape
    came = pl.BlockSpec((1, rows // 2, columns), lambda i: (1, 0, 0))
    part = pl.BlockSpec((rows // 2, columns), lambda i: (0, 0))
    block = pl.BlockSpec((rows, columns), lambda i: (0, 0))
    plain = pl.BlockSpec((ROWS, COL), lambda i: (0, 0))
    return pl.pallas_call(
        outer_kernel,
        grid=(1,),
        in_specs=[pl.BlockSpec(memory_space=pltpu.SMEM)]
        + [spot(0, 0, rows, columns)] * 2
        + [came, came, part, part, block, plain, plain, unread],
        out_specs=[plain, plain, block],
        scratch_shapes=[
            pltpu.VMEM((ROWS, 384), f32),
            pltpu.VMEM((ROWS, 384), f32),
            pltpu.VMEM((rows, columns), f32),
        ],
        out_shape=[
            jax.ShapeDtypeStruct((ROWS, COL), f32),
            jax.ShapeDtypeStruct((ROWS, COL), f32),
            jax.ShapeDtypeStruct((rows, columns), bf16),
        ],
        compiler_params=limit,
        cost_estimate=brief,
        name="outer_update",
    )(pos, keep, got, up, down, up2, down2, far, anchor, momentum, after)


def place_kernel(chips, pos_ref, *refs):
    out = refs[-1]
    count = sum(2 if cut else 1 for _, _, cut in chips)
    mine, theirs = refs[:count], refs[count : 2 * count]
    first_core = pos_ref[0] == 0
    low_lane = lax.broadcasted_iota(jnp.int32, (64, 128), 1) < 64
    index = 0
    for dy, dx, cut in chips:
        a, b = mine[index][...], theirs[index][...]
        index += 1
        if cut:
            early = pl.program_id(0) < cut
            a = jnp.where(early, a, mine[index][...])
            b = jnp.where(early, b, theirs[index][...])
            index += 1
        low, high = jnp.where(first_core, a, b), jnp.where(first_core, b, a)
        chip = lax.rem(pos_ref[2] + dx, N_XH) * N_Y + lax.rem(pos_ref[1] + dy, N_Y)

        def put(half, lane, value):
            lanes = pl.ds(pl.multiple_of(chip * PAIR + lane, 128), value.shape[1])
            out[half * 64 : half * 64 + 64, lanes] = value

        for half in range(2):
            put(half, 0, low[:, half * 256 : half * 256 + 256])
            put(half, 384, high[:, half * 256 : half * 256 + 256])
        low_rest, high_rest = low[:, 512:640].astype(f32), high[:, 512:640].astype(f32)
        put(0, 256, jnp.where(low_lane, low_rest, pltpu.roll(high_rest, 64, 1)).astype(bf16))
        put(1, 256, jnp.where(low_lane, pltpu.roll(low_rest, 64, 1), high_rest).astype(bf16))


def place(pos, chips, mine, theirs, after):
    def blocks(cut):
        if not cut:
            return [pl.BlockSpec((64, PAIR), lambda i, pos: (i, 0))]
        return [
            pl.BlockSpec((64, PAIR), lambda i, pos: (jnp.minimum(i, cut - 1), 0)),
            pl.BlockSpec((64, PAIR), lambda i, pos: (jnp.maximum(i - cut, 0), 0)),
        ]

    specs = [spec for _, _, cut in chips for spec in blocks(cut)]
    return pl.pallas_call(
        functools.partial(place_kernel, chips),
        grid_spec=pltpu.PrefetchScalarGridSpec(
            num_scalar_prefetch=1,
            grid=(ROWS // QBLOCK,),
            in_specs=specs * 2 + [unread] * len(after),
            out_specs=pl.BlockSpec((QBLOCK, N_Y * N_XH * PAIR), lambda i, pos: (i, 0)),
        ),
        out_shape=jax.ShapeDtypeStruct((ROWS, N_Y * N_XH * PAIR), bf16),
        compiler_params=limit,
        cost_estimate=brief,
        name="place",
    )(pos, *mine, *theirs, *after)


def parts_kernel(below, above, first, second):
    cut = first.shape[0]
    first[...] = below[0:cut]
    second[...] = above[cut:]


def parts(below, above, cut):
    rows, columns = below.shape
    return pl.pallas_call(
        parts_kernel,
        out_shape=[jax.ShapeDtypeStruct((n, columns), below.dtype) for n in (cut * 64, rows - cut * 64)],
        compiler_params=limit,
        cost_estimate=brief,
        name="parts",
    )(below, above)


def join_kernel(after, *refs):
    parts, out = refs[: -1 - after], refs[-1]
    at = 0
    for part in parts:
        out[at : at + part.shape[0]] = part[...]
        at += part.shape[0]


def join(parts, after):
    count = sum(part.shape[0] for part in parts)
    return pl.pallas_call(
        functools.partial(join_kernel, len(after)),
        in_specs=[pl.BlockSpec(memory_space=pltpu.VMEM)] * len(parts) + [unread] * len(after),
        out_shape=jax.ShapeDtypeStruct((count,) + parts[0].shape[1:], f32),
        compiler_params=limit,
        cost_estimate=brief,
        name="join",
    )(*parts, *after)


def settle_kernel(a, b, unread_ref, a_out, b_out, token):
    del a, b, unread_ref, a_out, b_out
    token[...] = jnp.zeros_like(token)


def settle(a, b, after):
    return pl.pallas_call(
        settle_kernel,
        in_specs=[unread] * 3,
        out_specs=[unread] * 2 + [pl.BlockSpec(memory_space=pltpu.VMEM)],
        out_shape=[jax.ShapeDtypeStruct(x.shape, x.dtype) for x in (a, b)] + [jax.ShapeDtypeStruct((8, 128), f32)],
        input_output_aliases={0: 0, 1: 1},
        cost_estimate=brief,
        name="settle",
    )(a, b, after)


def gate_kernel(*refs):
    del refs


def gate(arrays, after):
    count = len(arrays)
    return pl.pallas_call(
        gate_kernel,
        in_specs=[unread] * (count + len(after)),
        out_specs=[unread] * count,
        out_shape=[jax.ShapeDtypeStruct(a.shape, a.dtype) for a in arrays],
        input_output_aliases={i: i for i in range(count)},
        cost_estimate=brief,
        name="gate",
    )(*arrays, *after)


def total(*refs):
    return sum(ref.astype(f32) for ref in refs)


def spot(dy, x, rows, columns, part=0):
    return pl.BlockSpec((1, 1, rows, columns), lambda i: (dy, x, part, 0))


def first_kernel(keep1, got1, keep2, got2, keep3, got3, up, down):
    half = up.shape[1]
    low, high = slice(0, half), slice(half, 2 * half)
    up[0] = total(keep2[0, 0, low], got2[0, 0, low]).astype(bf16)
    down[0] = total(keep2[0, 0, high], got2[0, 0, high]).astype(bf16)
    up[1] = total(keep1[0, 0], got1[0, 0]).astype(bf16)
    down[1] = total(keep3[0, 0], got3[0, 0]).astype(bf16)


def first_messages(keep, got, x, after):
    _, _, rows, columns = keep.shape
    half = rows // 2
    part = pl.BlockSpec((2, half, columns), lambda i: (0, 0, 0))
    shape = jax.ShapeDtypeStruct((2, half, columns), bf16)

    def kernel(*refs):
        first_kernel(*refs[:6], *refs[6 + len(after) :])

    return pl.pallas_call(
        kernel,
        grid=(1,),
        in_specs=[spot(1, x, half, columns, 1)] * 2
        + [spot(2, x, rows, columns)] * 2
        + [spot(3, x, half, columns, 0)] * 2
        + [unread] * len(after),
        out_specs=[part] * 2,
        out_shape=[shape] * 2,
        compiler_params=limit,
        cost_estimate=brief,
        name="first_messages",
    )(keep, got, keep, got, keep, got, *after)


def second_kernel(keep1, got1, keep3, got3, up, down, *refs):
    up_out, down_out = refs[-2:]
    up_out[...] = total(keep1[0, 0], got1[0, 0], up[0]).astype(bf16)
    down_out[...] = total(keep3[0, 0], got3[0, 0], down[0]).astype(bf16)


def second_messages(keep, got, up, down, x, after):
    _, _, rows, columns = keep.shape
    half = rows // 2
    came = pl.BlockSpec((1, half, columns), lambda i: (0, 0, 0))
    part = pl.BlockSpec((half, columns), lambda i: (0, 0))
    shape = jax.ShapeDtypeStruct((half, columns), bf16)
    return pl.pallas_call(
        second_kernel,
        grid=(1,),
        in_specs=[spot(1, x, half, columns, 0)] * 2 + [spot(3, x, half, columns, 1)] * 2 + [came] * 2 + [unread] * len(after),
        out_specs=[part] * 2,
        out_shape=[shape] * 2,
        compiler_params=limit,
        cost_estimate=brief,
        name="second_messages",
    )(keep, got, keep, got, up, down, *after)


def chip_kernel(keep, got, up, down, up2, down2, out):
    half = up.shape[1]
    low, high = slice(0, half), slice(half, 2 * half)
    out[low] = total(keep[0, 0, low], got[0, 0, low], down[0], up2[...]).astype(out.dtype)
    out[high] = total(keep[0, 0, high], got[0, 0, high], up[0], down2[...]).astype(out.dtype)


def chip_sum(keep, got, up, down, up2, down2, x, dtype):
    _, _, rows, columns = keep.shape
    came = pl.BlockSpec((1, rows // 2, columns), lambda i: (1, 0, 0))
    part = pl.BlockSpec((rows // 2, columns), lambda i: (0, 0))
    return pl.pallas_call(
        chip_kernel,
        grid=(1,),
        in_specs=[spot(0, x, rows, columns)] * 2 + [came] * 2 + [part] * 2,
        out_specs=pl.BlockSpec((rows, columns), lambda i: (0, 0)),
        out_shape=jax.ShapeDtypeStruct((rows, columns), dtype),
        compiler_params=limit,
        cost_estimate=brief,
        name="chip_sum",
    )(keep, got, up, down, up2, down2)


def per_device(
    latents,
    target,
    timesteps,
    patch_weight,
    head_weight,
    modulation,
    time_weight,
    anchor,
    momentum,
    frag_start,
    frag_current,
):
    frag_current = frag_current[0]
    params = (patch_weight[0], head_weight[0], modulation[0], time_weight[0])
    columns = params[0].shape[1]
    width = float(columns * N_FSDP)
    tokens = float(latents.shape[0] * N_FSDP)
    replica = lax.axis_index("replica")
    pos = jnp.stack([replica % 2, (replica // 2) % 4, replica // 8]).astype(jnp.int32)

    to_core = [(r, r ^ 1) for r in range(16)]
    to_x = [(r, r ^ 8) for r in range(16)]

    def to_y(step):
        return [
            (xh * 8 + y * 2 + c, xh * 8 + ((y + step) % N_Y) * 2 + c)
            for xh in range(N_XH)
            for y in range(N_Y)
            for c in range(N_CORE)
        ]

    send = functools.partial(lax.ppermute, axis_name="replica")
    to_sibling = functools.partial(send, perm=to_core)

    def across(value, bit):
        return lax.ppermute(value, "fsdp", [(i, i ^ bit) for i in range(N_FSDP)])

    h0 = step_head(timesteps, params[0])[None]
    h1 = across(h0, 1)
    keep, sent = quantize(pos, frag_start, frag_current)
    got = to_sibling(sent)
    h01 = join([h0, h1], [keep])
    h2 = across(h01, 2)
    up, down = [None, None], [None, None]

    def ring(x, messages):
        up[x], down[x] = send(messages[0], perm=to_y(1)), send(messages[1], perm=to_y(-1))

    message = first_messages(keep, got, 1, [])
    ring(1, message)
    h03 = join([h01, h2], [message[0]])
    h4 = across(h03, 4)
    near, away, pre, center, sines = weight_products(h03, h4, *params, [message[0]], width)
    away = across(away, 4)
    away2 = across(near[2:4] + away[2:4], 2)
    away1 = across(near[1:2] + away[1:2] + away2[1:2], 1)

    far = second_messages(keep, got, up[1], down[1], 1, [])
    far_up, far_down = send(far[0], perm=to_y(1)), send(far[1], perm=to_y(-1))
    ring(0, first_messages(keep, got, 0, [far[0]]))
    far = send(chip_sum(keep, got, up[1], down[1], far_up, far_down, 1, bf16), perm=to_x)
    own = second_messages(keep, got, up[0], down[0], 0, [anchor, momentum])
    own_up, own_down = send(own[0], perm=to_y(1)), send(own[1], perm=to_y(-1))
    q0 = token_sums(near[0:1] + away[0:1] + away2[0:1], away1, latents.T, target.T, [], width, tokens)
    q1 = across(q0, 1)
    new_anchor, new_momentum, n0 = outer_update(
        pos, keep, got, up[0], down[0], own_up, own_down, far, anchor, momentum, q0
    )

    n1 = send(n0, perm=to_x)
    up0, down0 = send(n0, perm=to_y(1)), send(n0, perm=to_y(-1))
    q01 = join([q0, q1], [])
    q2 = across(q01, 2)
    anchor_t, momentum_t, settled = settle(new_anchor.T, new_momentum.T, q01)
    q4 = across(join([q01, q2], [settled]), 4)
    first0 = parts(up0, down0, 2)
    on0 = send(first0[0], perm=to_y(1)), send(first0[1], perm=to_y(-1))
    (n1,) = gate([n1], [q01])
    up1, down1 = send(n1, perm=to_y(1)), send(n1, perm=to_y(-1))
    first1 = parts(up1, down1, 3)
    on1 = send(first1[0], perm=to_y(1)), send(first1[1], perm=to_y(-1))
    inner = finish(q0, q1, q2, q4, pre, center, sines, params, [first1[0]])
    mine = [n0, up0, down0, n1, up1, down1, *on0]
    mine = gate(mine, [*on1, inner[2], settled])
    mine = [*mine, *on1]
    theirs = [to_sibling(part) for part in mine]
    chips = ((0, 0, 0), (3, 0, 0), (1, 0, 0), (0, 1, 0), (3, 1, 0), (1, 1, 0), (2, 0, 2), (2, 1, 3))
    new_params = place(pos, chips, mine, theirs, [inner[2], settled])
    return tuple(a[None] for a in inner) + (anchor_t.T, momentum_t.T, new_params)


def column(row):
    eye = lax.broadcasted_iota(jnp.int32, (64, 128), 0) == lax.broadcasted_iota(jnp.int32, (64, 128), 1)
    return jnp.sum(jnp.where(eye, row, 0.0), axis=1, keepdims=True)


def gains(pre, mod_ref):
    embed = pre * jax.nn.sigmoid(pre)
    mod = mod_ref[...].astype(bf16).astype(f32)
    return 1.0 + mod[1:2] + embed, mod[0:1] + embed


def weights_kernel(width, after, near_heads, away_heads, patch_ref, head_ref, mod_ref, time_ref, *refs):
    near, away, pre_ref, center_ref, sines_ref, high, low = refs[after:]
    count = N_FSDP
    total = jnp.zeros((1, 128), f32)
    for k in range(count):
        head = (near_heads if k < count // 2 else away_heads)[k % (count // 2)]
        total = total + head[8:9]
        sines_ref[4 * k : 4 * k + 4, 0:128] = head[0:4]
        sines_ref[4 * k : 4 * k + 4, 128:256] = head[4:8]
    pre = dot(sines_ref[...].astype(bf16), time_ref[...].astype(bf16), NN)
    pre_ref[...] = pre
    gain, shift = gains(pre, mod_ref)
    center = patch_ref[...].astype(bf16).astype(f32) - column(total / width)
    center_ref[...] = center
    samples = 4 * count
    for s in range(samples):
        k, i = s // 4, s % 4
        at = (i // 2) * (samples // 2 * 64) + (2 * k + i % 2) * 64
        hi, lo = split2(center * gain[s : s + 1])
        high[at : at + 64, :] = hi
        low[at : at + 64, :] = lo
    head = head_ref[...].astype(bf16)
    blank = jnp.zeros_like(head)
    left = jnp.concatenate([head, blank], axis=0)
    right = jnp.concatenate([blank, head], axis=0)
    part = samples // 2 * 64
    packed = dot(high[0:part], left, NT) + dot(low[0:part], left, NT)
    packed = packed + dot(high[part:], right, NT) + dot(low[part:], right, NT)
    chi, clo = split2(center)
    chi_left = jnp.concatenate([chi, blank], axis=0)
    clo_left = jnp.concatenate([clo, blank], axis=0)
    gram = dot(chi, chi_left, NT) + dot(clo, chi_left, NT) + dot(chi, clo_left, NT)
    for k in range(count):
        out = near if k < count // 2 else away
        slot = k % (count // 2)
        rows = jnp.concatenate([shift[4 * k : 4 * k + 4], gain[4 * k : 4 * k + 4]], axis=0)
        hi, lo = split2(rows)
        extra = dot(hi, right, NT) + dot(lo, right, NT)
        out[slot, 0:128, :] = packed[128 * k : 128 * k + 128]
        out[slot, 128:136, :] = gram[0:8] + extra
        out[slot, 136:192, :] = gram[8:64]


def row(column):
    eye = lax.broadcasted_iota(jnp.int32, (64, 128), 0) == lax.broadcasted_iota(jnp.int32, (64, 128), 1)
    return jnp.sum(jnp.where(eye, column, 0.0), axis=0, keepdims=True)


def tokens_kernel(width, tokens, after, own_ref, away_ref, latent_ref, target_ref, *refs):
    out, wide = refs[after:]
    total = own_ref[0] + away_ref[0]
    turned = pltpu.roll(total, 64, 1)
    gram = total[128:192, 0:64] / width
    g0 = gram.astype(bf16)
    g1, g2 = split2(gram - g0.astype(f32))
    gain_means = turned[132:136, :] / width
    wide[...] = jnp.zeros_like(wide)
    curve = jnp.zeros((64, 64), f32)
    sums = []
    for s in range(4):
        at = slice(s * SAMPLE_TOKENS, (s + 1) * SAMPLE_TOKENS)
        latent = latent_ref[:, at]
        latent_f = latent.astype(f32)
        mix = (total if s < 2 else turned)[(s % 2) * 64 : (s % 2) * 64 + 64, 0:64]
        mix_hi, mix_lo = split2(mix)
        spread = dot(g0, latent, NN) + dot(g1, latent, NN) + dot(g2, latent, NN)
        variance = jnp.sum(spread * latent_f, axis=0, keepdims=True)
        inv_std = lax.rsqrt(jnp.maximum(variance, 0.0) + epsilon)
        varied = inv_std * (dot(mix_hi, latent, TN) + dot(mix_lo, latent, TN))
        output = varied + column(turned[128 + s : 129 + s, :])
        grad_out = (2.0 * (output - target_ref[:, at].astype(f32)) / tokens).astype(bf16)
        grad_f = grad_out.astype(f32)
        along = jnp.sum(grad_f * varied, axis=0, keepdims=True) / width
        cross = dot((grad_f * inv_std).astype(bf16), latent, NT)
        curve = curve + dot((latent_f * (along * inv_std * inv_std)).astype(bf16), latent, NT)
        sums.append(row(jnp.sum(grad_f, axis=1, keepdims=True)))
        if s < 2:
            out[0, s * 64 : s * 64 + 64, 0:64] = cross
        else:
            wide[(s - 2) * 64 : (s - 2) * 64 + 64, 0:64] = cross
    for s in range(4):
        wide[128 + s : 129 + s, :] = sums[s]
    wide[132:136, 0:64] = gain_means[:, 0:64]
    packed = pltpu.roll(wide[...], 64, 1)
    low_lane = lax.broadcasted_iota(jnp.int32, (128, 128), 1) < 64
    out[0, 0:128, :] = jnp.where(low_lane, out[0, 0:128, :], packed[0:128])
    wide[128:192, 0:64] = curve
    out[0, 128:192, :] = jnp.where(low_lane[0:64], wide[128:192, :], packed[128:192])


def finish_kernel(
    after,
    parts0,
    parts1,
    parts2,
    parts4,
    pre_ref,
    center_ref,
    sines_ref,
    patch_ref,
    head_ref,
    mod_ref,
    time_ref,
    *refs,
):
    patch_new, head_new, mod_new, time_new, sums, slope_rows = refs[after:]
    count = N_FSDP
    parts = [ref[i] for ref in (parts0, parts1, parts2, parts4) for i in range(ref.shape[0])]
    pre = pre_ref[...]
    gain, shift = gains(pre, mod_ref)
    head = head_ref[...].astype(bf16)
    head_f = head.astype(f32)
    center = center_ref[...]
    chi, clo = split2(center)
    curve = parts[0][128:192, 0:64]
    for k in range(1, count):
        curve = curve + parts[k][128:192, 0:64]
    curve_hi, curve_lo = split2(curve)
    grad_patch = -(dot(curve_hi, chi, NN) + dot(curve_lo, chi, NN) + dot(curve_hi, clo, NN))
    grad_head = jnp.zeros_like(center)
    grad_scale = jnp.zeros_like(gain[0:1])
    for k in range(count):
        plain = parts[k]
        turned = pltpu.roll(plain, 64, 1)
        sums[4 * k : 4 * k + 4, :] = turned[128:132]
        crosses, fine = split2(jnp.concatenate([plain[0:128, 0:64], turned[0:128, 0:64]], axis=0))
        mixed = dot(crosses, chi, NN) + dot(fine, chi, NN) + dot(crosses, clo, NN)
        pulls = []
        for i in range(4):
            s = 4 * k + i
            one = mixed[i * 64 : i * 64 + 64]
            grad_head = grad_head + one * gain[s : s + 1]
            slope = jnp.sum(head_f * one, axis=0, keepdims=True)
            slope_rows[s : s + 1, :] = slope
            grad_scale = grad_scale + slope
            pulls.append((head_f * gain[s : s + 1] - column(turned[132 + i : 133 + i])).astype(bf16))
        grad_patch = grad_patch + dot(crosses, jnp.concatenate(pulls, axis=0), TN)
    sum_hi, sum_lo = split2(sums[:, 0:64])
    shift_hi, shift_lo = split2(shift)
    grad_head = grad_head + dot(sum_hi, shift_hi, TN) + dot(sum_lo, shift_hi, TN) + dot(sum_hi, shift_lo, TN)
    mixed_sums = dot(sum_hi, head, NN) + dot(sum_lo, head, NN)
    grad_shift = jnp.sum(mixed_sums, axis=0, keepdims=True)
    grad_embed = mixed_sums + slope_rows[...]
    sigmoid = jax.nn.sigmoid(pre)
    grad_pre = (grad_embed * (sigmoid * (1.0 + pre * (1.0 - sigmoid)))).astype(bf16)
    grad_time = dot(sines_ref[...].astype(bf16), grad_pre, TN)
    patch_new[...] = patch_ref[...] - inner_rate * grad_patch
    head_new[...] = head_ref[...] - inner_rate * grad_head
    mod_new[0:1, :] = mod_ref[0:1, :] - inner_rate * grad_shift
    mod_new[1:2, :] = mod_ref[1:2, :] - inner_rate * grad_scale
    time_new[...] = time_ref[...] - inner_rate * grad_time


def sinusoid(time_steps):
    index = jnp.arange(FREQ_DIM // 2, dtype=f32)
    frequency = jnp.exp(-math.log(10000.0) * index / (FREQ_DIM // 2))
    angles = time_steps.astype(f32)[:, None] * frequency[None, :]
    return jnp.cos(angles), jnp.sin(angles)


def step_head(timesteps, patch):
    cos, sin = sinusoid(timesteps)
    row_sums = jnp.sum(patch.astype(bf16).astype(f32), axis=1)
    return jnp.concatenate(
        [cos, sin, jnp.pad(row_sums, (0, 128 - PATCH_DIM))[None], jnp.zeros((7, 128), f32)], axis=0
    )


def weight_products(near, away, patch, head, mod, time, after, width):
    columns = patch.shape[1]
    samples = 4 * N_FSDP
    share = jax.ShapeDtypeStruct((N_FSDP // 2, 192, 128), f32)
    return pl.pallas_call(
        functools.partial(weights_kernel, width, len(after)),
        in_specs=[pl.BlockSpec(memory_space=pltpu.VMEM)] * 6 + [unread] * len(after),
        out_shape=[
            share,
            share,
            jax.ShapeDtypeStruct((samples, columns), f32),
            jax.ShapeDtypeStruct((PATCH_DIM, columns), f32),
            jax.ShapeDtypeStruct((samples, FREQ_DIM), f32),
        ],
        scratch_shapes=[pltpu.VMEM((samples * PATCH_DIM, columns), bf16)] * 2,
        compiler_params=limit,
        cost_estimate=brief,
        name="weight_products",
    )(near, away, patch, head, mod, time, *after)


def token_sums(own, away, latents, target, after, width, tokens):
    return pl.pallas_call(
        functools.partial(tokens_kernel, width, tokens, len(after)),
        in_specs=[pl.BlockSpec(memory_space=pltpu.VMEM)] * 4 + [unread] * len(after),
        out_shape=jax.ShapeDtypeStruct((1, 192, 128), f32),
        scratch_shapes=[pltpu.VMEM((192, 128), f32)],
        compiler_params=limit,
        cost_estimate=brief,
        name="token_sums",
    )(own, away, latents, target, *after)


def finish(q0, q1, q2, q4, pre, center, sines, params, after):
    samples, columns = pre.shape
    return pl.pallas_call(
        functools.partial(finish_kernel, len(after)),
        in_specs=[pl.BlockSpec(memory_space=pltpu.VMEM)] * 11 + [unread] * len(after),
        out_shape=[jax.ShapeDtypeStruct(a.shape, f32) for a in params],
        scratch_shapes=[pltpu.VMEM((samples, 128), f32), pltpu.VMEM((samples, columns), f32)],
        compiler_params=limit,
        cost_estimate=brief,
        name="finish",
    )(q0, q1, q2, q4, pre, center, sines, *params, *after)


def solution(mesh):
    in_specs = (
        P(("replica", "fsdp"), None),
        P(("replica", "fsdp"), None),
        P(("replica", "fsdp")),
        P("replica", None, "fsdp"),
        P("replica", None, "fsdp"),
        P("replica", None, "fsdp"),
        P("replica", None, "fsdp"),
        P("fsdp", "replica"),
        P("fsdp", "replica"),
        P("fsdp", None),
        P("replica", "fsdp", None),
    )
    out_specs = (
        P("replica", None, "fsdp"),
        P("replica", None, "fsdp"),
        P("replica", None, "fsdp"),
        P("replica", None, "fsdp"),
        P("fsdp", "replica"),
        P("fsdp", "replica"),
        P("fsdp", None),
    )
    return jax.shard_map(
        per_device, mesh=mesh, in_specs=in_specs, out_specs=out_specs, check_vma=False
    )
```

```python
import functools
import math

import jax
import jax.numpy as jnp
from jax import lax
from jax.experimental import pallas as pl
from jax.experimental.pallas import tpu as pltpu
from jax.sharding import PartitionSpec as P

FREQ_DIM = 256
PATCH_DIM = 64
QBLOCK = 128
SAMPLE_TOKENS = 512

epsilon = 1e-06
inner_rate = 0.5
outer_rate = 0.7
momentum_decay = 0.9

f32 = jnp.float32
bf16 = jnp.bfloat16

N_Y, N_XH, N_CORE, N_FSDP = 4, 2, 2, 8
COL = 320
PAIR = 640
ROWS = 640
ROUND = 1.5 * 2.0**23
NUDGE = 1.0 + 2.0**-21

limit = pltpu.CompilerParams(vmem_limit_bytes=62 * 2**20)
brief = pl.CostEstimate(flops=1, bytes_accessed=1, transcendentals=0)
unread = pl.BlockSpec(memory_space=pl.ANY)

NT = (((1,), (1,)), ((), ()))
TN = (((0,), (0,)), ((), ()))
NN = (((1,), (0,)), ((), ()))


def dot(a, b, dims):
    return lax.dot_general(a, b, dims, preferred_element_type=f32)


def split2(x):
    hi = x.astype(bf16)
    return hi, (x - hi.astype(f32)).astype(bf16)


def quantized(delta):
    peak = jnp.max(jnp.abs(delta), axis=0, keepdims=True)
    scale = (peak + epsilon).astype(bf16).astype(f32)
    ratio = (7.0 / scale) * NUDGE
    shifted = delta * ratio + ROUND
    code = jnp.clip(shifted, ROUND - 7.0, ROUND + 7.0) - ROUND
    return code * (scale / 7.0)


def quant_kernel(pos_ref, start_ref, current_ref, keep, send):
    first_core = pos_ref[0] == 0
    low_lane = lax.broadcasted_iota(jnp.int32, (64, 128), 1) < 64
    for chip in range(N_Y * N_XH):
        dy = lax.rem(chip % N_Y - pos_ref[1] + N_Y, N_Y)
        dx = lax.rem(chip // N_Y - pos_ref[2] + N_XH, N_XH)
        slot = dy * N_XH + dx

        def terms(tile):
            lanes = slice(chip * PAIR + tile * 128, chip * PAIR + (tile + 1) * 128)
            return quantized(start_ref[:, lanes].astype(f32) - current_ref[:, lanes].astype(f32))

        def put(lane, low, high):
            keep[slot, :, lane : lane + 128] = jnp.where(first_core, low, high).astype(bf16)
            send[slot, :, lane : lane + 128] = jnp.where(first_core, high, low).astype(bf16)

        for tile in range(2):
            low, high = terms(tile), terms(tile + 3)
            put(tile * 128, low[:64], high[:64])
            put(256 + tile * 128, low[64:], high[64:])
        both = terms(2)
        top, bottom = both[:64], both[64:]
        low = jnp.where(low_lane, top, pltpu.roll(bottom, 64, 1))
        high = jnp.where(low_lane, pltpu.roll(top, 64, 1), bottom)
        put(512, low, high)


def quantize(pos, frag_start, frag_current):
    chips = N_Y * N_XH
    whole = pl.BlockSpec((QBLOCK, frag_start.shape[1]), lambda i, pos: (i, 0))
    made = pl.BlockSpec((chips, QBLOCK // 2, PAIR), lambda i, pos: (0, i, 0))
    keep, sent = pl.pallas_call(
        quant_kernel,
        grid_spec=pltpu.PrefetchScalarGridSpec(
            num_scalar_prefetch=1,
            grid=(ROWS // QBLOCK,),
            in_specs=[whole, whole],
            out_specs=[made, made],
        ),
        out_shape=[jax.ShapeDtypeStruct((chips, ROWS // 2, PAIR), bf16)] * 2,
        compiler_params=limit,
        cost_estimate=brief,
        name="quantize",
    )(pos, frag_start, frag_current)
    return keep.reshape(N_Y, N_XH, ROWS // 2, PAIR), sent.reshape(N_Y, N_XH, ROWS // 2, PAIR)


def outer_kernel(pos_ref, keep, got, up, down, up2, down2, far_ref, anchor_ref, momentum_ref, unread_ref, *refs):
    del unread_ref
    new_anchor, new_momentum, params, native, fresh, own_ref = refs
    chip_kernel(keep, got, up, down, up2, down2, own_ref)
    low_lane = lax.broadcasted_iota(jnp.int32, (64, 128), 1) < 64
    first_core = pos_ref[0] == 0
    for block in range(ROWS // QBLOCK):
        message = slice(block * 64, block * 64 + 64)
        both = own_ref[message] + far_ref[message].astype(f32)
        rest = both[:, 512:640]
        for half, tail in ((0, rest), (1, pltpu.roll(rest, 64, 1))):
            rows = slice(block * 128 + half * 64, block * 128 + half * 64 + 64)
            main0 = both[:, half * 256 : half * 256 + 128]
            main1 = both[:, half * 256 + 128 : half * 256 + 256]
            turn0, turn1 = pltpu.roll(main0, 64, 1), pltpu.roll(main1, 64, 1)
            native[rows, 0:128] = jnp.where(first_core, main0, jnp.where(low_lane, tail, turn0))
            native[rows, 128:256] = jnp.where(first_core, main1, jnp.where(low_lane, turn0, turn1))
            native[rows, 256:384] = jnp.where(first_core, tail, turn1)
        rows = slice(block * 128, block * 128 + 128)
        average = native[rows, 0:COL] / float(N_Y * N_XH * N_CORE)
        momentum = momentum_decay * momentum_ref[rows] + average
        anchor = anchor_ref[rows] - outer_rate * (average + momentum_decay * momentum)
        new_momentum[rows] = momentum
        new_anchor[rows] = anchor
        fresh[rows, 0:COL] = anchor
        for half in range(2):
            rows = slice(block * 128 + half * 64, block * 128 + half * 64 + 64)
            tiles = [fresh[rows, t * 128 : t * 128 + 128] for t in range(3)]
            turn = [pltpu.roll(tile, 64, 1) for tile in tiles]
            for t in range(2):
                value = jnp.where(first_core, tiles[t], jnp.where(low_lane, turn[t], turn[t + 1]))
                at = half * 256 + t * 128
                params[message, at : at + 128] = value.astype(bf16)
            if half == 0:
                top = jnp.where(first_core, tiles[2], tiles[0])
            else:
                bottom = jnp.where(first_core, turn[2], turn[0])
        params[message, 512:640] = jnp.where(low_lane, top, bottom).astype(bf16)


def outer_update(pos, keep, got, up, down, up2, down2, far, anchor, momentum, after):
    _, _, rows, columns = keep.shape
    came = pl.BlockSpec((1, rows // 2, columns), lambda i: (1, 0, 0))
    part = pl.BlockSpec((rows // 2, columns), lambda i: (0, 0))
    block = pl.BlockSpec((rows, columns), lambda i: (0, 0))
    plain = pl.BlockSpec((ROWS, COL), lambda i: (0, 0))
    return pl.pallas_call(
        outer_kernel,
        grid=(1,),
        in_specs=[pl.BlockSpec(memory_space=pltpu.SMEM)]
        + [spot(0, 0, rows, columns)] * 2
        + [came, came, part, part, block, plain, plain, unread],
        out_specs=[plain, plain, block],
        scratch_shapes=[
            pltpu.VMEM((ROWS, 384), f32),
            pltpu.VMEM((ROWS, 384), f32),
            pltpu.VMEM((rows, columns), f32),
        ],
        out_shape=[
            jax.ShapeDtypeStruct((ROWS, COL), f32),
            jax.ShapeDtypeStruct((ROWS, COL), f32),
            jax.ShapeDtypeStruct((rows, columns), bf16),
        ],
        compiler_params=limit,
        cost_estimate=brief,
        name="outer_update",
    )(pos, keep, got, up, down, up2, down2, far, anchor, momentum, after)


def place_kernel(chips, pos_ref, *refs):
    out = refs[-1]
    count = sum(2 if cut else 1 for _, _, cut in chips)
    mine, theirs = refs[:count], refs[count : 2 * count]
    first_core = pos_ref[0] == 0
    low_lane = lax.broadcasted_iota(jnp.int32, (64, 128), 1) < 64
    index = 0
    for dy, dx, cut in chips:
        a, b = mine[index][...], theirs[index][...]
        index += 1
        if cut:
            early = pl.program_id(0) < cut
            a = jnp.where(early, a, mine[index][...])
            b = jnp.where(early, b, theirs[index][...])
            index += 1
        low, high = jnp.where(first_core, a, b), jnp.where(first_core, b, a)
        chip = lax.rem(pos_ref[2] + dx, N_XH) * N_Y + lax.rem(pos_ref[1] + dy, N_Y)

        def put(half, lane, value):
            lanes = pl.ds(pl.multiple_of(chip * PAIR + lane, 128), value.shape[1])
            out[half * 64 : half * 64 + 64, lanes] = value

        for half in range(2):
            put(half, 0, low[:, half * 256 : half * 256 + 256])
            put(half, 384, high[:, half * 256 : half * 256 + 256])
        low_rest, high_rest = low[:, 512:640].astype(f32), high[:, 512:640].astype(f32)
        put(0, 256, jnp.where(low_lane, low_rest, pltpu.roll(high_rest, 64, 1)).astype(bf16))
        put(1, 256, jnp.where(low_lane, pltpu.roll(low_rest, 64, 1), high_rest).astype(bf16))


def place(pos, chips, mine, theirs, after):
    def blocks(cut):
        if not cut:
            return [pl.BlockSpec((64, PAIR), lambda i, pos: (i, 0))]
        return [
            pl.BlockSpec((64, PAIR), lambda i, pos: (jnp.minimum(i, cut - 1), 0)),
            pl.BlockSpec((64, PAIR), lambda i, pos: (jnp.maximum(i - cut, 0), 0)),
        ]

    specs = [spec for _, _, cut in chips for spec in blocks(cut)]
    return pl.pallas_call(
        functools.partial(place_kernel, chips),
        grid_spec=pltpu.PrefetchScalarGridSpec(
            num_scalar_prefetch=1,
            grid=(ROWS // QBLOCK,),
            in_specs=specs * 2 + [unread] * len(after),
            out_specs=pl.BlockSpec((QBLOCK, N_Y * N_XH * PAIR), lambda i, pos: (i, 0)),
        ),
        out_shape=jax.ShapeDtypeStruct((ROWS, N_Y * N_XH * PAIR), bf16),
        compiler_params=limit,
        cost_estimate=brief,
        name="place",
    )(pos, *mine, *theirs, *after)


def parts_kernel(below, above, first, second):
    cut = first.shape[0]
    first[...] = below[0:cut]
    second[...] = above[cut:]


def parts(below, above, cut):
    rows, columns = below.shape
    return pl.pallas_call(
        parts_kernel,
        out_shape=[jax.ShapeDtypeStruct((n, columns), below.dtype) for n in (cut * 64, rows - cut * 64)],
        compiler_params=limit,
        cost_estimate=brief,
        name="parts",
    )(below, above)


def join_kernel(after, *refs):
    parts, out = refs[: -1 - after], refs[-1]
    at = 0
    for part in parts:
        out[at : at + part.shape[0]] = part[...]
        at += part.shape[0]


def join(parts, after):
    count = sum(part.shape[0] for part in parts)
    return pl.pallas_call(
        functools.partial(join_kernel, len(after)),
        in_specs=[pl.BlockSpec(memory_space=pltpu.VMEM)] * len(parts) + [unread] * len(after),
        out_shape=jax.ShapeDtypeStruct((count,) + parts[0].shape[1:], f32),
        compiler_params=limit,
        cost_estimate=brief,
        name="join",
    )(*parts, *after)


def settle_kernel(a, b, unread_ref, a_out, b_out, token):
    del a, b, unread_ref, a_out, b_out
    token[...] = jnp.zeros_like(token)


def settle(a, b, after):
    return pl.pallas_call(
        settle_kernel,
        in_specs=[unread] * 3,
        out_specs=[unread] * 2 + [pl.BlockSpec(memory_space=pltpu.VMEM)],
        out_shape=[jax.ShapeDtypeStruct(x.shape, x.dtype) for x in (a, b)] + [jax.ShapeDtypeStruct((8, 128), f32)],
        input_output_aliases={0: 0, 1: 1},
        cost_estimate=brief,
        name="settle",
    )(a, b, after)


def gate_kernel(*refs):
    del refs


def gate(arrays, after):
    count = len(arrays)
    return pl.pallas_call(
        gate_kernel,
        in_specs=[unread] * (count + len(after)),
        out_specs=[unread] * count,
        out_shape=[jax.ShapeDtypeStruct(a.shape, a.dtype) for a in arrays],
        input_output_aliases={i: i for i in range(count)},
        cost_estimate=brief,
        name="gate",
    )(*arrays, *after)


def total(*refs):
    return sum(ref.astype(f32) for ref in refs)


def spot(dy, x, rows, columns, part=0):
    return pl.BlockSpec((1, 1, rows, columns), lambda i: (dy, x, part, 0))


def first_kernel(keep1, got1, keep2, got2, keep3, got3, up, down):
    half = up.shape[1]
    low, high = slice(0, half), slice(half, 2 * half)
    up[0] = total(keep2[0, 0, low], got2[0, 0, low]).astype(bf16)
    down[0] = total(keep2[0, 0, high], got2[0, 0, high]).astype(bf16)
    up[1] = total(keep1[0, 0], got1[0, 0]).astype(bf16)
    down[1] = total(keep3[0, 0], got3[0, 0]).astype(bf16)


def first_messages(keep, got, x, after):
    _, _, rows, columns = keep.shape
    half = rows // 2
    part = pl.BlockSpec((2, half, columns), lambda i: (0, 0, 0))
    shape = jax.ShapeDtypeStruct((2, half, columns), bf16)

    def kernel(*refs):
        first_kernel(*refs[:6], *refs[6 + len(after) :])

    return pl.pallas_call(
        kernel,
        grid=(1,),
        in_specs=[spot(1, x, half, columns, 1)] * 2
        + [spot(2, x, rows, columns)] * 2
        + [spot(3, x, half, columns, 0)] * 2
        + [unread] * len(after),
        out_specs=[part] * 2,
        out_shape=[shape] * 2,
        compiler_params=limit,
        cost_estimate=brief,
        name="first_messages",
    )(keep, got, keep, got, keep, got, *after)


def second_kernel(keep1, got1, keep3, got3, up, down, *refs):
    up_out, down_out = refs[-2:]
    up_out[...] = total(keep1[0, 0], got1[0, 0], up[0]).astype(bf16)
    down_out[...] = total(keep3[0, 0], got3[0, 0], down[0]).astype(bf16)


def second_messages(keep, got, up, down, x, after):
    _, _, rows, columns = keep.shape
    half = rows // 2
    came = pl.BlockSpec((1, half, columns), lambda i: (0, 0, 0))
    part = pl.BlockSpec((half, columns), lambda i: (0, 0))
    shape = jax.ShapeDtypeStruct((half, columns), bf16)
    return pl.pallas_call(
        second_kernel,
        grid=(1,),
        in_specs=[spot(1, x, half, columns, 0)] * 2 + [spot(3, x, half, columns, 1)] * 2 + [came] * 2 + [unread] * len(after),
        out_specs=[part] * 2,
        out_shape=[shape] * 2,
        compiler_params=limit,
        cost_estimate=brief,
        name="second_messages",
    )(keep, got, keep, got, up, down, *after)


def chip_kernel(keep, got, up, down, up2, down2, out):
    half = up.shape[1]
    low, high = slice(0, half), slice(half, 2 * half)
    out[low] = total(keep[0, 0, low], got[0, 0, low], down[0], up2[...]).astype(out.dtype)
    out[high] = total(keep[0, 0, high], got[0, 0, high], up[0], down2[...]).astype(out.dtype)


def chip_sum(keep, got, up, down, up2, down2, x, dtype):
    _, _, rows, columns = keep.shape
    came = pl.BlockSpec((1, rows // 2, columns), lambda i: (1, 0, 0))
    part = pl.BlockSpec((rows // 2, columns), lambda i: (0, 0))
    return pl.pallas_call(
        chip_kernel,
        grid=(1,),
        in_specs=[spot(0, x, rows, columns)] * 2 + [came] * 2 + [part] * 2,
        out_specs=pl.BlockSpec((rows, columns), lambda i: (0, 0)),
        out_shape=jax.ShapeDtypeStruct((rows, columns), dtype),
        compiler_params=limit,
        cost_estimate=brief,
        name="chip_sum",
    )(keep, got, up, down, up2, down2)


def per_device(
    latents,
    target,
    timesteps,
    patch_weight,
    head_weight,
    modulation,
    time_weight,
    anchor,
    momentum,
    frag_start,
    frag_current,
):
    frag_current = frag_current[0]
    params = (patch_weight[0], head_weight[0], modulation[0], time_weight[0])
    columns = params[0].shape[1]
    width = float(columns * N_FSDP)
    tokens = float(latents.shape[0] * N_FSDP)
    replica = lax.axis_index("replica")
    pos = jnp.stack([replica % 2, (replica // 2) % 4, replica // 8]).astype(jnp.int32)

    to_core = [(r, r ^ 1) for r in range(16)]
    to_x = [(r, r ^ 8) for r in range(16)]

    def to_y(step):
        return [
            (xh * 8 + y * 2 + c, xh * 8 + ((y + step) % N_Y) * 2 + c)
            for xh in range(N_XH)
            for y in range(N_Y)
            for c in range(N_CORE)
        ]

    send = functools.partial(lax.ppermute, axis_name="replica")
    to_sibling = functools.partial(send, perm=to_core)

    def across(value, bit):
        return lax.ppermute(value, "fsdp", [(i, i ^ bit) for i in range(N_FSDP)])

    h0 = step_head(timesteps, params[0])[None]
    h1 = across(h0, 1)
    keep, sent = quantize(pos, frag_start, frag_current)
    got = to_sibling(sent)
    h01 = join([h0, h1], [keep])
    h2 = across(h01, 2)
    up, down = [None, None], [None, None]

    def ring(x, messages):
        up[x], down[x] = send(messages[0], perm=to_y(1)), send(messages[1], perm=to_y(-1))

    message = first_messages(keep, got, 1, [])
    ring(1, message)
    h03 = join([h01, h2], [message[0]])
    h4 = across(h03, 4)
    near, away, pre, center, sines = weight_products(h03, h4, *params, [message[0]], width)
    away = across(away, 4)
    away2 = across(near[2:4] + away[2:4], 2)
    away1 = across(near[1:2] + away[1:2] + away2[1:2], 1)

    far = second_messages(keep, got, up[1], down[1], 1, [])
    far_up, far_down = send(far[0], perm=to_y(1)), send(far[1], perm=to_y(-1))
    ring(0, first_messages(keep, got, 0, [far[0]]))
    far = send(chip_sum(keep, got, up[1], down[1], far_up, far_down, 1, bf16), perm=to_x)
    own = second_messages(keep, got, up[0], down[0], 0, [anchor, momentum])
    own_up, own_down = send(own[0], perm=to_y(1)), send(own[1], perm=to_y(-1))
    q0 = token_sums(near[0:1] + away[0:1] + away2[0:1], away1, latents.T, target.T, [], width, tokens)
    q1 = across(q0, 1)
    new_anchor, new_momentum, n0 = outer_update(
        pos, keep, got, up[0], down[0], own_up, own_down, far, anchor, momentum, q0
    )

    n1 = send(n0, perm=to_x)
    up0, down0 = send(n0, perm=to_y(1)), send(n0, perm=to_y(-1))
    q01 = join([q0, q1], [])
    q2 = across(q01, 2)
    anchor_t, momentum_t, settled = settle(new_anchor.T, new_momentum.T, q01)
    q4 = across(join([q01, q2], [settled]), 4)
    first0 = parts(up0, down0, 2)
    on0 = send(first0[0], perm=to_y(1)), send(first0[1], perm=to_y(-1))
    (n1,) = gate([n1], [q01])
    up1, down1 = send(n1, perm=to_y(1)), send(n1, perm=to_y(-1))
    first1 = parts(up1, down1, 3)
    on1 = send(first1[0], perm=to_y(1)), send(first1[1], perm=to_y(-1))
    inner = finish(q0, q1, q2, q4, pre, center, sines, params, [first1[0]])
    mine = [n0, up0, down0, n1, up1, down1, *on0]
    mine = gate(mine, [*on1, inner[2], settled])
    mine = [*mine, *on1]
    theirs = [to_sibling(part) for part in mine]
    chips = ((0, 0, 0), (3, 0, 0), (1, 0, 0), (0, 1, 0), (3, 1, 0), (1, 1, 0), (2, 0, 2), (2, 1, 3))
    new_params = place(pos, chips, mine, theirs, [inner[2], settled])
    return tuple(a[None] for a in inner) + (anchor_t.T, momentum_t.T, new_params)


def column(row):
    eye = lax.broadcasted_iota(jnp.int32, (64, 128), 0) == lax.broadcasted_iota(jnp.int32, (64, 128), 1)
    return jnp.sum(jnp.where(eye, row, 0.0), axis=1, keepdims=True)


def gains(pre, mod_ref):
    embed = pre * jax.nn.sigmoid(pre)
    mod = mod_ref[...].astype(bf16).astype(f32)
    return 1.0 + mod[1:2] + embed, mod[0:1] + embed


def weights_kernel(width, after, near_heads, away_heads, patch_ref, head_ref, mod_ref, time_ref, *refs):
    near, away, pre_ref, center_ref, sines_ref, high, low = refs[after:]
    count = N_FSDP
    total = jnp.zeros((1, 128), f32)
    for k in range(count):
        head = (near_heads if k < count // 2 else away_heads)[k % (count // 2)]
        total = total + head[8:9]
        sines_ref[4 * k : 4 * k + 4, 0:128] = head[0:4]
        sines_ref[4 * k : 4 * k + 4, 128:256] = head[4:8]
    pre = dot(sines_ref[...].astype(bf16), time_ref[...].astype(bf16), NN)
    pre_ref[...] = pre
    gain, shift = gains(pre, mod_ref)
    center = patch_ref[...].astype(bf16).astype(f32) - column(total / width)
    center_ref[...] = center
    samples = 4 * count
    for s in range(samples):
        k, i = s // 4, s % 4
        at = (i // 2) * (samples // 2 * 64) + (2 * k + i % 2) * 64
        hi, lo = split2(center * gain[s : s + 1])
        high[at : at + 64, :] = hi
        low[at : at + 64, :] = lo
    head = head_ref[...].astype(bf16)
    blank = jnp.zeros_like(head)
    left = jnp.concatenate([head, blank], axis=0)
    right = jnp.concatenate([blank, head], axis=0)
    part = samples // 2 * 64
    packed = dot(high[0:part], left, NT) + dot(low[0:part], left, NT)
    packed = packed + dot(high[part:], right, NT) + dot(low[part:], right, NT)
    chi, clo = split2(center)
    chi_left = jnp.concatenate([chi, blank], axis=0)
    clo_left = jnp.concatenate([clo, blank], axis=0)
    gram = dot(chi, chi_left, NT) + dot(clo, chi_left, NT) + dot(chi, clo_left, NT)
    for k in range(count):
        out = near if k < count // 2 else away
        slot = k % (count // 2)
        rows = jnp.concatenate([shift[4 * k : 4 * k + 4], gain[4 * k : 4 * k + 4]], axis=0)
        hi, lo = split2(rows)
        extra = dot(hi, right, NT) + dot(lo, right, NT)
        out[slot, 0:128, :] = packed[128 * k : 128 * k + 128]
        out[slot, 128:136, :] = gram[0:8] + extra
        out[slot, 136:192, :] = gram[8:64]


def row(column):
    eye = lax.broadcasted_iota(jnp.int32, (64, 128), 0) == lax.broadcasted_iota(jnp.int32, (64, 128), 1)
    return jnp.sum(jnp.where(eye, column, 0.0), axis=0, keepdims=True)


def tokens_kernel(width, tokens, after, own_ref, away_ref, latent_ref, target_ref, *refs):
    out, wide = refs[after:]
    total = own_ref[0] + away_ref[0]
    turned = pltpu.roll(total, 64, 1)
    gram = total[128:192, 0:64] / width
    g0 = gram.astype(bf16)
    g1, g2 = split2(gram - g0.astype(f32))
    gain_means = turned[132:136, :] / width
    wide[...] = jnp.zeros_like(wide)
    curve = jnp.zeros((64, 64), f32)
    sums = []
    for s in range(4):
        at = slice(s * SAMPLE_TOKENS, (s + 1) * SAMPLE_TOKENS)
        latent = latent_ref[:, at]
        latent_f = latent.astype(f32)
        mix = (total if s < 2 else turned)[(s % 2) * 64 : (s % 2) * 64 + 64, 0:64]
        mix_hi, mix_lo = split2(mix)
        spread = dot(g0, latent, NN) + dot(g1, latent, NN) + dot(g2, latent, NN)
        variance = jnp.sum(spread * latent_f, axis=0, keepdims=True)
        inv_std = lax.rsqrt(jnp.maximum(variance, 0.0) + epsilon)
        varied = inv_std * (dot(mix_hi, latent, TN) + dot(mix_lo, latent, TN))
        output = varied + column(turned[128 + s : 129 + s, :])
        grad_out = (2.0 * (output - target_ref[:, at].astype(f32)) / tokens).astype(bf16)
        grad_f = grad_out.astype(f32)
        along = jnp.sum(grad_f * varied, axis=0, keepdims=True) / width
        cross = dot((grad_f * inv_std).astype(bf16), latent, NT)
        curve = curve + dot((latent_f * (along * inv_std * inv_std)).astype(bf16), latent, NT)
        sums.append(row(jnp.sum(grad_f, axis=1, keepdims=True)))
        if s < 2:
            out[0, s * 64 : s * 64 + 64, 0:64] = cross
        else:
            wide[(s - 2) * 64 : (s - 2) * 64 + 64, 0:64] = cross
    for s in range(4):
        wide[128 + s : 129 + s, :] = sums[s]
    wide[132:136, 0:64] = gain_means[:, 0:64]
    packed = pltpu.roll(wide[...], 64, 1)
    low_lane = lax.broadcasted_iota(jnp.int32, (128, 128), 1) < 64
    out[0, 0:128, :] = jnp.where(low_lane, out[0, 0:128, :], packed[0:128])
    wide[128:192, 0:64] = curve
    out[0, 128:192, :] = jnp.where(low_lane[0:64], wide[128:192, :], packed[128:192])


def finish_kernel(
    after,
    parts0,
    parts1,
    parts2,
    parts4,
    pre_ref,
    center_ref,
    sines_ref,
    patch_ref,
    head_ref,
    mod_ref,
    time_ref,
    *refs,
):
    patch_new, head_new, mod_new, time_new, sums, slope_rows = refs[after:]
    count = N_FSDP
    parts = [ref[i] for ref in (parts0, parts1, parts2, parts4) for i in range(ref.shape[0])]
    pre = pre_ref[...]
    gain, shift = gains(pre, mod_ref)
    head = head_ref[...].astype(bf16)
    head_f = head.astype(f32)
    center = center_ref[...]
    chi, clo = split2(center)
    curve = parts[0][128:192, 0:64]
    for k in range(1, count):
        curve = curve + parts[k][128:192, 0:64]
    curve_hi, curve_lo = split2(curve)
    grad_patch = -(dot(curve_hi, chi, NN) + dot(curve_lo, chi, NN) + dot(curve_hi, clo, NN))
    grad_head = jnp.zeros_like(center)
    grad_scale = jnp.zeros_like(gain[0:1])
    for k in range(count):
        plain = parts[k]
        turned = pltpu.roll(plain, 64, 1)
        sums[4 * k : 4 * k + 4, :] = turned[128:132]
        crosses, fine = split2(jnp.concatenate([plain[0:128, 0:64], turned[0:128, 0:64]], axis=0))
        mixed = dot(crosses, chi, NN) + dot(fine, chi, NN) + dot(crosses, clo, NN)
        pulls = []
        for i in range(4):
            s = 4 * k + i
            one = mixed[i * 64 : i * 64 + 64]
            grad_head = grad_head + one * gain[s : s + 1]
            slope = jnp.sum(head_f * one, axis=0, keepdims=True)
            slope_rows[s : s + 1, :] = slope
            grad_scale = grad_scale + slope
            pulls.append((head_f * gain[s : s + 1] - column(turned[132 + i : 133 + i])).astype(bf16))
        grad_patch = grad_patch + dot(crosses, jnp.concatenate(pulls, axis=0), TN)
    sum_hi, sum_lo = split2(sums[:, 0:64])
    shift_hi, shift_lo = split2(shift)
    grad_head = grad_head + dot(sum_hi, shift_hi, TN) + dot(sum_lo, shift_hi, TN) + dot(sum_hi, shift_lo, TN)
    mixed_sums = dot(sum_hi, head, NN) + dot(sum_lo, head, NN)
    grad_shift = jnp.sum(mixed_sums, axis=0, keepdims=True)
    grad_embed = mixed_sums + slope_rows[...]
    sigmoid = jax.nn.sigmoid(pre)
    grad_pre = (grad_embed * (sigmoid * (1.0 + pre * (1.0 - sigmoid)))).astype(bf16)
    grad_time = dot(sines_ref[...].astype(bf16), grad_pre, TN)
    patch_new[...] = patch_ref[...] - inner_rate * grad_patch
    head_new[...] = head_ref[...] - inner_rate * grad_head
    mod_new[0:1, :] = mod_ref[0:1, :] - inner_rate * grad_shift
    mod_new[1:2, :] = mod_ref[1:2, :] - inner_rate * grad_scale
    time_new[...] = time_ref[...] - inner_rate * grad_time


def sinusoid(time_steps):
    index = jnp.arange(FREQ_DIM // 2, dtype=f32)
    frequency = jnp.exp(-math.log(10000.0) * index / (FREQ_DIM // 2))
    angles = time_steps.astype(f32)[:, None] * frequency[None, :]
    return jnp.cos(angles), jnp.sin(angles)


def step_head(timesteps, patch):
    cos, sin = sinusoid(timesteps)
    row_sums = jnp.sum(patch.astype(bf16).astype(f32), axis=1)
    return jnp.concatenate(
        [cos, sin, jnp.pad(row_sums, (0, 128 - PATCH_DIM))[None], jnp.zeros((7, 128), f32)], axis=0
    )


def weight_products(near, away, patch, head, mod, time, after, width):
    columns = patch.shape[1]
    samples = 4 * N_FSDP
    share = jax.ShapeDtypeStruct((N_FSDP // 2, 192, 128), f32)
    return pl.pallas_call(
        functools.partial(weights_kernel, width, len(after)),
        in_specs=[pl.BlockSpec(memory_space=pltpu.VMEM)] * 6 + [unread] * len(after),
        out_shape=[
            share,
            share,
            jax.ShapeDtypeStruct((samples, columns), f32),
            jax.ShapeDtypeStruct((PATCH_DIM, columns), f32),
            jax.ShapeDtypeStruct((samples, FREQ_DIM), f32),
        ],
        scratch_shapes=[pltpu.VMEM((samples * PATCH_DIM, columns), bf16)] * 2,
        compiler_params=limit,
        cost_estimate=brief,
        name="weight_products",
    )(near, away, patch, head, mod, time, *after)


def token_sums(own, away, latents, target, after, width, tokens):
    return pl.pallas_call(
        functools.partial(tokens_kernel, width, tokens, len(after)),
        in_specs=[pl.BlockSpec(memory_space=pltpu.VMEM)] * 4 + [unread] * len(after),
        out_shape=jax.ShapeDtypeStruct((1, 192, 128), f32),
        scratch_shapes=[pltpu.VMEM((192, 128), f32)],
        compiler_params=limit,
        cost_estimate=brief,
        name="token_sums",
    )(own, away, latents, target, *after)


def finish(q0, q1, q2, q4, pre, center, sines, params, after):
    samples, columns = pre.shape
    return pl.pallas_call(
        functools.partial(finish_kernel, len(after)),
        in_specs=[pl.BlockSpec(memory_space=pltpu.VMEM)] * 11 + [unread] * len(after),
        out_shape=[jax.ShapeDtypeStruct(a.shape, f32) for a in params],
        scratch_shapes=[pltpu.VMEM((samples, 128), f32), pltpu.VMEM((samples, columns), f32)],
        compiler_params=limit,
        cost_estimate=brief,
        name="finish",
    )(q0, q1, q2, q4, pre, center, sines, *params, *after)


def solution(mesh):
    in_specs = (
        P(("replica", "fsdp"), None),
        P(("replica", "fsdp"), None),
        P(("replica", "fsdp")),
        P("replica", None, "fsdp"),
        P("replica", None, "fsdp"),
        P("replica", None, "fsdp"),
        P("replica", None, "fsdp"),
        P("fsdp", "replica"),
        P("fsdp", "replica"),
        P("fsdp", None),
        P("replica", "fsdp", None),
    )
    out_specs = (
        P("replica", None, "fsdp"),
        P("replica", None, "fsdp"),
        P("replica", None, "fsdp"),
        P("replica", None, "fsdp"),
        P("fsdp", "replica"),
        P("fsdp", "replica"),
        P("fsdp", None),
    )
    return jax.shard_map(
        per_device, mesh=mesh, in_specs=in_specs, out_specs=out_specs, check_vma=False
    )
```
